128 devices in a mesh: dp: 8 (over x, core), mp: 16 (over y, z).
Axes of the slice: x: 4, y: 4, z: 4, core: 2. Of those that a mesh axis runs over, the one named last changes fastest.
Arguments:
- attention: bfloat16 [2048, 8192], P('dp', 'mp'), may hold values from -6 to 6
- out_proj: bfloat16 [8192, 8192], P('mp'), may hold values from -0.0625 to 0.0625
- residual: bfloat16 [2048, 8192], P('dp', 'mp')
- final_gain: float32 [8192], P('mp'), may hold values from 0.1 to 1.9
- adapter_weight: bfloat16 [8192, 3072], P('mp'), may hold values from -0.0625 to 0.0625
- token_slot: int32 [2048], P('dp'), may hold values from 0 to 127, as said below
- block_owner: int32 [16], replicated, may hold values from 0 to 7, as said below
- student_hidden: bfloat16 [8, 128, 4, 3072], P('dp', 'mp'), may hold values from -6 to 6
- cotangent: bfloat16 [8, 128, 4, 3072], P('dp', 'mp'), may hold values from -1.25 to 1.25
- student_gain: float32 [3072], replicated, may hold values from 0.1 to 1.9
- gate_weight: bfloat16 [3072, 8192], P(None, 'mp'), may hold values from -0.109375 to 0.109375
- up_weight: bfloat16 [3072, 8192], P(None, 'mp'), may hold values from -0.109375 to 0.109375
- down_weight: bfloat16 [3072, 8192], P(None, 'mp'), may hold values from -0.0625 to 0.0625
Outputs:
- student_out: bfloat16 [8, 128, 4, 3072], P('dp', 'mp')
- adapter_grad: float32 [8192, 3072], P('mp', 'dp')
The draws below stay inside these ranges and needn't reach their ends.
Inputs may be any that keep to these rules, and one draw needn't show every extreme that they name: `token_slot`: within each aligned block of 128 teacher tokens the slot never falls, and the block's last token has slot 127. `block_owner`: every dp index owns 2 blocks, except one that owns 2 * 2 and one that owns none; which ones varies.
All inputs are finite; a program needn't handle non-finite values.
Results may differ from the reference program's by a relative error of at most 0.03.
Values may be sent and summed in bfloat16 or wider, within the bound.
No kernel may reach another device: no remote copies, remote signals or barrier semaphores. Data moves between devices by JAX's collectives and lax.ppermute only.
A program may use at most 384 MiB of HBM per device.

```python
import math
import jax
import jax.numpy as jnp
from jax import lax

D = 8192
E = 3072
SF = 8192
BLK = 128
NBLK_DEV = 2
CAP = 4
NBLOCKS = 16
TEACHER_TOK = 2048
N_DP = 8
N_MP = 16


def draw_residual(key, part):
    key = jax.random.fold_in(key, 11)
    columns = jnp.exp(jnp.linspace(0.0, math.log(3.0), D))
    values = jax.random.normal(key, (TEACHER_TOK, D))
    return (values * columns[None, :]).astype(jnp.bfloat16)


def draw_token_slot(key, part):
    key = jax.random.fold_in(key, 37)
    steps_up = jax.random.randint(key, (NBLOCKS, BLK), 0, 3)
    climbed = jnp.cumsum(steps_up, axis=1) - steps_up
    clipped = jnp.minimum(climbed, BLK - 1)
    final_col = jnp.arange(BLK)[None, :] == BLK - 1
    return jnp.where(final_col, BLK - 1, clipped).astype(jnp.int32).reshape(NBLOCKS * BLK)


def draw_block_owner(key, part):
    key = jax.random.fold_in(key, 23)
    groups = NBLOCKS // NBLK_DEV
    subkeys = jax.random.split(key, 3)
    light = jax.random.randint(subkeys[0], (), 0, groups - 1)
    heavy = (light + jax.random.randint(subkeys[1], (), 1, groups)) % groups
    ordered = jnp.arange(NBLOCKS, dtype=jnp.int32) // NBLK_DEV
    ordered = jnp.where(ordered == light, heavy, ordered)
    return ordered[jax.random.permutation(subkeys[2], NBLOCKS)].astype(jnp.int32)


def levels(own_key, extent, cuts, least, top_value):
    level = 1.0
    for position, shards_of in cuts:
        heights = jax.random.uniform(jax.random.fold_in(jax.random.fold_in(own_key, 6), position), (shards_of,), jnp.float32, least / len(cuts), top_value / len(cuts))
        level = level * jnp.repeat(jnp.exp(heights), extent[position] // shards_of).reshape((-1,) + (1,) * (len(extent) - 1 - position))
    return level


def gaussian(stream_key, extent, width, bound, cuts=(), held_as=jnp.bfloat16):
    entries = width * jax.random.normal(stream_key, extent, jnp.float32)
    if cuts:
        entries = entries * levels(stream_key, extent, cuts, -0.22, 0.18)
    return jnp.clip(entries, -bound, bound).astype(held_as)


def setup_inputs(seed: int = 0) -> dict:
    splits = jax.random.split(jax.random.key(seed), 14)
    attention = gaussian(splits[0], (TEACHER_TOK, D), 1.0, 6.0, ((0, 8), (1, 16)))
    out_proj = gaussian(splits[1], (D, D), D ** -0.5, 0.0625, ((0, 16),))
    residual = draw_residual(jax.random.fold_in(splits[13], 71), 0)
    final_gain = jnp.clip(1.0 + 0.18 * jax.random.normal(splits[3], (D,), jnp.float32), 0.1, 1.9)
    adapter_weight = gaussian(splits[4], (D, E), D ** -0.5, 0.0625, ((0, 16),))
    token_slot = draw_token_slot(jax.random.fold_in(splits[13], 71), 0)
    block_owner = draw_block_owner(jax.random.fold_in(splits[13], 71), 0)
    student_hidden = gaussian(splits[7], (N_DP, BLK, CAP, E), 1.0, 6.0, ((0, 8), (1, 16)))
    cotangent = gaussian(splits[8], (N_DP, BLK, CAP, E), (4.0 / (NBLOCKS * BLK) ** 0.5), 1.25, ((0, 8), (1, 16)))
    student_gain = jnp.clip(1.0 + 0.18 * jax.random.normal(splits[9], (E,), jnp.float32), 0.1, 1.9)
    gate_weight = gaussian(splits[10], (E, SF), E ** -0.5, 0.109375, ((1, 16),))
    up_weight = gaussian(splits[11], (E, SF), E ** -0.5, 0.109375, ((1, 16),))
    down_weight = gaussian(splits[12], (E, SF), SF ** -0.5, 0.0625, ((1, 16),))
    return dict(attention=attention, out_proj=out_proj, residual=residual, final_gain=final_gain, adapter_weight=adapter_weight, token_slot=token_slot, block_owner=block_owner, student_hidden=student_hidden, cotangent=cotangent, student_gain=student_gain, gate_weight=gate_weight, up_weight=up_weight, down_weight=down_weight)


epsilon = 1e-06

def rounded(value):
    return lax.optimization_barrier(value.astype(jnp.bfloat16)).astype(jnp.float32)

def reference(attention, out_proj, residual, final_gain, adapter_weight, token_slot, block_owner, student_hidden, cotangent, student_gain, gate_weight, up_weight, down_weight):
    width_group = D // N_MP

    def head_group(index, running):
        part_in = lax.dynamic_slice_in_dim(attention, index * width_group, width_group, 1)
        part_weight = lax.dynamic_slice_in_dim(out_proj, index * width_group, width_group, 0)
        return running + rounded(jnp.dot(part_in, part_weight, preferred_element_type=jnp.float32))
    summed = lax.fori_loop(0, N_MP, head_group, jnp.zeros((TEACHER_TOK, D), jnp.float32))
    hidden = residual.astype(jnp.float32) + summed
    inverse_rms = lax.rsqrt(lax.optimization_barrier(jnp.mean(hidden * hidden, axis=1, keepdims=True)) + epsilon)
    normed = (hidden * inverse_rms * final_gain).astype(jnp.bfloat16)
    blocked = normed.reshape(NBLOCKS, BLK, D).astype(jnp.float32)
    slots_block = token_slot.reshape(NBLOCKS, BLK)
    onehot = (slots_block[:, None, :] == jnp.arange(BLK, dtype=jnp.int32)[None, :, None]).astype(jnp.float32)
    counts = lax.optimization_barrier(jnp.sum(onehot, axis=2))
    pooled = jnp.einsum('krt,ktd->krd', onehot, blocked)
    pooled = (pooled / jnp.maximum(counts, 1.0)[:, :, None]).astype(jnp.bfloat16)

    def proj_group(index, running):
        part_in = lax.dynamic_slice_in_dim(pooled, index * width_group, width_group, 2).astype(jnp.float32)
        part_weight = lax.dynamic_slice_in_dim(adapter_weight, index * width_group, width_group, 0).astype(jnp.float32)
        return running + rounded(jnp.einsum('krd,de->kre', part_in, part_weight))
    projected = lax.fori_loop(0, N_MP, proj_group, jnp.zeros((NBLOCKS, BLK, E), jnp.float32)).astype(jnp.bfloat16)
    owned = block_owner[None, :] == jnp.arange(N_DP, dtype=jnp.int32)[:, None]
    owned_int = owned.astype(jnp.int32)
    ranks = jnp.cumsum(owned_int, axis=1) - owned_int
    select = owned[:, None, :] & (ranks[:, None, :] == jnp.arange(CAP, dtype=jnp.int32)[None, :, None])
    select_float = select.astype(jnp.float32)
    live = lax.optimization_barrier(jnp.sum(select_float, axis=2)) > 0.5
    placed = jnp.einsum('gcb,bre->grce', select_float, projected.astype(jnp.float32))
    state = student_hidden.astype(jnp.float32) + placed
    inverse_student = lax.rsqrt(lax.optimization_barrier(jnp.mean(state * state, axis=-1, keepdims=True)) + epsilon)
    normed_student = (state * inverse_student * student_gain).astype(jnp.bfloat16)
    rows_flat = normed_student.reshape(-1, E)
    gate_val = jnp.dot(rows_flat, gate_weight, preferred_element_type=jnp.float32)
    up_val = jnp.dot(rows_flat, up_weight, preferred_element_type=jnp.float32)
    act = (jax.nn.silu(gate_val) * up_val).astype(jnp.bfloat16)
    contract = (((1,), (1,)), ((), ()))
    output = lax.dot_general(act, down_weight, contract, preferred_element_type=jnp.float32).reshape(state.shape)
    live_mask = live[:, None, :, None]
    student_out = jnp.where(live_mask, state + output, 0.0).astype(jnp.bfloat16)
    grad_out = jnp.where(live_mask, cotangent, jnp.zeros_like(cotangent))
    grad_hidden = jnp.dot(grad_out.reshape(-1, E), down_weight, preferred_element_type=jnp.float32)
    sigma = jax.nn.sigmoid(gate_val)
    grad_gate = (grad_hidden * up_val * sigma * (1.0 + gate_val * (1.0 - sigma))).astype(jnp.bfloat16)
    grad_up = (grad_hidden * jax.nn.silu(gate_val)).astype(jnp.bfloat16)
    grad_norm = lax.dot_general(grad_gate, gate_weight, contract, preferred_element_type=jnp.float32)
    grad_norm = grad_norm + lax.dot_general(grad_up, up_weight, contract, preferred_element_type=jnp.float32)
    grad_norm = grad_norm.reshape(state.shape)
    gained = student_gain * grad_norm
    grad_state = grad_out.astype(jnp.float32) + inverse_student * gained
    grad_state = grad_state - state * inverse_student ** 3 * lax.optimization_barrier(jnp.mean(gained * state, axis=-1, keepdims=True))
    grad_proj = jnp.where(live_mask, grad_state, 0.0).astype(jnp.bfloat16)
    grad_blocks = jnp.einsum('gcb,grce->bre', select_float, grad_proj.astype(jnp.float32)).astype(jnp.bfloat16)

    def grad_group(index, running):
        part_pool = lax.dynamic_slice_in_dim(pooled, index * NBLK_DEV, NBLK_DEV, 0).astype(jnp.float32)
        part_grad = lax.dynamic_slice_in_dim(grad_blocks, index * NBLK_DEV, NBLK_DEV, 0).astype(jnp.float32)
        return running + rounded(jnp.einsum('krd,kre->de', part_pool, part_grad))
    adapter_grad = lax.fori_loop(0, N_DP, grad_group, jnp.zeros((D, E), jnp.float32))
    return (student_out, adapter_grad)
```

```python
import jax
import jax.numpy as jnp
from jax import lax
from jax.experimental import pallas as pl
from jax.experimental.pallas import tpu as pltpu
from jax.sharding import PartitionSpec as P

BLK = 128
epsilon = 1e-06
half = jnp.bfloat16
full = jnp.float32


def exchange(pieces, axis):
    return lax.all_to_all(pieces, axis, split_axis=0, concat_axis=0, tiled=True)


def share(piece, axis):
    size = lax.axis_size(axis)
    return exchange(jnp.broadcast_to(piece[None], (size,) + piece.shape), axis)


def three_parts(value):
    first = lax.reduce_precision(value, 8, 7)
    rest = value - first
    second = lax.reduce_precision(rest, 8, 7)
    return jnp.stack([first, second, rest - second]).astype(half)


def times_rows(left, right):
    return lax.dot_general(left, right, (((1,), (1,)), ((), ())), preferred_element_type=full)


def piece_kernel(left, right, out):
    out[0] = jnp.dot(left[...], right[...], preferred_element_type=full).astype(out.dtype)


def product_in_pieces(left, right, pieces):
    rows, depth = left.shape
    width = right.shape[1] // pieces
    return pl.pallas_call(
        piece_kernel,
        grid=(pieces,),
        in_specs=[
            pl.BlockSpec((rows, depth), lambda i: (0, 0)),
            pl.BlockSpec((depth, width), lambda i: (0, i)),
        ],
        out_specs=pl.BlockSpec((1, rows, width), lambda i: (i, 0, 0)),
        out_shape=jax.ShapeDtypeStruct((pieces, rows, width), half),
        compiler_params=pltpu.CompilerParams(vmem_limit_bytes=16 * 1024 * 1024),
        cost_estimate=pl.CostEstimate(
            flops=2 * rows * depth * width * pieces,
            bytes_accessed=2 * (depth + rows) * width * pieces,
            transcendentals=0,
        ),
    )(left, right)


def on_device(
    attention,
    out_proj,
    residual,
    final_gain,
    adapter_weight,
    token_slot,
    block_owner,
    student_hidden,
    cotangent,
    student_gain,
    gate_weight,
    up_weight,
    down_weight,
):
    tokens, width_here = attention.shape
    width_full = out_proj.shape[1]
    student_width = adapter_weight.shape[1]
    blocks = tokens // BLK
    n_mp = lax.axis_size("mp")
    n_dp = lax.axis_size("dp")
    dp = lax.axis_index("dp")
    mp = lax.axis_index("mp")
    slots = student_hidden.shape[2]
    rows = BLK // n_mp
    groups = n_mp // blocks
    cols = student_width // groups
    out_cols = student_width // n_dp
    mine_rows = blocks * rows

    owned = block_owner[None, :] == jnp.arange(n_dp, dtype=jnp.int32)[:, None]
    ranks = jnp.sum(jnp.where(owned, jnp.cumsum(owned.astype(jnp.int32), axis=1) - 1, 0), axis=0)
    place = block_owner * slots + ranks
    my_place = lax.dynamic_slice_in_dim(place, dp * blocks, blocks)

    def fetch(array):
        by_slot = jnp.swapaxes(array[0], 0, 1)
        everyone = lax.all_gather(by_slot, "dp", axis=0, tiled=True)
        return jnp.stack(
            [lax.dynamic_index_in_dim(everyone, my_place[k], 0, False) for k in range(blocks)]
        )

    sh_rows = fetch(student_hidden)
    dy_rows = fetch(cotangent).reshape(mine_rows, student_width)
    dy = lax.all_gather(dy_rows, "mp", axis=0, tiled=True)

    terms = product_in_pieces(attention, out_proj, n_mp)
    hidden = residual.astype(full) + jnp.sum(exchange(terms, "mp").astype(full), axis=0)
    squares = jnp.sum(hidden * hidden, axis=1)
    gained_hidden = hidden * final_gain
    parts = jnp.einsum(
        "ktd,dce->kcte",
        gained_hidden.astype(half).reshape(blocks, BLK, width_here),
        adapter_weight.reshape(width_here, groups, cols),
        preferred_element_type=full,
    ).astype(half)
    sh_parts = jnp.swapaxes(sh_rows.reshape(blocks, rows, groups, cols), 1, 2)
    sq_parts = jnp.zeros((8, cols), half).at[:3, :tokens].set(three_parts(squares))
    message = jnp.concatenate(
        [
            parts,
            sh_parts,
            jnp.broadcast_to(sq_parts[None, None], (blocks, groups) + sq_parts.shape),
        ],
        axis=2,
    )
    message = exchange(message.reshape(n_mp, BLK + rows + 8, cols), "mp")
    token_proj = jnp.sum(message[:, :BLK].astype(full), axis=0)
    sh_here = message[:, BLK : BLK + rows].reshape(BLK, cols)
    squares_all = jnp.sum(message[:, BLK + rows : BLK + rows + 3].astype(full), axis=(0, 1))[:tokens]
    inverse_rms = lax.rsqrt(squares_all / width_full + epsilon)

    slots_block = token_slot.reshape(blocks, BLK)
    onehot = slots_block[:, None, :] == jnp.arange(BLK, dtype=jnp.int32)[None, :, None]
    counts = jnp.maximum(jnp.sum(onehot.astype(full), axis=2), 1.0)
    onehot = onehot.astype(half)
    my_block = mp // groups
    inv_block = lax.dynamic_index_in_dim(inverse_rms.reshape(blocks, BLK), my_block, 0, False)
    onehot_block = lax.dynamic_index_in_dim(onehot, my_block, 0, False)
    counts_block = lax.dynamic_index_in_dim(counts, my_block, 0, False)
    placed = jnp.dot(
        onehot_block, (token_proj * inv_block[:, None]).astype(half), preferred_element_type=full
    )
    placed = (placed / counts_block[:, None]).astype(half).astype(full)
    state_here = (sh_here.astype(full) + placed).astype(half)
    state = share(state_here, "mp")
    state = state.reshape(blocks, groups, n_mp, rows, cols)
    state = jnp.transpose(state, (2, 0, 3, 1, 4)).reshape(tokens, student_width)

    normed = (gained_hidden * inverse_rms[:, None]).astype(half).reshape(blocks, BLK, width_here)
    pooled = jnp.einsum("krt,ktd->krd", onehot, normed, preferred_element_type=full)
    pooled = (pooled / counts[:, :, None]).astype(half)
    pooled = jnp.swapaxes(pooled.reshape(blocks, n_mp, rows, width_here), 0, 1)
    pooled_all = lax.all_gather(pooled.reshape(1, n_mp, mine_rows, width_here), "dp", axis=0, tiled=True)
    pooled_all = jnp.swapaxes(pooled_all, 0, 1).reshape(n_dp * tokens, width_here)

    wide = state.astype(full)
    inverse = lax.rsqrt(jnp.mean(wide * wide, axis=-1, keepdims=True) + epsilon)
    normed_student = (wide * inverse * student_gain).astype(half)
    dh = jnp.dot(dy, down_weight, preferred_element_type=full)
    gate = jnp.dot(normed_student, gate_weight, preferred_element_type=full)
    up = jnp.dot(normed_student, up_weight, preferred_element_type=full)
    sigma = jax.nn.sigmoid(gate)
    silu = gate * sigma
    act = (silu * up).astype(half)
    grad_gate = (dh * up * sigma * (1.0 + gate * (1.0 - sigma))).astype(half)
    grad_up = (dh * silu).astype(half)
    dn = (times_rows(grad_gate, gate_weight) + times_rows(grad_up, up_weight)).astype(half)
    output = times_rows(act, down_weight).astype(half)
    both = jnp.stack(
        [
            dn.reshape(n_mp, mine_rows, student_width),
            output.reshape(n_mp, mine_rows, student_width),
        ],
        axis=1,
    )
    both = jnp.sum(exchange(both, "mp").astype(full), axis=0)
    state_rows = lax.dynamic_slice_in_dim(state, mp * mine_rows, mine_rows, 0).astype(full)
    inv_rows = lax.dynamic_slice_in_dim(inverse, mp * mine_rows, mine_rows, 0)
    gained = student_gain * both[0]
    dx = dy_rows.astype(full) + inv_rows * gained
    dx = dx - state_rows * inv_rows**3 * jnp.mean(gained * state_rows, axis=-1, keepdims=True)
    dproj = jnp.swapaxes(dx.astype(half).reshape(mine_rows, n_dp, out_cols), 0, 1)
    dproj = share(exchange(dproj, "dp"), "mp")
    adapter_grad = lax.dot_general(
        pooled_all,
        dproj.reshape(n_dp * tokens, out_cols),
        (((0,), (0,)), ((), ())),
        preferred_element_type=full,
    )

    out_rows = (state_rows + both[1]).astype(half)
    back = lax.all_gather(
        out_rows.reshape(blocks, rows, student_width), "dp", axis=0, tiled=True
    )
    mine = block_owner == dp
    picks = []
    for slot in range(slots):
        chosen = mine & (ranks == slot)
        index = jnp.sum(jnp.where(chosen, jnp.arange(chosen.shape[0], dtype=jnp.int32), 0))
        piece = lax.dynamic_index_in_dim(back, index, 0, False)
        picks.append(jnp.where(jnp.any(chosen), piece, jnp.zeros((), half)))
    student_out = jnp.stack(picks, axis=1)
    return (student_out[None], adapter_grad)


def solution(mesh):
    return jax.shard_map(
        on_device,
        mesh=mesh,
        in_specs=(
            P("dp", "mp"),
            P("mp", None),
            P("dp", "mp"),
            P("mp"),
            P("mp", None),
            P("dp"),
            P(),
            P("dp", "mp", None, None),
            P("dp", "mp", None, None),
            P(),
            P(None, "mp"),
            P(None, "mp"),
            P(None, "mp"),
        ),
        out_specs=(P("dp", "mp", None, None), P("mp", "dp")),
        check_vma=False,
    )
```

```python
import jax
import jax.numpy as jnp
from jax import lax
from jax.experimental import pallas as pl
from jax.experimental.pallas import tpu as pltpu
from jax.sharding import PartitionSpec as P

BLK = 128
epsilon = 1e-06
half = jnp.bfloat16
full = jnp.float32


def exchange(pieces, axis):
    return lax.all_to_all(pieces, axis, split_axis=0, concat_axis=0, tiled=True)


def share(piece, axis):
    size = lax.axis_size(axis)
    return exchange(jnp.broadcast_to(piece[None], (size,) + piece.shape), axis)


def three_parts(value):
    first = lax.reduce_precision(value, 8, 7)
    rest = value - first
    second = lax.reduce_precision(rest, 8, 7)
    return jnp.stack([first, second, rest - second]).astype(half)


def times_rows(left, right):
    return lax.dot_general(left, right, (((1,), (1,)), ((), ())), preferred_element_type=full)


SIDE = 4


def step(value, along_y, along_z):
    pairs = []
    for y in range(SIDE):
        for z in range(SIDE):
            to = ((y + along_y) % SIDE) * SIDE + (z + along_z) % SIDE
            pairs.append((y * SIDE + z, to))
    return lax.ppermute(value, "mp", pairs)


def piece_kernel(ids, left, right, out):
    out[0] = jnp.dot(left[...], right[...], preferred_element_type=full).astype(out.dtype)


def product_pieces(left, right, block, ids, width):
    depth = left.shape[1]
    count = ids.shape[0]
    return pl.pallas_call(
        piece_kernel,
        grid_spec=pltpu.PrefetchScalarGridSpec(
            num_scalar_prefetch=1,
            grid=(count,),
            in_specs=[
                pl.BlockSpec((BLK, depth), lambda i, ids: (block, 0)),
                pl.BlockSpec((depth, width), lambda i, ids: (0, ids[i])),
            ],
            out_specs=pl.BlockSpec((1, BLK, width), lambda i, ids: (i, 0, 0)),
        ),
        out_shape=jax.ShapeDtypeStruct((count, BLK, width), half),
        compiler_params=pltpu.CompilerParams(vmem_limit_bytes=48 * 1024 * 1024),
        cost_estimate=pl.CostEstimate(
            flops=2 * BLK * depth * width * count,
            bytes_accessed=2 * (depth + BLK) * width * count,
            transcendentals=0,
        ),
    )(ids, left, right)


def total(values):
    result = values[0].astype(full)
    for value in values[1:]:
        result = result + value.astype(full)
    return result


def teacher_terms(attention, out_proj, mp):
    y, z = mp // SIDE, mp % SIDE
    width = attention.shape[1]
    along = jnp.arange(SIDE, dtype=jnp.int32)
    kept, moved = {}, {}
    for distance in (2, 1, 3, 0):
        for block in (0, 1):
            if block == 0:
                ids = ((y + distance) % SIDE) * SIDE + along
            else:
                ids = along * SIDE + (z + distance) % SIDE
            terms = product_pieces(attention, out_proj, block, ids.astype(jnp.int32), width)
            if distance == 0:
                kept[block] = terms
            else:
                moved[block, distance] = (
                    step(terms, distance, 0) if block == 0 else step(terms, 0, distance)
                )
    results = []
    for block in (0, 1):
        here = z if block == 0 else y
        arrays = [kept[block]] + [moved[block, distance] for distance in (2, 1, 3)]

        def piece(distance):
            at = (here + distance) % SIDE
            return total([lax.dynamic_index_in_dim(a, at, 0, False) for a in arrays])

        arrived = []
        for distance in (2, 1, 3):
            sent = piece(distance).astype(half)
            arrived.append(step(sent, 0, distance) if block == 0 else step(sent, distance, 0))
        results.append(piece(0) + total(arrived))
    return results


def normalise_kernel(pieces, gain, state, normed):
    groups = state.shape[1] // pieces.shape[2]
    cols = pieces.shape[2]
    for block in range(state.shape[0] // BLK):
        rows = pl.ds(block * BLK, BLK)
        squares = jnp.zeros((BLK, 128), full)
        for group in range(groups):
            value = pieces[block * groups + group]
            state[rows, pl.ds(group * cols, cols)] = value
            wide = value.astype(full)
            wide = wide * wide
            for lane in range(0, cols, 128):
                squares = squares + wide[:, lane : lane + 128]
        mean = jnp.sum(squares, axis=1, keepdims=True) / state.shape[1]
        inverse = lax.rsqrt(mean + epsilon)
        for group in range(groups):
            at = pl.ds(group * cols, cols)
            wide = pieces[block * groups + group].astype(full)
            normed[rows, at] = (wide * inverse * gain[:, at]).astype(normed.dtype)


def normalise(pieces, gain, rows, width):
    whole = pl.BlockSpec(memory_space=pltpu.VMEM)
    shape = jax.ShapeDtypeStruct((rows, width), half)
    return pl.pallas_call(
        normalise_kernel,
        in_specs=[whole, whole],
        out_specs=[whole, whole],
        out_shape=[shape, shape],
        compiler_params=pltpu.CompilerParams(vmem_limit_bytes=16 * 1024 * 1024),
        cost_estimate=pl.CostEstimate(
            flops=6 * rows * width, bytes_accessed=6 * rows * width, transcendentals=rows
        ),
    )(pieces, gain[None])


def slope_kernel(terms, dy, state, gain, out):
    rows, width = dy.shape
    cols = out.shape[2]
    wide = state[...].astype(full)
    inverse = lax.rsqrt(jnp.mean(wide * wide, axis=1, keepdims=True) + epsilon)
    dn = terms[0].astype(full)
    for source in range(1, terms.shape[0]):
        dn = dn + terms[source].astype(full)
    gained = gain[...] * dn
    mean = jnp.mean(gained * wide, axis=1, keepdims=True)
    dx = dy[...].astype(full) + inverse * gained - wide * (inverse * inverse * inverse) * mean
    for group in range(out.shape[0]):
        out[group] = dx[:, group * cols : (group + 1) * cols].astype(out.dtype)


def slope(terms, dy, state, gain, groups):
    rows, width = dy.shape
    whole = pl.BlockSpec(memory_space=pltpu.VMEM)
    return pl.pallas_call(
        slope_kernel,
        in_specs=[whole] * 4,
        out_specs=whole,
        out_shape=jax.ShapeDtypeStruct((groups, rows, width // groups), half),
        compiler_params=pltpu.CompilerParams(vmem_limit_bytes=16 * 1024 * 1024),
        cost_estimate=pl.CostEstimate(
            flops=30 * rows * width, bytes_accessed=40 * rows * width, transcendentals=rows
        ),
    )(terms, dy, state, gain[None])


def on_device(
    attention,
    out_proj,
    residual,
    final_gain,
    adapter_weight,
    token_slot,
    block_owner,
    student_hidden,
    cotangent,
    student_gain,
    gate_weight,
    up_weight,
    down_weight,
):
    tokens, width_here = attention.shape
    width_full = out_proj.shape[1]
    student_width = adapter_weight.shape[1]
    blocks = tokens // BLK
    n_mp = lax.axis_size("mp")
    n_dp = lax.axis_size("dp")
    dp = lax.axis_index("dp")
    mp = lax.axis_index("mp")
    slots = student_hidden.shape[2]
    rows = BLK // n_mp
    groups = n_mp // blocks
    cols = student_width // groups
    out_cols = student_width // n_dp
    mine_rows = blocks * rows

    owned = block_owner[None, :] == jnp.arange(n_dp, dtype=jnp.int32)[:, None]
    ranks = jnp.sum(jnp.where(owned, jnp.cumsum(owned.astype(jnp.int32), axis=1) - 1, 0), axis=0)
    place = block_owner * slots + ranks
    my_place = lax.dynamic_slice_in_dim(place, dp * blocks, blocks)

    both = jnp.concatenate(
        [jnp.swapaxes(student_hidden[0], 0, 1), jnp.swapaxes(cotangent[0], 0, 1)], axis=0
    )
    everyone = lax.all_gather(both, "dp", axis=0, tiled=False)

    def fetch(offset):
        picked = []
        for k in range(blocks):
            at = (my_place[k] // slots, my_place[k] % slots + offset, 0, 0)
            piece = lax.dynamic_slice(everyone, at, (1, 1, rows, student_width))
            picked.append(piece.reshape(rows, student_width))
        return jnp.stack(picked)

    sh_rows = fetch(0)
    dy = lax.all_gather(fetch(slots), "mp", axis=0, tiled=False)
    dy = jnp.swapaxes(dy, 0, 1).reshape(tokens, student_width)

    hidden = residual.astype(full) + jnp.concatenate(teacher_terms(attention, out_proj, mp), axis=0)
    squares = jnp.sum(hidden * hidden, axis=1)
    gained_hidden = hidden * final_gain
    parts = jnp.einsum(
        "ktd,dce->kcte",
        gained_hidden.astype(half).reshape(blocks, BLK, width_here),
        adapter_weight.reshape(width_here, groups, cols),
        preferred_element_type=full,
    ).astype(half)
    sh_parts = jnp.swapaxes(sh_rows.reshape(blocks, rows, groups, cols), 1, 2)
    sq_parts = jnp.zeros((8, cols), half).at[:3, :tokens].set(three_parts(squares))
    message = jnp.concatenate(
        [
            parts,
            sh_parts,
            jnp.broadcast_to(sq_parts[None, None], (blocks, groups) + sq_parts.shape),
        ],
        axis=2,
    )
    message = exchange(message.reshape(n_mp, BLK + rows + 8, cols), "mp")
    token_proj = jnp.sum(message[:, :BLK].astype(full), axis=0)
    sh_here = message[:, BLK : BLK + rows].reshape(BLK, cols)
    squares_all = jnp.sum(message[:, BLK + rows : BLK + rows + 3].astype(full), axis=(0, 1))[:tokens]
    inverse_rms = lax.rsqrt(squares_all / width_full + epsilon)

    slots_block = token_slot.reshape(blocks, BLK)
    onehot = slots_block[:, None, :] == jnp.arange(BLK, dtype=jnp.int32)[None, :, None]
    counts = jnp.maximum(jnp.sum(onehot.astype(full), axis=2), 1.0)
    onehot = onehot.astype(half)
    my_block = mp // groups
    inv_block = lax.dynamic_index_in_dim(inverse_rms.reshape(blocks, BLK), my_block, 0, False)
    onehot_block = lax.dynamic_index_in_dim(onehot, my_block, 0, False)
    counts_block = lax.dynamic_index_in_dim(counts, my_block, 0, False)
    placed = jnp.dot(
        onehot_block, (token_proj * inv_block[:, None]).astype(half), preferred_element_type=full
    )
    placed = (placed / counts_block[:, None]).astype(half).astype(full)
    state_here = (sh_here.astype(full) + placed).astype(half)
    state, normed_student = normalise(share(state_here, "mp"), student_gain, tokens, student_width)

    normed = (gained_hidden * inverse_rms[:, None]).astype(half).reshape(blocks, BLK, width_here)
    pooled = jnp.einsum("krt,ktd->krd", onehot, normed, preferred_element_type=full)
    pooled = (pooled / counts[:, :, None]).astype(half)
    pooled_all = lax.all_gather(pooled.reshape(n_mp, mine_rows, width_here), "dp", axis=0, tiled=False)
    pooled_all = jnp.swapaxes(pooled_all, 0, 1).reshape(n_dp * tokens, width_here)

    dh = jnp.dot(dy, down_weight, preferred_element_type=full)
    gate = jnp.dot(normed_student, gate_weight, preferred_element_type=full)
    up = jnp.dot(normed_student, up_weight, preferred_element_type=full)
    sigma = jax.nn.sigmoid(gate)
    silu = gate * sigma
    act = (silu * up).astype(half)
    grad_gate = (dh * up * sigma * (1.0 + gate * (1.0 - sigma))).astype(half)
    grad_up = (dh * silu).astype(half)
    dn = (times_rows(grad_gate, gate_weight) + times_rows(grad_up, up_weight)).astype(half)
    output = times_rows(act, down_weight).astype(half)
    dn = exchange(dn.reshape(n_mp, mine_rows, student_width), "mp")
    output = jnp.swapaxes(output.reshape(blocks, n_mp, rows, student_width), 0, 1)
    output = jnp.sum(exchange(output, "mp").astype(full), axis=0)
    here = mp * mine_rows
    dproj = slope(
        dn,
        lax.dynamic_slice_in_dim(dy, here, mine_rows, 0),
        lax.dynamic_slice_in_dim(state, here, mine_rows, 0),
        student_gain,
        n_dp,
    )
    dproj = share(exchange(dproj, "dp"), "mp")
    adapter_grad = lax.dot_general(
        pooled_all,
        dproj.reshape(n_dp * tokens, out_cols),
        (((0,), (0,)), ((), ())),
        preferred_element_type=full,
    )

    state_rows = lax.dynamic_slice_in_dim(
        state.reshape(blocks, BLK, student_width), mp * rows, rows, 1
    )
    out_rows = (state_rows.astype(full) + output).astype(half)
    out_rows = jnp.concatenate([out_rows, state_rows[:1]], axis=0)
    back = lax.all_gather(out_rows, "dp", axis=0, tiled=False)[:, :blocks]
    back = back.reshape(n_dp * blocks, rows, student_width)
    mine = block_owner == dp
    picks = []
    for slot in range(slots):
        chosen = mine & (ranks == slot)
        index = jnp.sum(jnp.where(chosen, jnp.arange(chosen.shape[0], dtype=jnp.int32), 0))
        piece = lax.dynamic_index_in_dim(back, index, 0, False)
        picks.append(jnp.where(jnp.any(chosen), piece, jnp.zeros((), half)))
    student_out = jnp.stack(picks, axis=1)
    return (student_out[None], adapter_grad)


def solution(mesh):
    return jax.shard_map(
        on_device,
        mesh=mesh,
        in_specs=(
            P("dp", "mp"),
            P("mp", None),
            P("dp", "mp"),
            P("mp"),
            P("mp", None),
            P("dp"),
            P(),
            P("dp", "mp", None, None),
            P("dp", "mp", None, None),
            P(),
            P(None, "mp"),
            P(None, "mp"),
            P(None, "mp"),
        ),
        out_specs=(P("dp", "mp", None, None), P("mp", "dp")),
        check_vma=False,
    )
```

```python
import jax
import jax.numpy as jnp
from jax import lax
from jax.experimental import pallas as pl
from jax.experimental.pallas import tpu as pltpu
from jax.sharding import PartitionSpec as P

BLK = 128
epsilon = 1e-06
half = jnp.bfloat16
full = jnp.float32


def exchange(pieces, axis):
    return lax.all_to_all(pieces, axis, split_axis=0, concat_axis=0, tiled=True)


def share(piece, axis):
    size = lax.axis_size(axis)
    return exchange(jnp.broadcast_to(piece[None], (size,) + piece.shape), axis)


def three_parts(value):
    first = lax.reduce_precision(value, 8, 7)
    rest = value - first
    second = lax.reduce_precision(rest, 8, 7)
    return jnp.stack([first, second, rest - second]).astype(half)


def times_rows(left, right):
    return lax.dot_general(left, right, (((1,), (1,)), ((), ())), preferred_element_type=full)


SIDE = 4


def step(value, along_y, along_z):
    pairs = []
    for y in range(SIDE):
        for z in range(SIDE):
            to = ((y + along_y) % SIDE) * SIDE + (z + along_z) % SIDE
            pairs.append((y * SIDE + z, to))
    return lax.ppermute(value, "mp", pairs)


def terms_kernel(place, left, right, *refs):
    outs, held, sems = refs[: 2 * SIDE], refs[2 * SIDE], refs[2 * SIDE + 1]
    width = held.shape[2]
    y, z = place[0], place[1]

    def load(index):
        piece = lax.rem(y + index // SIDE, SIDE) * SIDE + lax.rem(index, SIDE)
        columns = pl.ds(pl.multiple_of(piece * width, width), width)
        return pltpu.make_async_copy(right.at[:, columns], held.at[index], sems.at[index])

    for index in range(SIDE * SIDE):
        load(index).start()

    @pl.loop(0, SIDE * SIDE)
    def _(index):
        load(index).wait()
        value = jnp.dot(left[...], held[index], preferred_element_type=full).astype(half)
        along_y, at_z = index // SIDE, lax.rem(index, SIDE)
        at_y, along_z = lax.rem(y + along_y, SIDE), lax.rem(at_z - z + SIDE, SIDE)
        for distance in range(SIDE):

            @pl.when(along_y == distance)
            def _():
                outs[distance][at_z] = value[:BLK]

            @pl.when(along_z == distance)
            def _():
                outs[SIDE + distance][at_y] = value[BLK:]


def product_pieces(left, right, y, z):
    rows, depth = left.shape
    width = right.shape[1] // (SIDE * SIDE)
    whole = pl.BlockSpec(memory_space=pltpu.VMEM)
    return pl.pallas_call(
        terms_kernel,
        in_specs=[pl.BlockSpec(memory_space=pltpu.SMEM), whole, pl.BlockSpec(memory_space=pl.ANY)],
        out_specs=[whole] * (2 * SIDE),
        out_shape=[jax.ShapeDtypeStruct((SIDE, BLK, width), half)] * (2 * SIDE),
        scratch_shapes=[
            pltpu.VMEM((SIDE * SIDE, depth, width), half),
            pltpu.SemaphoreType.DMA((SIDE * SIDE,)),
        ],
        compiler_params=pltpu.CompilerParams(vmem_limit_bytes=56 * 1024 * 1024),
        cost_estimate=pl.CostEstimate(
            flops=2 * rows * right.size,
            bytes_accessed=2 * right.size,
            transcendentals=0,
        ),
    )(jnp.stack([y, z]).astype(jnp.int32), left, right)


def total(values):
    result = values[0].astype(full)
    for value in values[1:]:
        result = result + value.astype(full)
    return result


def teacher_terms(attention, out_proj, mp):
    y, z = mp // SIDE, mp % SIDE
    pieces = product_pieces(attention, out_proj, y, z)
    kept = {0: pieces[0], 1: pieces[SIDE]}
    moved = {}
    for distance in (2, 1, 3):
        moved[0, distance] = step(pieces[distance], distance, 0)
        moved[1, distance] = step(pieces[SIDE + distance], 0, distance)
    results = []
    for block in (0, 1):
        here = z if block == 0 else y
        arrays = [kept[block]] + [moved[block, distance] for distance in (2, 1, 3)]

        def piece(distance):
            at = (here + distance) % SIDE
            return total([lax.dynamic_index_in_dim(a, at, 0, False) for a in arrays])

        arrived = []
        for distance in (2, 1, 3):
            sent = piece(distance).astype(half)
            arrived.append(step(sent, 0, distance) if block == 0 else step(sent, distance, 0))
        results.append(piece(0) + total(arrived))
    return results


def normalise_kernel(pieces, gain, state, normed):
    groups = state.shape[1] // pieces.shape[2]
    cols = pieces.shape[2]
    for block in range(state.shape[0] // BLK):
        rows = pl.ds(block * BLK, BLK)
        squares = jnp.zeros((BLK, 128), full)
        for group in range(groups):
            value = pieces[block * groups + group]
            state[rows, pl.ds(group * cols, cols)] = value
            wide = value.astype(full)
            wide = wide * wide
            for lane in range(0, cols, 128):
                squares = squares + wide[:, lane : lane + 128]
        mean = jnp.sum(squares, axis=1, keepdims=True) / state.shape[1]
        inverse = lax.rsqrt(mean + epsilon)
        for group in range(groups):
            at = pl.ds(group * cols, cols)
            wide = pieces[block * groups + group].astype(full)
            normed[rows, at] = (wide * inverse * gain[:, at]).astype(normed.dtype)


def normalise(pieces, gain, rows, width):
    whole = pl.BlockSpec(memory_space=pltpu.VMEM)
    shape = jax.ShapeDtypeStruct((rows, width), half)
    return pl.pallas_call(
        normalise_kernel,
        in_specs=[whole, whole],
        out_specs=[whole, whole],
        out_shape=[shape, shape],
        compiler_params=pltpu.CompilerParams(vmem_limit_bytes=16 * 1024 * 1024),
        cost_estimate=pl.CostEstimate(
            flops=6 * rows * width, bytes_accessed=6 * rows * width, transcendentals=rows
        ),
    )(pieces, gain[None])


def slope_kernel(terms, dy, state, gain, out):
    rows, width = dy.shape
    cols = out.shape[2]
    wide = state[...].astype(full)
    inverse = lax.rsqrt(jnp.mean(wide * wide, axis=1, keepdims=True) + epsilon)
    dn = terms[0].astype(full)
    for source in range(1, terms.shape[0]):
        dn = dn + terms[source].astype(full)
    gained = gain[...] * dn
    mean = jnp.mean(gained * wide, axis=1, keepdims=True)
    dx = dy[...].astype(full) + inverse * gained - wide * (inverse * inverse * inverse) * mean
    for group in range(out.shape[0]):
        out[group] = dx[:, group * cols : (group + 1) * cols].astype(out.dtype)


def slope(terms, dy, state, gain, groups):
    rows, width = dy.shape
    whole = pl.BlockSpec(memory_space=pltpu.VMEM)
    return pl.pallas_call(
        slope_kernel,
        in_specs=[whole] * 4,
        out_specs=whole,
        out_shape=jax.ShapeDtypeStruct((groups, rows, width // groups), half),
        compiler_params=pltpu.CompilerParams(vmem_limit_bytes=16 * 1024 * 1024),
        cost_estimate=pl.CostEstimate(
            flops=30 * rows * width, bytes_accessed=40 * rows * width, transcendentals=rows
        ),
    )(terms, dy, state, gain[None])


def on_device(
    attention,
    out_proj,
    residual,
    final_gain,
    adapter_weight,
    token_slot,
    block_owner,
    student_hidden,
    cotangent,
    student_gain,
    gate_weight,
    up_weight,
    down_weight,
):
    tokens, width_here = attention.shape
    width_full = out_proj.shape[1]
    student_width = adapter_weight.shape[1]
    blocks = tokens // BLK
    n_mp = lax.axis_size("mp")
    n_dp = lax.axis_size("dp")
    dp = lax.axis_index("dp")
    mp = lax.axis_index("mp")
    slots = student_hidden.shape[2]
    rows = BLK // n_mp
    groups = n_mp // blocks
    cols = student_width // groups
    out_cols = student_width // n_dp
    mine_rows = blocks * rows

    owned = block_owner[None, :] == jnp.arange(n_dp, dtype=jnp.int32)[:, None]
    ranks = jnp.sum(jnp.where(owned, jnp.cumsum(owned.astype(jnp.int32), axis=1) - 1, 0), axis=0)
    place = block_owner * slots + ranks
    my_place = lax.dynamic_slice_in_dim(place, dp * blocks, blocks)

    both = jnp.concatenate([student_hidden[0], cotangent[0]], axis=1)
    everyone = lax.all_gather(both, "dp", axis=0, tiled=False)

    def fetch(offset):
        picked = []
        for k in range(blocks):
            at = (my_place[k] // slots, 0, my_place[k] % slots + offset, 0)
            piece = lax.dynamic_slice(everyone, at, (1, rows, 1, student_width))
            picked.append(piece.reshape(rows, student_width))
        return jnp.stack(picked)

    sh_rows = fetch(0)
    dy = lax.all_gather(fetch(slots), "mp", axis=0, tiled=False)

    hidden = residual.astype(full) + jnp.concatenate(teacher_terms(attention, out_proj, mp), axis=0)
    squares = jnp.sum(hidden * hidden, axis=1)
    gained_hidden = hidden * final_gain
    parts = jnp.einsum(
        "ktd,dce->kcte",
        gained_hidden.astype(half).reshape(blocks, BLK, width_here),
        adapter_weight.reshape(width_here, groups, cols),
        preferred_element_type=full,
    ).astype(half)
    sh_parts = jnp.swapaxes(sh_rows.reshape(blocks, rows, groups, cols), 1, 2)
    sq_parts = jnp.zeros((8, cols), half).at[:3, :tokens].set(three_parts(squares))
    message = jnp.concatenate(
        [
            parts,
            sh_parts,
            jnp.broadcast_to(sq_parts[None, None], (blocks, groups) + sq_parts.shape),
        ],
        axis=2,
    )
    message = exchange(message.reshape(n_mp, BLK + rows + 8, cols), "mp")
    token_proj = jnp.sum(message[:, :BLK].astype(full), axis=0)
    sh_here = message[:, BLK : BLK + rows].reshape(BLK, cols)
    squares_all = jnp.sum(message[:, BLK + rows : BLK + rows + 3].astype(full), axis=(0, 1))[:tokens]
    inverse_rms = lax.rsqrt(squares_all / width_full + epsilon)

    slots_block = token_slot.reshape(blocks, BLK)
    onehot = slots_block[:, None, :] == jnp.arange(BLK, dtype=jnp.int32)[None, :, None]
    counts = jnp.maximum(jnp.sum(onehot.astype(full), axis=2), 1.0)
    onehot = onehot.astype(half)
    my_block = mp // groups
    inv_block = lax.dynamic_index_in_dim(inverse_rms.reshape(blocks, BLK), my_block, 0, False)
    onehot_block = lax.dynamic_index_in_dim(onehot, my_block, 0, False)
    counts_block = lax.dynamic_index_in_dim(counts, my_block, 0, False)
    placed = jnp.dot(
        onehot_block, (token_proj * inv_block[:, None]).astype(half), preferred_element_type=full
    )
    placed = (placed / counts_block[:, None]).astype(half).astype(full)
    state_here = (sh_here.astype(full) + placed).astype(half)
    state, normed_student = normalise(share(state_here, "mp"), student_gain, tokens, student_width)

    normed = (gained_hidden * inverse_rms[:, None]).astype(half).reshape(blocks, BLK, width_here)
    pooled = jnp.einsum("krt,ktd->krd", onehot, normed, preferred_element_type=full)
    pooled = (pooled / counts[:, :, None]).astype(half)
    pooled_all = lax.all_gather(pooled.reshape(n_mp, mine_rows, width_here), "dp", axis=0, tiled=False)
    pooled_all = jnp.swapaxes(pooled_all, 0, 1).reshape(n_dp * tokens, width_here)

    gate = jnp.dot(normed_student, gate_weight, preferred_element_type=full)
    up = jnp.dot(normed_student, up_weight, preferred_element_type=full)
    sigma = jax.nn.sigmoid(gate)
    silu = gate * sigma
    act = (silu * up).astype(half)
    output = times_rows(act, down_weight).astype(half)
    dy, _ = lax.optimization_barrier((dy, output[:8, :128]))
    dy = jnp.swapaxes(dy, 0, 1).reshape(tokens, student_width)
    dh = jnp.dot(dy, down_weight, preferred_element_type=full)
    grad_gate = (dh * up * sigma * (1.0 + gate * (1.0 - sigma))).astype(half)
    grad_up = (dh * silu).astype(half)
    dn = (times_rows(grad_gate, gate_weight) + times_rows(grad_up, up_weight)).astype(half)
    output = jnp.swapaxes(output.reshape(blocks, n_mp, rows, student_width), 0, 1)
    output = exchange(output, "mp")
    dn, output = lax.optimization_barrier((dn, output))
    dn = exchange(dn.reshape(n_mp, mine_rows, student_width), "mp")
    output = jnp.sum(output.astype(full), axis=0)
    here = mp * mine_rows
    dproj = slope(
        dn,
        lax.dynamic_slice_in_dim(dy, here, mine_rows, 0),
        lax.dynamic_slice_in_dim(state, here, mine_rows, 0),
        student_gain,
        n_dp,
    )
    dproj = share(exchange(dproj, "dp"), "mp")
    adapter_grad = lax.dot_general(
        pooled_all,
        dproj.reshape(n_dp * tokens, out_cols),
        (((0,), (0,)), ((), ())),
        preferred_element_type=full,
    )

    state_rows = lax.dynamic_slice_in_dim(
        state.reshape(blocks, BLK, student_width), mp * rows, rows, 1
    )
    out_rows = (state_rows.astype(full) + output).astype(half)
    out_rows = jnp.concatenate([out_rows, state_rows[:1]], axis=0)
    back = lax.all_gather(out_rows, "dp", axis=0, tiled=False)[:, :blocks]
    back = back.reshape(n_dp * blocks, rows, student_width)
    mine = block_owner == dp
    picks = []
    for slot in range(slots):
        chosen = mine & (ranks == slot)
        index = jnp.sum(jnp.where(chosen, jnp.arange(chosen.shape[0], dtype=jnp.int32), 0))
        piece = lax.dynamic_index_in_dim(back, index, 0, False)
        picks.append(jnp.where(jnp.any(chosen), piece, jnp.zeros((), half)))
    student_out = jnp.stack(picks, axis=1)
    return (student_out[None], adapter_grad)


def solution(mesh):
    return jax.shard_map(
        on_device,
        mesh=mesh,
        in_specs=(
            P("dp", "mp"),
            P("mp", None),
            P("dp", "mp"),
            P("mp"),
            P("mp", None),
            P("dp"),
            P(),
            P("dp", "mp", None, None),
            P("dp", "mp", None, None),
            P(),
            P(None, "mp"),
            P(None, "mp"),
            P(None, "mp"),
        ),
        out_specs=(P("dp", "mp", None, None), P("mp", "dp")),
        check_vma=False,
    )
```

```python
import jax
import jax.numpy as jnp
from jax import lax
from jax.experimental import pallas as pl
from jax.experimental.pallas import tpu as pltpu
from jax.sharding import PartitionSpec as P

BLK = 128
epsilon = 1e-06
half = jnp.bfloat16
full = jnp.float32


def exchange(pieces, axis):
    return lax.all_to_all(pieces, axis, split_axis=0, concat_axis=0, tiled=True)


def share(piece, axis):
    size = lax.axis_size(axis)
    return exchange(jnp.broadcast_to(piece[None], (size,) + piece.shape), axis)


def three_parts(value):
    first = lax.reduce_precision(value, 8, 7)
    rest = value - first
    second = lax.reduce_precision(rest, 8, 7)
    return jnp.stack([first, second, rest - second]).astype(half)


def times_rows(left, right):
    return lax.dot_general(left, right, (((1,), (1,)), ((), ())), preferred_element_type=full)


SIDE = 4


def step(value, along_y, along_z):
    pairs = []
    for y in range(SIDE):
        for z in range(SIDE):
            to = ((y + along_y) % SIDE) * SIDE + (z + along_z) % SIDE
            pairs.append((y * SIDE + z, to))
    return lax.ppermute(value, "mp", pairs)


def terms_kernel(place, left, right, *refs):
    outs, held, sems = refs[:10], refs[10], refs[11]
    width = held.shape[2]
    y, z = place[0], place[1]

    def load(index):
        piece = lax.rem(y + index // SIDE, SIDE) * SIDE + lax.rem(index, SIDE)
        columns = pl.ds(pl.multiple_of(piece * width, width), width)
        return pltpu.make_async_copy(right.at[:, columns], held.at[index], sems.at[index])

    for index in range(SIDE * SIDE):
        load(index).start()

    @pl.loop(0, SIDE * SIDE)
    def _(index):
        load(index).wait()
        value = jnp.dot(left[...], held[index], preferred_element_type=full).astype(half)
        along_y, at_z = index // SIDE, lax.rem(index, SIDE)
        at_y, along_z = lax.rem(y + along_y, SIDE), lax.rem(at_z - z + SIDE, SIDE)
        for distance in range(SIDE):
            for block, away, at in ((0, along_y, at_z), (1, along_z, at_y)):

                @pl.when(away == distance)
                def _():
                    base, first = 5 * block, BLK * block
                    if distance == 2:
                        outs[base + 3][at] = value[first : first + BLK // 2]
                        outs[base + 4][at] = value[first + BLK // 2 : first + BLK]
                    else:
                        outs[base + min(distance, 2)][at] = value[first : first + BLK]


def merge_kernel(*refs):
    ins, outs = refs[:8], refs[8:]
    middle = BLK // 2
    for block in (0, 1):
        up, down, lower, upper = ins[4 * block : 4 * block + 4]
        to_up, to_down = outs[2 * block], outs[2 * block + 1]
        for piece in range(SIDE):
            to_up[piece, :middle] = (
                up[piece, :middle].astype(full) + lower[piece].astype(full)
            ).astype(half)
            to_up[piece, middle:] = up[piece, middle:]
            to_down[piece, :middle] = down[piece, :middle]
            to_down[piece, middle:] = (
                down[piece, middle:].astype(full) + upper[piece].astype(full)
            ).astype(half)


def gather_kernel(place, *refs):
    ins, outs = refs[:6], refs[8:]
    for block in (0, 1):
        kept, from_down, from_up = ins[3 * block : 3 * block + 3]
        here = place[1 - block]
        for distance in range(SIDE):
            at = lax.rem(here + distance, SIDE)
            value = kept[at].astype(full) + from_down[at].astype(full) + from_up[at].astype(full)
            out = outs[SIDE * block + distance]
            out[...] = value.astype(out.dtype)


def teacher_terms(attention, out_proj, mp, order):
    width = attention.shape[1]
    whole = pl.BlockSpec(memory_space=pltpu.VMEM)
    scalars = pl.BlockSpec(memory_space=pltpu.SMEM)
    anywhere = pl.BlockSpec(memory_space=pl.ANY)
    limit = pltpu.CompilerParams(vmem_limit_bytes=24 * 1024 * 1024)
    place = jnp.stack([mp // SIDE, mp % SIDE]).astype(jnp.int32)
    full_piece = jax.ShapeDtypeStruct((SIDE, BLK, width), half)
    half_piece = jax.ShapeDtypeStruct((SIDE, BLK // 2, width), half)
    moves = full_piece.size

    kept0, up0, down0, lower0, upper0, kept1, up1, down1, lower1, upper1 = pl.pallas_call(
        terms_kernel,
        in_specs=[scalars, whole, anywhere],
        out_specs=[whole] * 10,
        out_shape=[full_piece, full_piece, full_piece, half_piece, half_piece] * 2,
        scratch_shapes=[
            pltpu.VMEM((SIDE * SIDE, width, width), half),
            pltpu.SemaphoreType.DMA((SIDE * SIDE,)),
        ],
        compiler_params=limit,
        cost_estimate=pl.CostEstimate(
            flops=2 * attention.shape[0] * out_proj.size,
            bytes_accessed=2 * out_proj.size,
            transcendentals=0,
        ),
    )(place, attention, out_proj)
    lower0, upper0 = step(lower0, 1, 0), step(upper0, -1, 0)
    lower1, upper1 = step(lower1, 0, 1), step(upper1, 0, -1)
    up0, down0, up1, down1 = pl.pallas_call(
        merge_kernel,
        in_specs=[whole] * 8,
        out_specs=[whole] * 4,
        out_shape=[full_piece] * 4,
        compiler_params=limit,
        cost_estimate=pl.CostEstimate(
            flops=4 * moves, bytes_accessed=20 * moves, transcendentals=0
        ),
    )(up0, down0, lower0, upper0, up1, down1, lower1, upper1)
    from_down0, from_up0 = step(up0, 1, 0), step(down0, -1, 0)
    from_down1, from_up1 = step(up1, 0, 1), step(down1, 0, -1)
    sums = pl.pallas_call(
        gather_kernel,
        in_specs=[scalars] + [whole] * 6 + [anywhere] * 2,
        out_specs=[whole] * (2 * SIDE),
        out_shape=[
            jax.ShapeDtypeStruct((BLK, width), half if distance else full)
            for block in (0, 1)
            for distance in range(SIDE)
        ],
        compiler_params=limit,
        cost_estimate=pl.CostEstimate(
            flops=4 * moves, bytes_accessed=16 * moves, transcendentals=0
        ),
    )(place, kept0, from_down0, from_up0, kept1, from_down1, from_up1, *order)
    results = []
    for block in (0, 1):
        mine = sums[SIDE * block : SIDE * block + SIDE]
        arrived = [
            step(mine[d], 0, d) if block == 0 else step(mine[d], d, 0) for d in range(1, SIDE)
        ]
        results.append([mine[0]] + arrived)
    return results


def total(values):
    result = values[0].astype(full)
    for value in values[1:]:
        result = result + value.astype(full)
    return result


def backward_kernel(dy, down, gate, up, order, grad_gate, grad_up, dh):
    del order
    rows = 8
    for chunk in range(2):
        columns = pl.ds(chunk * (down.shape[1] // 2), down.shape[1] // 2)
        value = jnp.dot(dy[...], down[:, columns], preferred_element_type=full)
        for index in range(value.shape[0] // rows):
            to = (index % 2) * BLK + (index // 2) * rows
            dh[pl.ds(to, rows), columns] = value[index * rows : index * rows + rows]
    gate_val = gate[...]
    sigma = jax.nn.sigmoid(gate_val)
    grad_gate[...] = (dh[...] * up[...] * sigma * (1.0 + gate_val * (1.0 - sigma))).astype(half)
    grad_up[...] = (dh[...] * (gate_val * sigma)).astype(half)


def backward(dy, down, gate, up, order):
    whole = pl.BlockSpec(memory_space=pltpu.VMEM)
    shape = jax.ShapeDtypeStruct(gate.shape, half)
    return pl.pallas_call(
        backward_kernel,
        in_specs=[whole] * 4 + [pl.BlockSpec(memory_space=pl.ANY)],
        out_specs=[whole, whole],
        out_shape=[shape, shape],
        scratch_shapes=[pltpu.VMEM(gate.shape, full)],
        compiler_params=pltpu.CompilerParams(vmem_limit_bytes=24 * 1024 * 1024),
        cost_estimate=pl.CostEstimate(
            flops=2 * dy.shape[0] * down.size,
            bytes_accessed=2 * (down.size + dy.size) + 16 * gate.size,
            transcendentals=gate.size,
        ),
    )(dy, down, gate, up, order)


def spread_kernel(piece, order, out):
    del order
    for index in range(out.shape[0]):
        out[index] = piece[...]


def spread(piece, count, order):
    whole = pl.BlockSpec(memory_space=pltpu.VMEM)
    return pl.pallas_call(
        spread_kernel,
        in_specs=[whole, pl.BlockSpec(memory_space=pl.ANY)],
        out_specs=whole,
        out_shape=jax.ShapeDtypeStruct((count,) + piece.shape, piece.dtype),
        compiler_params=pltpu.CompilerParams(vmem_limit_bytes=16 * 1024 * 1024),
        cost_estimate=pl.CostEstimate(
            flops=0, bytes_accessed=4 * count * piece.size, transcendentals=0
        ),
    )(piece, order)


def home_kernel(terms, state, order, out):
    del order
    value = state[...].astype(full)
    for source in range(terms.shape[0]):
        value = value + terms[source].astype(full)
    rows = state.shape[0]
    out[pl.ds(0, rows), :] = value.astype(half)
    out[pl.ds(rows, rows), :] = jnp.zeros(state.shape, half)


def home(terms, state, order):
    rows, width = state.shape
    whole = pl.BlockSpec(memory_space=pltpu.VMEM)
    return pl.pallas_call(
        home_kernel,
        in_specs=[whole, whole, pl.BlockSpec(memory_space=pl.ANY)],
        out_specs=whole,
        out_shape=jax.ShapeDtypeStruct((2 * rows, width), half),
        compiler_params=pltpu.CompilerParams(vmem_limit_bytes=16 * 1024 * 1024),
        cost_estimate=pl.CostEstimate(
            flops=17 * rows * width, bytes_accessed=40 * rows * width, transcendentals=0
        ),
    )(terms, state, order)


def normalise_kernel(pieces, gain, order, state, normed):
    del order
    groups = state.shape[1] // pieces.shape[2]
    cols = pieces.shape[2]
    for block in range(state.shape[0] // BLK):
        rows = pl.ds(block * BLK, BLK)
        squares = jnp.zeros((BLK, 128), full)
        for group in range(groups):
            value = pieces[block * groups + group]
            state[rows, pl.ds(group * cols, cols)] = value
            wide = value.astype(full)
            wide = wide * wide
            for lane in range(0, cols, 128):
                squares = squares + wide[:, lane : lane + 128]
        mean = jnp.sum(squares, axis=1, keepdims=True) / state.shape[1]
        inverse = lax.rsqrt(mean + epsilon)
        for group in range(groups):
            at = pl.ds(group * cols, cols)
            wide = pieces[block * groups + group].astype(full)
            normed[rows, at] = (wide * inverse * gain[:, at]).astype(normed.dtype)


def normalise(pieces, gain, rows, width, order):
    whole = pl.BlockSpec(memory_space=pltpu.VMEM)
    shape = jax.ShapeDtypeStruct((rows, width), half)
    return pl.pallas_call(
        normalise_kernel,
        in_specs=[whole, whole, pl.BlockSpec(memory_space=pl.ANY)],
        out_specs=[whole, whole],
        out_shape=[shape, shape],
        compiler_params=pltpu.CompilerParams(vmem_limit_bytes=16 * 1024 * 1024),
        cost_estimate=pl.CostEstimate(
            flops=6 * rows * width, bytes_accessed=6 * rows * width, transcendentals=rows
        ),
    )(pieces, gain[None], order)


def slope_kernel(terms, dy, state, gain, out):
    rows, width = dy.shape
    cols = out.shape[2]
    wide = state[...].astype(full)
    inverse = lax.rsqrt(jnp.mean(wide * wide, axis=1, keepdims=True) + epsilon)
    dn = terms[0].astype(full)
    for source in range(1, terms.shape[0]):
        dn = dn + terms[source].astype(full)
    gained = gain[...] * dn
    mean = jnp.mean(gained * wide, axis=1, keepdims=True)
    dx = dy[...].astype(full) + inverse * gained - wide * (inverse * inverse * inverse) * mean
    for group in range(out.shape[0]):
        out[group] = dx[:, group * cols : (group + 1) * cols].astype(out.dtype)


def slope(terms, dy, state, gain, groups):
    rows, width = dy.shape
    whole = pl.BlockSpec(memory_space=pltpu.VMEM)
    return pl.pallas_call(
        slope_kernel,
        in_specs=[whole] * 4,
        out_specs=whole,
        out_shape=jax.ShapeDtypeStruct((groups, rows, width // groups), half),
        compiler_params=pltpu.CompilerParams(vmem_limit_bytes=16 * 1024 * 1024),
        cost_estimate=pl.CostEstimate(
            flops=30 * rows * width, bytes_accessed=40 * rows * width, transcendentals=rows
        ),
    )(terms, dy, state, gain[None])


def on_device(
    attention,
    out_proj,
    residual,
    final_gain,
    adapter_weight,
    token_slot,
    block_owner,
    student_hidden,
    cotangent,
    student_gain,
    gate_weight,
    up_weight,
    down_weight,
):
    tokens, width_here = attention.shape
    width_full = out_proj.shape[1]
    student_width = adapter_weight.shape[1]
    blocks = tokens // BLK
    n_mp = lax.axis_size("mp")
    n_dp = lax.axis_size("dp")
    dp = lax.axis_index("dp")
    mp = lax.axis_index("mp")
    slots = student_hidden.shape[2]
    rows = BLK // n_mp
    groups = n_mp // blocks
    cols = student_width // groups
    out_cols = student_width // n_dp
    mine_rows = blocks * rows

    owned = block_owner[None, :] == jnp.arange(n_dp, dtype=jnp.int32)[:, None]
    ranks = jnp.sum(jnp.where(owned, jnp.cumsum(owned.astype(jnp.int32), axis=1) - 1, 0), axis=0)
    place = block_owner * slots + ranks
    my_place = lax.dynamic_slice_in_dim(place, dp * blocks, blocks)

    both = jnp.concatenate([student_hidden[0], cotangent[0]], axis=1)
    everyone = lax.all_gather(both, "dp", axis=0, tiled=False)

    def fetch(offset):
        picked = []
        for k in range(blocks):
            at = (my_place[k] // slots, 0, my_place[k] % slots + offset, 0)
            piece = lax.dynamic_slice(everyone, at, (1, rows, 1, student_width))
            picked.append(piece.reshape(rows, student_width))
        return jnp.stack(picked)

    sh_rows = fetch(0)
    dy_rows = fetch(slots)
    dy = lax.all_gather(dy_rows, "mp", axis=0, tiled=False)

    hidden = residual.astype(full) + jnp.concatenate(
        [total(v) for v in teacher_terms(attention, out_proj, mp, (sh_rows, dy_rows))], axis=0
    )
    squares = jnp.sum(hidden * hidden, axis=1)
    gained_hidden = hidden * final_gain
    parts = jnp.einsum(
        "ktd,dce->kcte",
        gained_hidden.astype(half).reshape(blocks, BLK, width_here),
        adapter_weight.reshape(width_here, groups, cols),
        preferred_element_type=full,
    ).astype(half)
    sh_parts = jnp.swapaxes(sh_rows.reshape(blocks, rows, groups, cols), 1, 2)
    sq_parts = jnp.zeros((8, cols), half).at[:3, :tokens].set(three_parts(squares))
    message = jnp.concatenate(
        [
            parts,
            sh_parts,
            jnp.broadcast_to(sq_parts[None, None], (blocks, groups) + sq_parts.shape),
        ],
        axis=2,
    )
    message = exchange(message.reshape(n_mp, BLK + rows + 8, cols), "mp")
    token_proj = jnp.sum(message[:, :BLK].astype(full), axis=0)
    sh_here = message[:, BLK : BLK + rows].reshape(BLK, cols)
    squares_all = jnp.sum(message[:, BLK + rows : BLK + rows + 3].astype(full), axis=(0, 1))[:tokens]
    inverse_rms = lax.rsqrt(squares_all / width_full + epsilon)

    slots_block = token_slot.reshape(blocks, BLK)
    onehot = slots_block[:, None, :] == jnp.arange(BLK, dtype=jnp.int32)[None, :, None]
    counts = jnp.maximum(jnp.sum(onehot.astype(full), axis=2), 1.0)
    onehot = onehot.astype(half)
    my_block = mp // groups
    inv_block = lax.dynamic_index_in_dim(inverse_rms.reshape(blocks, BLK), my_block, 0, False)
    onehot_block = lax.dynamic_index_in_dim(onehot, my_block, 0, False)
    counts_block = lax.dynamic_index_in_dim(counts, my_block, 0, False)
    placed = jnp.dot(
        onehot_block, (token_proj * inv_block[:, None]).astype(half), preferred_element_type=full
    )
    placed = (placed / counts_block[:, None]).astype(half).astype(full)
    state_here = (sh_here.astype(full) + placed).astype(half)
    normed = (gained_hidden * inverse_rms[:, None]).astype(half).reshape(blocks, BLK, width_here)
    pooled = jnp.einsum("krt,ktd->krd", onehot, normed, preferred_element_type=full)
    pooled = (pooled / counts[:, :, None]).astype(half)
    pooled_all = lax.all_gather(pooled.reshape(n_mp, mine_rows, width_here), "dp", axis=0, tiled=False)
    pooled_all = jnp.swapaxes(pooled_all, 0, 1).reshape(n_dp * tokens, width_here)

    state, normed_student = normalise(
        share(state_here, "mp"), student_gain, tokens, student_width, pooled
    )

    gate = jnp.dot(normed_student, gate_weight, preferred_element_type=full)
    up = jnp.dot(normed_student, up_weight, preferred_element_type=full)
    sigma = jax.nn.sigmoid(gate)
    silu = gate * sigma
    act = (silu * up).astype(half)
    output = times_rows(act, down_weight).astype(half)
    grad_gate, grad_up = backward(dy.reshape(tokens, student_width), down_weight, gate, up, output)
    dn = (times_rows(grad_gate, gate_weight) + times_rows(grad_up, up_weight)).astype(half)
    output = jnp.swapaxes(output.reshape(blocks, n_mp, rows, student_width), 0, 1)
    output = exchange(output, "mp")
    dn, output = lax.optimization_barrier((dn, output))
    dn = exchange(dn.reshape(n_mp, mine_rows, student_width), "mp")
    here = mp * mine_rows
    dproj = slope(
        dn,
        lax.dynamic_slice(
            dy, ((mp % groups) * blocks, mp // groups, 0, 0), (blocks, 1, rows, student_width)
        ).reshape(mine_rows, student_width),
        lax.dynamic_slice_in_dim(state, here, mine_rows, 0),
        student_gain,
        n_dp,
    )
    state_rows = lax.dynamic_slice_in_dim(
        state.reshape(blocks, BLK, student_width), mp * rows, rows, 1
    )
    out_rows = home(
        output.reshape(n_mp, mine_rows, student_width),
        state_rows.reshape(mine_rows, student_width),
        dproj,
    )
    dproj = exchange(spread(exchange(dproj, "dp"), n_mp, out_rows), "mp")
    adapter_grad = lax.dot_general(
        pooled_all,
        dproj.reshape(n_dp * tokens, out_cols),
        (((0,), (0,)), ((), ())),
        preferred_element_type=full,
    )

    back = lax.all_gather(out_rows, "dp", axis=0, tiled=False)
    mine = block_owner == dp
    picks = []
    for slot in range(slots):
        chosen = mine & (ranks == slot)
        index = jnp.sum(jnp.where(chosen, jnp.arange(chosen.shape[0], dtype=jnp.int32), 0))
        at = (index // blocks, (index % blocks) * rows, 0)
        piece = lax.dynamic_slice(back, at, (1, rows, student_width))[0]
        picks.append(jnp.where(jnp.any(chosen), piece, jnp.zeros((), half)))
    student_out = jnp.stack(picks, axis=1)
    return (student_out[None], adapter_grad)


def solution(mesh):
    return jax.shard_map(
        on_device,
        mesh=mesh,
        in_specs=(
            P("dp", "mp"),
            P("mp", None),
            P("dp", "mp"),
            P("mp"),
            P("mp", None),
            P("dp"),
            P(),
            P("dp", "mp", None, None),
            P("dp", "mp", None, None),
            P(),
            P(None, "mp"),
            P(None, "mp"),
            P(None, "mp"),
        ),
        out_specs=(P("dp", "mp", None, None), P("mp", "dp")),
        check_vma=False,
    )
```

```python
import jax
import jax.numpy as jnp
from jax import lax
from jax.experimental import pallas as pl
from jax.experimental.pallas import tpu as pltpu
from jax.sharding import PartitionSpec as P

BLK = 128
epsilon = 1e-06
half = jnp.bfloat16
full = jnp.float32


def exchange(pieces, axis):
    return lax.all_to_all(pieces, axis, split_axis=0, concat_axis=0, tiled=True)


def three_parts(value):
    first = lax.reduce_precision(value, 8, 7)
    rest = value - first
    second = lax.reduce_precision(rest, 8, 7)
    return jnp.stack([first, second, rest - second]).astype(half)


def times_rows(left, right):
    return lax.dot_general(left, right, (((1,), (1,)), ((), ())), preferred_element_type=full)


SIDE = 4


def step(value, along_y, along_z):
    pairs = []
    for y in range(SIDE):
        for z in range(SIDE):
            to = ((y + along_y) % SIDE) * SIDE + (z + along_z) % SIDE
            pairs.append((y * SIDE + z, to))
    return lax.ppermute(value, "mp", pairs)


def terms_kernel(place, left, right, *refs):
    outs, held, sems = refs[:10], refs[10], refs[11]
    width = held.shape[2]
    y, z = place[0], place[1]

    def load(index):
        piece = lax.rem(y + index // SIDE, SIDE) * SIDE + lax.rem(index, SIDE)
        columns = pl.ds(pl.multiple_of(piece * width, width), width)
        return pltpu.make_async_copy(right.at[:, columns], held.at[index], sems.at[index])

    for index in range(SIDE * SIDE):
        load(index).start()

    @pl.loop(0, SIDE * SIDE)
    def _(index):
        load(index).wait()
        value = jnp.dot(left[...], held[index], preferred_element_type=full).astype(half)
        along_y, at_z = index // SIDE, lax.rem(index, SIDE)
        at_y, along_z = lax.rem(y + along_y, SIDE), lax.rem(at_z - z + SIDE, SIDE)
        for distance in range(SIDE):
            for block, away, at in ((0, along_y, at_z), (1, along_z, at_y)):

                @pl.when(away == distance)
                def _():
                    base, first = 5 * block, BLK * block
                    if distance == 2:
                        outs[base + 3][at] = value[first : first + BLK // 2]
                        outs[base + 4][at] = value[first + BLK // 2 : first + BLK]
                    else:
                        outs[base + min(distance, 2)][at] = value[first : first + BLK]


def merge_kernel(*refs):
    ins, outs = refs[:8], refs[8:]
    middle = BLK // 2
    for block in (0, 1):
        up, down, lower, upper = ins[4 * block : 4 * block + 4]
        to_up, to_down = outs[2 * block], outs[2 * block + 1]
        to_up[0, :middle] = (up[0, :middle].astype(full) + lower[0].astype(full)).astype(half)
        to_up[0, middle:] = up[0, middle:]
        to_down[0, :middle] = down[0, :middle]
        to_down[0, middle:] = (down[0, middle:].astype(full) + upper[0].astype(full)).astype(half)


def gather_kernel(place, *refs):
    ins, outs = refs[:6], refs[8:]
    for block in (0, 1):
        kept, from_down, from_up = ins[3 * block : 3 * block + 3]
        here = place[1 - block]
        for distance in range(SIDE):
            at = lax.rem(here + distance, SIDE)
            value = kept[at].astype(full) + from_down[at].astype(full) + from_up[at].astype(full)
            out = outs[SIDE * block + distance]
            out[...] = value.astype(out.dtype)


def teacher_terms(attention, out_proj, mp, order):
    width = attention.shape[1]
    whole = pl.BlockSpec(memory_space=pltpu.VMEM)
    scalars = pl.BlockSpec(memory_space=pltpu.SMEM)
    anywhere = pl.BlockSpec(memory_space=pl.ANY)
    limit = pltpu.CompilerParams(vmem_limit_bytes=40 * 1024 * 1024)
    place = jnp.stack([mp // SIDE, mp % SIDE]).astype(jnp.int32)
    full_piece = jax.ShapeDtypeStruct((SIDE, BLK, width), half)
    half_piece = jax.ShapeDtypeStruct((SIDE, BLK // 2, width), half)
    moves = full_piece.size
    one_piece = pl.BlockSpec((1, BLK, width), lambda i: (i, 0, 0))
    one_half = pl.BlockSpec((1, BLK // 2, width), lambda i: (i, 0, 0))

    kept0, up0, down0, lower0, upper0, kept1, up1, down1, lower1, upper1 = pl.pallas_call(
        terms_kernel,
        in_specs=[scalars, whole, pl.BlockSpec(memory_space=pltpu.HBM)],
        out_specs=[whole] * 10,
        out_shape=[full_piece, full_piece, full_piece, half_piece, half_piece] * 2,
        scratch_shapes=[
            pltpu.VMEM((SIDE * SIDE, width, width), half),
            pltpu.SemaphoreType.DMA((SIDE * SIDE,)),
        ],
        compiler_params=pltpu.CompilerParams(vmem_limit_bytes=48 * 1024 * 1024),
        cost_estimate=pl.CostEstimate(
            flops=2 * attention.shape[0] * out_proj.size,
            bytes_accessed=2 * out_proj.size,
            transcendentals=0,
        ),
    )(place, attention, out_proj)
    lower0, upper0 = step(lower0, 1, 0), step(upper0, -1, 0)
    lower1, upper1 = step(lower1, 0, 1), step(upper1, 0, -1)
    up0, down0, up1, down1 = pl.pallas_call(
        merge_kernel,
        grid=(SIDE,),
        in_specs=[one_piece, one_piece, one_half, one_half] * 2,
        out_specs=[one_piece] * 4,
        out_shape=[full_piece] * 4,
        compiler_params=limit,
        cost_estimate=pl.CostEstimate(
            flops=4 * moves, bytes_accessed=20 * moves, transcendentals=0
        ),
    )(up0, down0, lower0, upper0, up1, down1, lower1, upper1)
    from_down0, from_up0 = step(up0, 1, 0), step(down0, -1, 0)
    from_down1, from_up1 = step(up1, 0, 1), step(down1, 0, -1)
    sums = pl.pallas_call(
        gather_kernel,
        in_specs=[scalars] + [whole] * 6 + [anywhere] * 2,
        out_specs=[whole] * (2 * SIDE),
        out_shape=[
            jax.ShapeDtypeStruct((BLK, width), half if distance else full)
            for block in (0, 1)
            for distance in range(SIDE)
        ],
        compiler_params=limit,
        cost_estimate=pl.CostEstimate(
            flops=4 * moves, bytes_accessed=16 * moves, transcendentals=0
        ),
    )(place, kept0, from_down0, from_up0, kept1, from_down1, from_up1, *order)
    results = []
    for block in (0, 1):
        mine = sums[SIDE * block : SIDE * block + SIDE]
        arrived = [
            step(mine[d], 0, d) if block == 0 else step(mine[d], d, 0) for d in range(1, SIDE)
        ]
        results.append([mine[0]] + arrived)
    return results


def total(values):
    result = values[0].astype(full)
    for value in values[1:]:
        result = result + value.astype(full)
    return result


def backward_kernel(dy, down, gate, up, order, grad_gate, grad_up, dh):
    del order
    rows = 8
    for chunk in range(2):
        columns = pl.ds(chunk * (down.shape[1] // 2), down.shape[1] // 2)
        value = jnp.dot(dy[...], down[:, columns], preferred_element_type=full)
        for index in range(value.shape[0] // rows):
            to = (index % 2) * BLK + (index // 2) * rows
            dh[pl.ds(to, rows), columns] = value[index * rows : index * rows + rows]
    gate_val = gate[...]
    sigma = jax.nn.sigmoid(gate_val)
    grad_gate[...] = (dh[...] * up[...] * sigma * (1.0 + gate_val * (1.0 - sigma))).astype(half)
    grad_up[...] = (dh[...] * (gate_val * sigma)).astype(half)


def backward(dy, down, gate, up, order):
    whole = pl.BlockSpec(memory_space=pltpu.VMEM)
    shape = jax.ShapeDtypeStruct(gate.shape, half)
    return pl.pallas_call(
        backward_kernel,
        in_specs=[whole] * 4 + [pl.BlockSpec(memory_space=pl.ANY)],
        out_specs=[whole, whole],
        out_shape=[shape, shape],
        scratch_shapes=[pltpu.VMEM(gate.shape, full)],
        compiler_params=pltpu.CompilerParams(vmem_limit_bytes=56 * 1024 * 1024),
        cost_estimate=pl.CostEstimate(
            flops=2 * dy.shape[0] * down.size,
            bytes_accessed=2 * (down.size + dy.size) + 16 * gate.size,
            transcendentals=gate.size,
        ),
    )(dy, down, gate, up, order)


def spread_kernel(piece, out, sems):
    copies = [
        pltpu.make_async_copy(piece, out.at[to], sems.at[to]) for to in range(out.shape[0])
    ]
    for copy in copies:
        copy.start()
    for copy in copies:
        copy.wait()


def spread(piece, count):
    whole = pl.BlockSpec(memory_space=pltpu.VMEM)
    return pl.pallas_call(
        spread_kernel,
        in_specs=[whole],
        out_specs=pl.BlockSpec(memory_space=pltpu.HBM),
        scratch_shapes=[pltpu.SemaphoreType.DMA((count,))],
        out_shape=jax.ShapeDtypeStruct((count,) + piece.shape, piece.dtype),
        compiler_params=pltpu.CompilerParams(vmem_limit_bytes=16 * 1024 * 1024),
        cost_estimate=pl.CostEstimate(
            flops=0, bytes_accessed=4 * count * piece.size, transcendentals=0
        ),
    )(piece)


def home_kernel(terms, state, out):
    value = state[...].astype(full)
    for source in range(terms.shape[0]):
        value = value + terms[source].astype(full)
    rows = state.shape[0]
    out[pl.ds(0, rows), :] = value.astype(half)
    out[pl.ds(rows, rows), :] = jnp.zeros(state.shape, half)


def home(terms, state):
    rows, width = state.shape
    whole = pl.BlockSpec(memory_space=pltpu.VMEM)
    return pl.pallas_call(
        home_kernel,
        in_specs=[whole, whole],
        out_specs=whole,
        out_shape=jax.ShapeDtypeStruct((2 * rows, width), half),
        compiler_params=pltpu.CompilerParams(vmem_limit_bytes=16 * 1024 * 1024),
        cost_estimate=pl.CostEstimate(
            flops=17 * rows * width, bytes_accessed=40 * rows * width, transcendentals=0
        ),
    )(terms, state)


def pool_kernel(place, message, token_slot, out, inverse, sh, weights, state, sems):
    sources, _, cols = message.shape
    rows = BLK // sources
    token_proj = message[0, :BLK].astype(full)
    for source in range(1, sources):
        token_proj = token_proj + message[source, :BLK].astype(full)
    squares = jnp.zeros((rows, cols), full)
    for source in range(sources):
        tail = message[source, BLK:].astype(full)
        sh[pl.ds(source * rows, rows), :] = tail[:rows]
        squares = squares + tail[rows:]
    tokens = token_slot.shape[1]
    squares = jnp.sum(squares, axis=0, keepdims=True)[:, :tokens]
    inverse[...] = lax.rsqrt(squares / place[1].astype(full) + epsilon)
    slots = jnp.where(place[0] == 0, token_slot[:, :BLK], token_slot[:, BLK:])
    scale = jnp.where(place[0] == 0, inverse[:, :BLK], inverse[:, BLK:])
    hits = slots == lax.broadcasted_iota(jnp.int32, (BLK, BLK), 0)
    counts = jnp.maximum(jnp.sum(hits.astype(full), axis=1, keepdims=True), 1.0)
    weights[...] = jnp.where(hits, scale, 0.0)
    first = weights[...].astype(half)
    second = (weights[...] - lax.reduce_precision(weights[...], 8, 7)).astype(half)
    token_proj = token_proj.astype(half)
    placed = jnp.dot(first, token_proj, preferred_element_type=full)
    placed = placed + jnp.dot(second, token_proj, preferred_element_type=full)
    placed = (placed / counts).astype(half).astype(full)
    state[...] = (sh[...] + placed).astype(half)
    copies = [
        pltpu.make_async_copy(state, out.at[to], sems.at[to]) for to in range(sources)
    ]
    for copy in copies:
        copy.start()
    for copy in copies:
        copy.wait()


def pool(message, token_slot, block, width_full):
    sources, _, cols = message.shape
    whole = pl.BlockSpec(memory_space=pltpu.VMEM)
    tokens = token_slot.shape[0]
    place = jnp.stack([block, jnp.full_like(block, width_full)]).astype(jnp.int32)
    return pl.pallas_call(
        pool_kernel,
        in_specs=[pl.BlockSpec(memory_space=pltpu.SMEM), whole, whole],
        out_specs=[pl.BlockSpec(memory_space=pltpu.HBM), whole],
        out_shape=[
            jax.ShapeDtypeStruct((sources, BLK, cols), half),
            jax.ShapeDtypeStruct((1, tokens), full),
        ],
        scratch_shapes=[
            pltpu.VMEM((BLK, cols), full),
            pltpu.VMEM((BLK, BLK), full),
            pltpu.VMEM((BLK, cols), half),
            pltpu.SemaphoreType.DMA((sources,)),
        ],
        compiler_params=pltpu.CompilerParams(vmem_limit_bytes=40 * 1024 * 1024),
        cost_estimate=pl.CostEstimate(
            flops=6 * message.size, bytes_accessed=4 * message.size, transcendentals=tokens
        ),
    )(place, message, token_slot[None])


def forward_kernel(
    pieces, gain, order, gate_hbm, up_hbm, down_hbm, state, gate, up, out, normed, act, held, sems
):
    del order
    loads = []
    for index, source in enumerate((gate_hbm, up_hbm, down_hbm)):
        part = source.shape[0] // 3
        for third in range(3):
            at = pl.ds(third * part, part)
            load = pltpu.make_async_copy(
                source.at[at], held.at[index, at], sems.at[3 * index + third]
            )
            load.start()
            loads.append(load)
    gate_w, up_w, down_w = held.at[0], held.at[1], held.at[2]
    cols = pieces.shape[2]
    groups = state.shape[1] // cols
    for block in range(state.shape[0] // BLK):
        rows = pl.ds(block * BLK, BLK)
        squares = jnp.zeros((BLK, 128), full)
        for group in range(groups):
            value = pieces[block * groups + group]
            state[rows, pl.ds(group * cols, cols)] = value
            wide = value.astype(full)
            wide = wide * wide
            for lane in range(0, cols, 128):
                squares = squares + wide[:, lane : lane + 128]
        mean = jnp.sum(squares, axis=1, keepdims=True) / state.shape[1]
        inverse = lax.rsqrt(mean + epsilon)
        for group in range(groups):
            at = pl.ds(group * cols, cols)
            wide = pieces[block * groups + group].astype(full)
            normed[rows, at] = (wide * inverse * gain[:, at]).astype(normed.dtype)
    for load in loads[:6]:
        load.wait()
    chunk = gate.shape[1] // 2
    for index in range(2):
        at = pl.ds(index * chunk, chunk)
        gate_val = jnp.dot(normed[...], gate_w[:, at], preferred_element_type=full)
        up_val = jnp.dot(normed[...], up_w[:, at], preferred_element_type=full)
        gate[:, at] = gate_val
        up[:, at] = up_val
        act[:, at] = (gate_val * jax.nn.sigmoid(gate_val) * up_val).astype(half)
    for load in loads[6:]:
        load.wait()
    rows = out.shape[1] // 2
    wide_chunk = 512

    @pl.loop(0, state.shape[1] // wide_chunk)
    def _(index):
        at = pl.ds(pl.multiple_of(index * wide_chunk, wide_chunk), wide_chunk)
        value = times_rows(act[...], down_w[at, :])
        for to in range(out.shape[0]):
            first = value[to * rows : to * rows + rows]
            second = value[BLK + to * rows : BLK + to * rows + rows]
            out[to, :, at] = jnp.concatenate([first, second], axis=0).astype(half)


def forward(pieces, gain, gate_w, up_w, down_w, order):
    width, hidden = gate_w.shape
    n_mp = pieces.shape[0]
    rows = 2 * BLK
    whole = pl.BlockSpec(memory_space=pltpu.VMEM)
    return pl.pallas_call(
        forward_kernel,
        in_specs=[whole, whole, pl.BlockSpec(memory_space=pl.ANY)]
        + [pl.BlockSpec(memory_space=pltpu.HBM)] * 3,
        out_specs=[whole] * 4,
        out_shape=[
            jax.ShapeDtypeStruct((rows, width), half),
            jax.ShapeDtypeStruct((rows, hidden), full),
            jax.ShapeDtypeStruct((rows, hidden), full),
            jax.ShapeDtypeStruct((n_mp, rows // n_mp, width), half),
        ],
        scratch_shapes=[
            pltpu.VMEM((rows, width), half),
            pltpu.VMEM((rows, hidden), half),
            pltpu.VMEM((3, width, hidden), half),
            pltpu.SemaphoreType.DMA((9,)),
        ],
        compiler_params=pltpu.CompilerParams(vmem_limit_bytes=56 * 1024 * 1024),
        cost_estimate=pl.CostEstimate(
            flops=6 * rows * width * hidden,
            bytes_accessed=6 * width * hidden + 10 * rows * width,
            transcendentals=rows * hidden,
        ),
    )(pieces, gain[None], order, gate_w, up_w, down_w)


def slope_kernel(terms, dy, state, gain, order, out):
    del order
    rows, width = dy.shape
    cols = out.shape[2]
    wide = state[...].astype(full)
    inverse = lax.rsqrt(jnp.mean(wide * wide, axis=1, keepdims=True) + epsilon)
    dn = terms[0].astype(full)
    for source in range(1, terms.shape[0]):
        dn = dn + terms[source].astype(full)
    gained = gain[...] * dn
    mean = jnp.mean(gained * wide, axis=1, keepdims=True)
    dx = dy[...].astype(full) + inverse * gained - wide * (inverse * inverse * inverse) * mean
    for group in range(out.shape[0]):
        out[group] = dx[:, group * cols : (group + 1) * cols].astype(out.dtype)


def slope(terms, dy, state, gain, groups, order):
    rows, width = dy.shape
    whole = pl.BlockSpec(memory_space=pltpu.VMEM)
    return pl.pallas_call(
        slope_kernel,
        in_specs=[whole] * 4 + [pl.BlockSpec(memory_space=pl.ANY)],
        out_specs=whole,
        out_shape=jax.ShapeDtypeStruct((groups, rows, width // groups), half),
        compiler_params=pltpu.CompilerParams(vmem_limit_bytes=16 * 1024 * 1024),
        cost_estimate=pl.CostEstimate(
            flops=30 * rows * width, bytes_accessed=40 * rows * width, transcendentals=rows
        ),
    )(terms, dy, state, gain[None], order)


def on_device(
    attention,
    out_proj,
    residual,
    final_gain,
    adapter_weight,
    token_slot,
    block_owner,
    student_hidden,
    cotangent,
    student_gain,
    gate_weight,
    up_weight,
    down_weight,
):
    tokens, width_here = attention.shape
    width_full = out_proj.shape[1]
    student_width = adapter_weight.shape[1]
    blocks = tokens // BLK
    n_mp = lax.axis_size("mp")
    n_dp = lax.axis_size("dp")
    dp = lax.axis_index("dp")
    mp = lax.axis_index("mp")
    slots = student_hidden.shape[2]
    rows = BLK // n_mp
    groups = n_mp // blocks
    cols = student_width // groups
    out_cols = student_width // n_dp
    mine_rows = blocks * rows

    owned = block_owner[None, :] == jnp.arange(n_dp, dtype=jnp.int32)[:, None]
    ranks = jnp.sum(jnp.where(owned, jnp.cumsum(owned.astype(jnp.int32), axis=1) - 1, 0), axis=0)
    place = block_owner * slots + ranks
    my_place = lax.dynamic_slice_in_dim(place, dp * blocks, blocks)

    both = jnp.concatenate([student_hidden[0], cotangent[0]], axis=1)
    everyone = lax.all_gather(both, "dp", axis=0, tiled=False)

    def fetch(offset):
        picked = []
        for k in range(blocks):
            at = (my_place[k] // slots, 0, my_place[k] % slots + offset, 0)
            piece = lax.dynamic_slice(everyone, at, (1, rows, 1, student_width))
            picked.append(piece.reshape(rows, student_width))
        return jnp.stack(picked)

    sh_rows = fetch(0)
    dy_rows = fetch(slots)
    dy = lax.all_gather(dy_rows, "mp", axis=0, tiled=False)

    hidden = residual.astype(full) + jnp.concatenate(
        [total(v) for v in teacher_terms(attention, out_proj, mp, (sh_rows, dy_rows))], axis=0
    )
    squares = jnp.sum(hidden * hidden, axis=1)
    gained_hidden = hidden * final_gain
    parts = jnp.einsum(
        "ktd,dce->kcte",
        gained_hidden.astype(half).reshape(blocks, BLK, width_here),
        adapter_weight.reshape(width_here, groups, cols),
        preferred_element_type=full,
    ).astype(half)
    sh_parts = jnp.swapaxes(sh_rows.reshape(blocks, rows, groups, cols), 1, 2)
    sq_parts = jnp.zeros((8, cols), half).at[:3, :tokens].set(three_parts(squares))
    message = jnp.concatenate(
        [
            parts,
            sh_parts,
            jnp.broadcast_to(sq_parts[None, None], (blocks, groups) + sq_parts.shape),
        ],
        axis=2,
    )
    message = exchange(message.reshape(n_mp, BLK + rows + 8, cols), "mp")
    states, inverse_rms = pool(message, token_slot, mp // groups, width_full)
    states = exchange(states, "mp")

    slots_block = token_slot.reshape(blocks, BLK)
    onehot = slots_block[:, None, :] == jnp.arange(BLK, dtype=jnp.int32)[None, :, None]
    counts = jnp.maximum(jnp.sum(onehot.astype(full), axis=2), 1.0)
    onehot = onehot.astype(half)
    normed = (gained_hidden * inverse_rms.reshape(tokens, 1)).astype(half).reshape(blocks, BLK, width_here)
    pooled = jnp.einsum("krt,ktd->krd", onehot, normed, preferred_element_type=full)
    pooled = (pooled / counts[:, :, None]).astype(half)
    pooled_all = lax.all_gather(pooled.reshape(n_mp, mine_rows, width_here), "dp", axis=0, tiled=False)
    pooled_all = jnp.swapaxes(pooled_all, 0, 1).reshape(n_dp * tokens, width_here)

    state, gate, up, output = forward(
        states, student_gain, gate_weight, up_weight, down_weight, pooled
    )
    grad_gate, grad_up = backward(dy.reshape(tokens, student_width), down_weight, gate, up, output)
    dn = (times_rows(grad_gate, gate_weight) + times_rows(grad_up, up_weight)).astype(half)
    output = exchange(output, "mp")
    dn, output = lax.optimization_barrier((dn, output))
    dn = exchange(dn.reshape(n_mp, mine_rows, student_width), "mp")
    here = mp * mine_rows
    state_rows = lax.dynamic_slice_in_dim(
        state.reshape(blocks, BLK, student_width), mp * rows, rows, 1
    )
    out_rows = home(output, state_rows.reshape(mine_rows, student_width))
    dproj = slope(
        dn,
        lax.dynamic_slice(
            dy, ((mp % groups) * blocks, mp // groups, 0, 0), (blocks, 1, rows, student_width)
        ).reshape(mine_rows, student_width),
        lax.dynamic_slice_in_dim(state, here, mine_rows, 0),
        student_gain,
        n_dp,
        out_rows,
    )
    dproj = exchange(spread(exchange(dproj, "dp"), n_mp), "mp")
    adapter_grad = lax.dot_general(
        pooled_all,
        dproj.reshape(n_dp * tokens, out_cols),
        (((0,), (0,)), ((), ())),
        preferred_element_type=full,
    )

    back = lax.all_gather(out_rows, "dp", axis=0, tiled=False)
    mine = block_owner == dp
    picks = []
    for slot in range(slots):
        chosen = mine & (ranks == slot)
        index = jnp.sum(jnp.where(chosen, jnp.arange(chosen.shape[0], dtype=jnp.int32), 0))
        at = (index // blocks, (index % blocks) * rows, 0)
        piece = lax.dynamic_slice(back, at, (1, rows, student_width))[0]
        picks.append(jnp.where(jnp.any(chosen), piece, jnp.zeros((), half)))
    student_out = jnp.stack(picks, axis=1)
    return (student_out[None], adapter_grad)


def solution(mesh):
    return jax.shard_map(
        on_device,
        mesh=mesh,
        in_specs=(
            P("dp", "mp"),
            P("mp", None),
            P("dp", "mp"),
            P("mp"),
            P("mp", None),
            P("dp"),
            P(),
            P("dp", "mp", None, None),
            P("dp", "mp", None, None),
            P(),
            P(None, "mp"),
            P(None, "mp"),
            P(None, "mp"),
        ),
        out_specs=(P("dp", "mp", None, None), P("mp", "dp")),
        check_vma=False,
    )
```

```python
import jax
import jax.numpy as jnp
from jax import lax
from jax.experimental import pallas as pl
from jax.experimental.pallas import tpu as pltpu
from jax.sharding import PartitionSpec as P

BLK = 128
epsilon = 1e-06
half = jnp.bfloat16
full = jnp.float32


def exchange(pieces, axis):
    return lax.all_to_all(pieces, axis, split_axis=0, concat_axis=0, tiled=True)


def three_parts(value):
    first = lax.reduce_precision(value, 8, 7)
    rest = value - first
    second = lax.reduce_precision(rest, 8, 7)
    return jnp.stack([first, second, rest - second]).astype(half)


def times_rows(left, right):
    return lax.dot_general(left, right, (((1,), (1,)), ((), ())), preferred_element_type=full)


SIDE = 4


def step(value, along_y, along_z):
    pairs = []
    for y in range(SIDE):
        for z in range(SIDE):
            to = ((y + along_y) % SIDE) * SIDE + (z + along_z) % SIDE
            pairs.append((y * SIDE + z, to))
    return lax.ppermute(value, "mp", pairs)


def far_kernel(place, left, right, lower0, upper0, lower1, upper1, held, sems):
    width = held.shape[2]
    y, z = lax.rem(place[0] + 2, SIDE), lax.rem(place[1] + 2, SIDE)
    middle = BLK // 2
    loads = []
    for index in range(2 * SIDE):
        piece = y * SIDE + index if index < SIDE else (index - SIDE) * SIDE + z
        columns = pl.ds(pl.multiple_of(piece * width, width), width)
        load = pltpu.make_async_copy(right.at[:, columns], held.at[index], sems.at[index])
        load.start()
        loads.append(load)
    for index in range(2 * SIDE):
        loads[index].wait()
        block, at = index // SIDE, index % SIDE
        value = jnp.dot(
            left[pl.ds(block * BLK, BLK), :], held[index], preferred_element_type=full
        ).astype(half)
        lower, upper = (lower0, upper0) if block == 0 else (lower1, upper1)
        lower[at] = value[:middle]
        upper[at] = value[middle:]


def near_kernel(place, left, right, kept0, up0, down0, kept1, up1, down1, held, sems):
    outs = {0: (kept0, kept1), 1: (up0, up1), 3: (down0, down1)}
    width = held.shape[2]
    y, z = place[0], place[1]

    def load(index):
        piece = lax.rem(y + index // SIDE, SIDE) * SIDE + lax.rem(index, SIDE)
        columns = pl.ds(pl.multiple_of(piece * width, width), width)
        return pltpu.make_async_copy(right.at[:, columns], held.at[index], sems.at[index])

    for index in range(SIDE * SIDE):
        load(index).start()

    @pl.loop(0, SIDE * SIDE)
    def _(index):
        load(index).wait()
        value = jnp.dot(left[...], held[index], preferred_element_type=full).astype(half)
        along_y, at_z = index // SIDE, lax.rem(index, SIDE)
        at_y, along_z = lax.rem(y + along_y, SIDE), lax.rem(at_z - z + SIDE, SIDE)
        for distance, (first, second) in outs.items():

            @pl.when(along_y == distance)
            def _():
                first[at_z] = value[:BLK]

            @pl.when(along_z == distance)
            def _():
                second[at_y] = value[BLK:]


def merge_kernel(*refs):
    ins, outs = refs[:8], refs[8:]
    middle = BLK // 2
    for block in (0, 1):
        up, down, lower, upper = ins[4 * block : 4 * block + 4]
        to_up, to_down = outs[2 * block], outs[2 * block + 1]
        to_up[0, :middle] = (up[0, :middle].astype(full) + lower[0].astype(full)).astype(half)
        to_up[0, middle:] = up[0, middle:]
        to_down[0, :middle] = down[0, :middle]
        to_down[0, middle:] = (down[0, middle:].astype(full) + upper[0].astype(full)).astype(half)


def gather_kernel(place, *refs):
    ins, outs = refs[:6], refs[8:]
    for block in (0, 1):
        kept, from_down, from_up = ins[3 * block : 3 * block + 3]
        here = place[1 - block]
        for distance in range(SIDE):
            at = lax.rem(here + distance, SIDE)
            value = kept[at].astype(full) + from_down[at].astype(full) + from_up[at].astype(full)
            out = outs[SIDE * block + distance]
            out[...] = value.astype(out.dtype)


def teacher_terms(attention, out_proj, mp, order):
    width = attention.shape[1]
    whole = pl.BlockSpec(memory_space=pltpu.VMEM)
    scalars = pl.BlockSpec(memory_space=pltpu.SMEM)
    anywhere = pl.BlockSpec(memory_space=pl.ANY)
    limit = pltpu.CompilerParams(vmem_limit_bytes=40 * 1024 * 1024)
    place = jnp.stack([mp // SIDE, mp % SIDE]).astype(jnp.int32)
    full_piece = jax.ShapeDtypeStruct((SIDE, BLK, width), half)
    half_piece = jax.ShapeDtypeStruct((SIDE, BLK // 2, width), half)
    moves = full_piece.size
    one_piece = pl.BlockSpec((1, BLK, width), lambda i: (i, 0, 0))
    one_half = pl.BlockSpec((1, BLK // 2, width), lambda i: (i, 0, 0))

    def terms(kernel, pieces, count, blocks):
        return pl.pallas_call(
            kernel,
            in_specs=[scalars, whole, pl.BlockSpec(memory_space=pltpu.HBM)],
            out_specs=[whole] * len(pieces),
            out_shape=pieces,
            scratch_shapes=[
                pltpu.VMEM((count, width, width), half),
                pltpu.SemaphoreType.DMA((count,)),
            ],
            compiler_params=pltpu.CompilerParams(vmem_limit_bytes=48 * 1024 * 1024),
            cost_estimate=pl.CostEstimate(
                flops=2 * blocks * BLK * count * width * width,
                bytes_accessed=2 * count * width * width,
                transcendentals=0,
            ),
        )(place, attention, out_proj)

    lower0, upper0, lower1, upper1 = terms(far_kernel, [half_piece] * 4, 2 * SIDE, 1)
    kept0, up0, down0, kept1, up1, down1 = terms(near_kernel, [full_piece] * 6, SIDE * SIDE, 2)
    lower0, upper0 = step(lower0, 1, 0), step(upper0, -1, 0)
    lower1, upper1 = step(lower1, 0, 1), step(upper1, 0, -1)
    up0, down0, up1, down1 = pl.pallas_call(
        merge_kernel,
        grid=(SIDE,),
        in_specs=[one_piece, one_piece, one_half, one_half] * 2,
        out_specs=[one_piece] * 4,
        out_shape=[full_piece] * 4,
        compiler_params=limit,
        cost_estimate=pl.CostEstimate(
            flops=4 * moves, bytes_accessed=20 * moves, transcendentals=0
        ),
    )(up0, down0, lower0, upper0, up1, down1, lower1, upper1)
    from_down0, from_up0 = step(up0, 1, 0), step(down0, -1, 0)
    from_down1, from_up1 = step(up1, 0, 1), step(down1, 0, -1)
    sums = pl.pallas_call(
        gather_kernel,
        in_specs=[scalars] + [whole] * 6 + [anywhere] * 2,
        out_specs=[whole] * (2 * SIDE),
        out_shape=[
            jax.ShapeDtypeStruct((BLK, width), half if distance else full)
            for block in (0, 1)
            for distance in range(SIDE)
        ],
        compiler_params=limit,
        cost_estimate=pl.CostEstimate(
            flops=4 * moves, bytes_accessed=16 * moves, transcendentals=0
        ),
    )(place, kept0, from_down0, from_up0, kept1, from_down1, from_up1, *order)
    results = []
    for block in (0, 1):
        mine = sums[SIDE * block : SIDE * block + SIDE]
        arrived = [
            step(mine[d], 0, d) if block == 0 else step(mine[d], d, 0) for d in range(1, SIDE)
        ]
        results.append([mine[0]] + arrived)
    return results


def total(values):
    result = values[0].astype(full)
    for value in values[1:]:
        result = result + value.astype(full)
    return result


def backward_kernel(dy, down, gate, up, order, grad_gate, grad_up, dh):
    del order
    rows = 8
    for chunk in range(2):
        columns = pl.ds(chunk * (down.shape[1] // 2), down.shape[1] // 2)
        value = jnp.dot(dy[...], down[:, columns], preferred_element_type=full)
        for index in range(value.shape[0] // rows):
            to = (index % 2) * BLK + (index // 2) * rows
            dh[pl.ds(to, rows), columns] = value[index * rows : index * rows + rows]
    gate_val = gate[...]
    sigma = jax.nn.sigmoid(gate_val)
    grad_gate[...] = (dh[...] * up[...] * sigma * (1.0 + gate_val * (1.0 - sigma))).astype(half)
    grad_up[...] = (dh[...] * (gate_val * sigma)).astype(half)


def backward(dy, down, gate, up, order):
    whole = pl.BlockSpec(memory_space=pltpu.VMEM)
    shape = jax.ShapeDtypeStruct(gate.shape, half)
    return pl.pallas_call(
        backward_kernel,
        in_specs=[whole] * 4 + [pl.BlockSpec(memory_space=pl.ANY)],
        out_specs=[whole, whole],
        out_shape=[shape, shape],
        scratch_shapes=[pltpu.VMEM(gate.shape, full)],
        compiler_params=pltpu.CompilerParams(vmem_limit_bytes=56 * 1024 * 1024),
        cost_estimate=pl.CostEstimate(
            flops=2 * dy.shape[0] * down.size,
            bytes_accessed=2 * (down.size + dy.size) + 16 * gate.size,
            transcendentals=gate.size,
        ),
    )(dy, down, gate, up, order)


def spread_kernel(piece, order, out, sems):
    del order
    copies = [
        pltpu.make_async_copy(piece, out.at[to], sems.at[to]) for to in range(out.shape[0])
    ]
    for copy in copies:
        copy.start()
    for copy in copies:
        copy.wait()


def spread(piece, count, order):
    whole = pl.BlockSpec(memory_space=pltpu.VMEM)
    return pl.pallas_call(
        spread_kernel,
        in_specs=[whole, pl.BlockSpec(memory_space=pl.ANY)],
        out_specs=pl.BlockSpec(memory_space=pltpu.HBM),
        scratch_shapes=[pltpu.SemaphoreType.DMA((count,))],
        out_shape=jax.ShapeDtypeStruct((count,) + piece.shape, piece.dtype),
        compiler_params=pltpu.CompilerParams(vmem_limit_bytes=16 * 1024 * 1024),
        cost_estimate=pl.CostEstimate(
            flops=0, bytes_accessed=4 * count * piece.size, transcendentals=0
        ),
    )(piece, order)


def home_kernel(terms, state, out):
    value = state[...].astype(full)
    for source in range(terms.shape[0]):
        value = value + terms[source].astype(full)
    rows = state.shape[0]
    out[pl.ds(0, rows), :] = value.astype(half)
    out[pl.ds(rows, rows), :] = jnp.zeros(state.shape, half)


def home(terms, state):
    rows, width = state.shape
    whole = pl.BlockSpec(memory_space=pltpu.VMEM)
    return pl.pallas_call(
        home_kernel,
        in_specs=[whole, whole],
        out_specs=whole,
        out_shape=jax.ShapeDtypeStruct((2 * rows, width), half),
        compiler_params=pltpu.CompilerParams(vmem_limit_bytes=16 * 1024 * 1024),
        cost_estimate=pl.CostEstimate(
            flops=17 * rows * width, bytes_accessed=40 * rows * width, transcendentals=0
        ),
    )(terms, state)


def pool_kernel(place, message, token_slot, order, out, inverse, sh, weights, state, sems):
    del order
    sources, _, cols = message.shape
    rows = BLK // sources
    token_proj = message[0, :BLK].astype(full)
    for source in range(1, sources):
        token_proj = token_proj + message[source, :BLK].astype(full)
    squares = jnp.zeros((rows, cols), full)
    for source in range(sources):
        tail = message[source, BLK:].astype(full)
        sh[pl.ds(source * rows, rows), :] = tail[:rows]
        squares = squares + tail[rows:]
    tokens = token_slot.shape[1]
    squares = jnp.sum(squares, axis=0, keepdims=True)[:, :tokens]
    inverse[...] = lax.rsqrt(squares / place[1].astype(full) + epsilon)
    slots = jnp.where(place[0] == 0, token_slot[:, :BLK], token_slot[:, BLK:])
    scale = jnp.where(place[0] == 0, inverse[:, :BLK], inverse[:, BLK:])
    hits = slots == lax.broadcasted_iota(jnp.int32, (BLK, BLK), 0)
    counts = jnp.maximum(jnp.sum(hits.astype(full), axis=1, keepdims=True), 1.0)
    weights[...] = jnp.where(hits, scale, 0.0)
    first = weights[...].astype(half)
    second = (weights[...] - lax.reduce_precision(weights[...], 8, 7)).astype(half)
    token_proj = token_proj.astype(half)
    placed = jnp.dot(first, token_proj, preferred_element_type=full)
    placed = placed + jnp.dot(second, token_proj, preferred_element_type=full)
    placed = (placed / counts).astype(half).astype(full)
    state[...] = (sh[...] + placed).astype(half)
    copies = [
        pltpu.make_async_copy(state, out.at[to], sems.at[to]) for to in range(sources)
    ]
    for copy in copies:
        copy.start()
    for copy in copies:
        copy.wait()


def pool(message, token_slot, block, width_full, order):
    sources, _, cols = message.shape
    whole = pl.BlockSpec(memory_space=pltpu.VMEM)
    tokens = token_slot.shape[0]
    place = jnp.stack([block, jnp.full_like(block, width_full)]).astype(jnp.int32)
    return pl.pallas_call(
        pool_kernel,
        in_specs=[pl.BlockSpec(memory_space=pltpu.SMEM), whole, whole]
        + [pl.BlockSpec(memory_space=pl.ANY)],
        out_specs=[pl.BlockSpec(memory_space=pltpu.HBM), whole],
        out_shape=[
            jax.ShapeDtypeStruct((sources, BLK, cols), half),
            jax.ShapeDtypeStruct((1, tokens), full),
        ],
        scratch_shapes=[
            pltpu.VMEM((BLK, cols), full),
            pltpu.VMEM((BLK, BLK), full),
            pltpu.VMEM((BLK, cols), half),
            pltpu.SemaphoreType.DMA((sources,)),
        ],
        compiler_params=pltpu.CompilerParams(vmem_limit_bytes=40 * 1024 * 1024),
        cost_estimate=pl.CostEstimate(
            flops=6 * message.size, bytes_accessed=4 * message.size, transcendentals=tokens
        ),
    )(place, message, token_slot[None], order)


def forward_kernel(
    pieces, gain, order, gate_hbm, up_hbm, down_hbm, state, gate, up, out, normed, act, held, sems
):
    del order
    loads = []
    for index, source in enumerate((gate_hbm, up_hbm, down_hbm)):
        part = source.shape[0] // 3
        for third in range(3):
            at = pl.ds(third * part, part)
            load = pltpu.make_async_copy(
                source.at[at], held.at[index, at], sems.at[3 * index + third]
            )
            load.start()
            loads.append(load)
    gate_w, up_w, down_w = held.at[0], held.at[1], held.at[2]
    cols = pieces.shape[2]
    groups = state.shape[1] // cols
    for block in range(state.shape[0] // BLK):
        rows = pl.ds(block * BLK, BLK)
        squares = jnp.zeros((BLK, 128), full)
        for group in range(groups):
            value = pieces[block * groups + group]
            state[rows, pl.ds(group * cols, cols)] = value
            wide = value.astype(full)
            wide = wide * wide
            for lane in range(0, cols, 128):
                squares = squares + wide[:, lane : lane + 128]
        mean = jnp.sum(squares, axis=1, keepdims=True) / state.shape[1]
        inverse = lax.rsqrt(mean + epsilon)
        for group in range(groups):
            at = pl.ds(group * cols, cols)
            wide = pieces[block * groups + group].astype(full)
            normed[rows, at] = (wide * inverse * gain[:, at]).astype(normed.dtype)
    for load in loads[:6]:
        load.wait()
    chunk = gate.shape[1] // 2
    for index in range(2):
        at = pl.ds(index * chunk, chunk)
        gate_val = jnp.dot(normed[...], gate_w[:, at], preferred_element_type=full)
        up_val = jnp.dot(normed[...], up_w[:, at], preferred_element_type=full)
        gate[:, at] = gate_val
        up[:, at] = up_val
        act[:, at] = (gate_val * jax.nn.sigmoid(gate_val) * up_val).astype(half)
    for load in loads[6:]:
        load.wait()
    rows = out.shape[1] // 2
    wide_chunk = 512

    @pl.loop(0, state.shape[1] // wide_chunk)
    def _(index):
        at = pl.ds(pl.multiple_of(index * wide_chunk, wide_chunk), wide_chunk)
        value = times_rows(act[...], down_w[at, :])
        for to in range(out.shape[0]):
            first = value[to * rows : to * rows + rows]
            second = value[BLK + to * rows : BLK + to * rows + rows]
            out[to, :, at] = jnp.concatenate([first, second], axis=0).astype(half)


def forward(pieces, gain, gate_w, up_w, down_w, order):
    width, hidden = gate_w.shape
    n_mp = pieces.shape[0]
    rows = 2 * BLK
    whole = pl.BlockSpec(memory_space=pltpu.VMEM)
    return pl.pallas_call(
        forward_kernel,
        in_specs=[whole, whole, pl.BlockSpec(memory_space=pl.ANY)]
        + [pl.BlockSpec(memory_space=pltpu.HBM)] * 3,
        out_specs=[whole] * 4,
        out_shape=[
            jax.ShapeDtypeStruct((rows, width), half),
            jax.ShapeDtypeStruct((rows, hidden), full),
            jax.ShapeDtypeStruct((rows, hidden), full),
            jax.ShapeDtypeStruct((n_mp, rows // n_mp, width), half),
        ],
        scratch_shapes=[
            pltpu.VMEM((rows, width), half),
            pltpu.VMEM((rows, hidden), half),
            pltpu.VMEM((3, width, hidden), half),
            pltpu.SemaphoreType.DMA((9,)),
        ],
        compiler_params=pltpu.CompilerParams(vmem_limit_bytes=56 * 1024 * 1024),
        cost_estimate=pl.CostEstimate(
            flops=6 * rows * width * hidden,
            bytes_accessed=6 * width * hidden + 10 * rows * width,
            transcendentals=rows * hidden,
        ),
    )(pieces, gain[None], order, gate_w, up_w, down_w)


def slope_kernel(terms, dy, state, gain, order, out):
    del order
    rows, width = dy.shape
    cols = out.shape[2]
    wide = state[...].astype(full)
    inverse = lax.rsqrt(jnp.mean(wide * wide, axis=1, keepdims=True) + epsilon)
    dn = terms[0].astype(full)
    for source in range(1, terms.shape[0]):
        dn = dn + terms[source].astype(full)
    gained = gain[...] * dn
    mean = jnp.mean(gained * wide, axis=1, keepdims=True)
    dx = dy[...].astype(full) + inverse * gained - wide * (inverse * inverse * inverse) * mean
    for group in range(out.shape[0]):
        out[group] = dx[:, group * cols : (group + 1) * cols].astype(out.dtype)


def slope(terms, dy, state, gain, groups, order):
    rows, width = dy.shape
    whole = pl.BlockSpec(memory_space=pltpu.VMEM)
    return pl.pallas_call(
        slope_kernel,
        in_specs=[whole] * 4 + [pl.BlockSpec(memory_space=pl.ANY)],
        out_specs=whole,
        out_shape=jax.ShapeDtypeStruct((groups, rows, width // groups), half),
        compiler_params=pltpu.CompilerParams(vmem_limit_bytes=16 * 1024 * 1024),
        cost_estimate=pl.CostEstimate(
            flops=30 * rows * width, bytes_accessed=40 * rows * width, transcendentals=rows
        ),
    )(terms, dy, state, gain[None], order)


def on_device(
    attention,
    out_proj,
    residual,
    final_gain,
    adapter_weight,
    token_slot,
    block_owner,
    student_hidden,
    cotangent,
    student_gain,
    gate_weight,
    up_weight,
    down_weight,
):
    tokens, width_here = attention.shape
    width_full = out_proj.shape[1]
    student_width = adapter_weight.shape[1]
    blocks = tokens // BLK
    n_mp = lax.axis_size("mp")
    n_dp = lax.axis_size("dp")
    dp = lax.axis_index("dp")
    mp = lax.axis_index("mp")
    slots = student_hidden.shape[2]
    rows = BLK // n_mp
    groups = n_mp // blocks
    cols = student_width // groups
    out_cols = student_width // n_dp
    mine_rows = blocks * rows

    owned = block_owner[None, :] == jnp.arange(n_dp, dtype=jnp.int32)[:, None]
    ranks = jnp.sum(jnp.where(owned, jnp.cumsum(owned.astype(jnp.int32), axis=1) - 1, 0), axis=0)
    place = block_owner * slots + ranks
    my_place = lax.dynamic_slice_in_dim(place, dp * blocks, blocks)

    both = jnp.concatenate([student_hidden[0], cotangent[0]], axis=1)
    everyone = lax.all_gather(both, "dp", axis=0, tiled=False)

    def fetch(offset):
        picked = []
        for k in range(blocks):
            at = (my_place[k] // slots, 0, my_place[k] % slots + offset, 0)
            piece = lax.dynamic_slice(everyone, at, (1, rows, 1, student_width))
            picked.append(piece.reshape(rows, student_width))
        return jnp.stack(picked)

    sh_rows = fetch(0)
    dy_rows = fetch(slots)
    dy = lax.all_gather(dy_rows, "mp", axis=0, tiled=False)

    hidden = residual.astype(full) + jnp.concatenate(
        [total(v) for v in teacher_terms(attention, out_proj, mp, (sh_rows, dy_rows))], axis=0
    )
    squares = jnp.sum(hidden * hidden, axis=1)
    gained_hidden = hidden * final_gain
    parts = jnp.einsum(
        "ktd,dce->kcte",
        gained_hidden.astype(half).reshape(blocks, BLK, width_here),
        adapter_weight.reshape(width_here, groups, cols),
        preferred_element_type=full,
    ).astype(half)
    sh_parts = jnp.swapaxes(sh_rows.reshape(blocks, rows, groups, cols), 1, 2)
    sq_parts = jnp.zeros((8, cols), half).at[:3, :tokens].set(three_parts(squares))
    message = jnp.concatenate(
        [
            parts,
            sh_parts,
            jnp.broadcast_to(sq_parts[None, None], (blocks, groups) + sq_parts.shape),
        ],
        axis=2,
    )
    message = exchange(message.reshape(n_mp, BLK + rows + 8, cols), "mp")
    states, inverse_rms = pool(message, token_slot, mp // groups, width_full, dy[0, 0, :, :128])
    states = exchange(states, "mp")

    slots_block = token_slot.reshape(blocks, BLK)
    onehot = slots_block[:, None, :] == jnp.arange(BLK, dtype=jnp.int32)[None, :, None]
    counts = jnp.maximum(jnp.sum(onehot.astype(full), axis=2), 1.0)
    onehot = onehot.astype(half)
    normed = (gained_hidden * inverse_rms.reshape(tokens, 1)).astype(half).reshape(blocks, BLK, width_here)
    pooled = jnp.einsum("krt,ktd->krd", onehot, normed, preferred_element_type=full)
    pooled = (pooled / counts[:, :, None]).astype(half)
    pooled_all = lax.all_gather(pooled.reshape(n_mp, mine_rows, width_here), "dp", axis=0, tiled=False)
    pooled_all = jnp.swapaxes(pooled_all, 0, 1).reshape(n_dp * tokens, width_here)

    state, gate, up, output = forward(
        states, student_gain, gate_weight, up_weight, down_weight, pooled
    )
    grad_gate, grad_up = backward(dy.reshape(tokens, student_width), down_weight, gate, up, output)
    dn = (times_rows(grad_gate, gate_weight) + times_rows(grad_up, up_weight)).astype(half)
    output = exchange(output, "mp")
    dn, output = lax.optimization_barrier((dn, output))
    dn = exchange(dn.reshape(n_mp, mine_rows, student_width), "mp")
    here = mp * mine_rows
    state_rows = lax.dynamic_slice_in_dim(
        state.reshape(blocks, BLK, student_width), mp * rows, rows, 1
    )
    out_rows = home(output, state_rows.reshape(mine_rows, student_width))
    dproj = slope(
        dn,
        lax.dynamic_slice(
            dy, ((mp % groups) * blocks, mp // groups, 0, 0), (blocks, 1, rows, student_width)
        ).reshape(mine_rows, student_width),
        lax.dynamic_slice_in_dim(state, here, mine_rows, 0),
        student_gain,
        n_dp,
        out_rows,
    )
    dproj = exchange(spread(exchange(dproj, "dp"), n_mp, pooled_all[:16, :128]), "mp")
    adapter_grad = lax.dot_general(
        pooled_all,
        dproj.reshape(n_dp * tokens, out_cols),
        (((0,), (0,)), ((), ())),
        preferred_element_type=full,
    )

    back = lax.all_gather(out_rows, "dp", axis=0, tiled=False)
    mine = block_owner == dp
    picks = []
    for slot in range(slots):
        chosen = mine & (ranks == slot)
        index = jnp.sum(jnp.where(chosen, jnp.arange(chosen.shape[0], dtype=jnp.int32), 0))
        at = (index // blocks, (index % blocks) * rows, 0)
        piece = lax.dynamic_slice(back, at, (1, rows, student_width))[0]
        picks.append(jnp.where(jnp.any(chosen), piece, jnp.zeros((), half)))
    student_out = jnp.stack(picks, axis=1)
    return (student_out[None], adapter_grad)


def solution(mesh):
    return jax.shard_map(
        on_device,
        mesh=mesh,
        in_specs=(
            P("dp", "mp"),
            P("mp", None),
            P("dp", "mp"),
            P("mp"),
            P("mp", None),
            P("dp"),
            P(),
            P("dp", "mp", None, None),
            P("dp", "mp", None, None),
            P(),
            P(None, "mp"),
            P(None, "mp"),
            P(None, "mp"),
        ),
        out_specs=(P("dp", "mp", None, None), P("mp", "dp")),
        check_vma=False,
    )
```

```python
import jax
import jax.numpy as jnp
from jax import lax
from jax.experimental import pallas as pl
from jax.experimental.pallas import tpu as pltpu
from jax.sharding import PartitionSpec as P

BLK = 128
epsilon = 1e-06
half = jnp.bfloat16
full = jnp.float32


def exchange(pieces, axis):
    return lax.all_to_all(pieces, axis, split_axis=0, concat_axis=0, tiled=True)


def three_parts(value):
    first = lax.reduce_precision(value, 8, 7)
    rest = value - first
    second = lax.reduce_precision(rest, 8, 7)
    return jnp.stack([first, second, rest - second]).astype(half)


def times_rows(left, right):
    return lax.dot_general(left, right, (((1,), (1,)), ((), ())), preferred_element_type=full)


SIDE = 4


def step(value, along_y, along_z):
    pairs = []
    for y in range(SIDE):
        for z in range(SIDE):
            to = ((y + along_y) % SIDE) * SIDE + (z + along_z) % SIDE
            pairs.append((y * SIDE + z, to))
    return lax.ppermute(value, "mp", pairs)


def far_kernel(place, left, right, lower0, upper0, lower1, upper1, held, sems):
    width = held.shape[2]
    y, z = lax.rem(place[0] + 2, SIDE), lax.rem(place[1] + 2, SIDE)
    middle = BLK // 2
    loads = []
    for index in range(2 * SIDE):
        piece = y * SIDE + index if index < SIDE else (index - SIDE) * SIDE + z
        columns = pl.ds(pl.multiple_of(piece * width, width), width)
        load = pltpu.make_async_copy(right.at[:, columns], held.at[index], sems.at[index])
        load.start()
        loads.append(load)
    for index in range(2 * SIDE):
        loads[index].wait()
        block, at = index // SIDE, index % SIDE
        value = jnp.dot(
            left[pl.ds(block * BLK, BLK), :], held[index], preferred_element_type=full
        ).astype(half)
        lower, upper = (lower0, upper0) if block == 0 else (lower1, upper1)
        lower[at] = value[:middle]
        upper[at] = value[middle:]


def near_kernel(place, left, right, kept0, up0, down0, kept1, up1, down1, held, sems):
    outs = {0: (kept0, kept1), 1: (up0, up1), 3: (down0, down1)}
    width = held.shape[2]
    y, z = place[0], place[1]

    def load(index):
        piece = lax.rem(y + index // SIDE, SIDE) * SIDE + lax.rem(index, SIDE)
        columns = pl.ds(pl.multiple_of(piece * width, width), width)
        return pltpu.make_async_copy(right.at[:, columns], held.at[index], sems.at[index])

    for index in range(SIDE * SIDE):
        load(index).start()

    @pl.loop(0, SIDE * SIDE)
    def _(index):
        load(index).wait()
        value = jnp.dot(left[...], held[index], preferred_element_type=full).astype(half)
        along_y, at_z = index // SIDE, lax.rem(index, SIDE)
        at_y, along_z = lax.rem(y + along_y, SIDE), lax.rem(at_z - z + SIDE, SIDE)
        for distance, (first, second) in outs.items():

            @pl.when(along_y == distance)
            def _():
                first[at_z] = value[:BLK]

            @pl.when(along_z == distance)
            def _():
                second[at_y] = value[BLK:]


def merge_kernel(*refs):
    ins, outs = refs[:8], refs[8:]
    middle = BLK // 2
    for block in (0, 1):
        up, down, lower, upper = ins[4 * block : 4 * block + 4]
        to_up, to_down = outs[2 * block], outs[2 * block + 1]
        to_up[0, :middle] = (up[0, :middle].astype(full) + lower[0].astype(full)).astype(half)
        to_up[0, middle:] = up[0, middle:]
        to_down[0, :middle] = down[0, :middle]
        to_down[0, middle:] = (down[0, middle:].astype(full) + upper[0].astype(full)).astype(half)


def gather_kernel(place, *refs):
    ins, outs = refs[:6], refs[7:]
    for block in (0, 1):
        kept, from_down, from_up = ins[3 * block : 3 * block + 3]
        here = place[1 - block]
        for distance in range(SIDE):
            at = lax.rem(here + distance, SIDE)
            value = kept[at].astype(full) + from_down[at].astype(full) + from_up[at].astype(full)
            out = outs[SIDE * block + distance]
            out[...] = value.astype(out.dtype)


def teacher_terms(attention, out_proj, mp, order):
    width = attention.shape[1]
    whole = pl.BlockSpec(memory_space=pltpu.VMEM)
    scalars = pl.BlockSpec(memory_space=pltpu.SMEM)
    anywhere = pl.BlockSpec(memory_space=pl.ANY)
    limit = pltpu.CompilerParams(vmem_limit_bytes=40 * 1024 * 1024)
    place = jnp.stack([mp // SIDE, mp % SIDE]).astype(jnp.int32)
    full_piece = jax.ShapeDtypeStruct((SIDE, BLK, width), half)
    half_piece = jax.ShapeDtypeStruct((SIDE, BLK // 2, width), half)
    moves = full_piece.size
    one_piece = pl.BlockSpec((1, BLK, width), lambda i: (i, 0, 0))
    one_half = pl.BlockSpec((1, BLK // 2, width), lambda i: (i, 0, 0))

    def terms(kernel, pieces, count, blocks):
        return pl.pallas_call(
            kernel,
            in_specs=[scalars, whole, pl.BlockSpec(memory_space=pltpu.HBM)],
            out_specs=[whole] * len(pieces),
            out_shape=pieces,
            scratch_shapes=[
                pltpu.VMEM((count, width, width), half),
                pltpu.SemaphoreType.DMA((count,)),
            ],
            compiler_params=pltpu.CompilerParams(vmem_limit_bytes=48 * 1024 * 1024),
            cost_estimate=pl.CostEstimate(
                flops=2 * blocks * BLK * count * width * width,
                bytes_accessed=2 * count * width * width,
                transcendentals=0,
            ),
        )(place, attention, out_proj)

    lower0, upper0, lower1, upper1 = terms(far_kernel, [half_piece] * 4, 2 * SIDE, 1)
    kept0, up0, down0, kept1, up1, down1 = terms(near_kernel, [full_piece] * 6, SIDE * SIDE, 2)
    lower0, upper0 = step(lower0, 1, 0), step(upper0, -1, 0)
    lower1, upper1 = step(lower1, 0, 1), step(upper1, 0, -1)
    up0, down0, up1, down1 = pl.pallas_call(
        merge_kernel,
        grid=(SIDE,),
        in_specs=[one_piece, one_piece, one_half, one_half] * 2,
        out_specs=[one_piece] * 4,
        out_shape=[full_piece] * 4,
        compiler_params=limit,
        cost_estimate=pl.CostEstimate(
            flops=4 * moves, bytes_accessed=20 * moves, transcendentals=0
        ),
    )(up0, down0, lower0, upper0, up1, down1, lower1, upper1)
    from_down0, from_up0 = step(up0, 1, 0), step(down0, -1, 0)
    from_down1, from_up1 = step(up1, 0, 1), step(down1, 0, -1)
    sums = pl.pallas_call(
        gather_kernel,
        in_specs=[scalars] + [whole] * 6 + [anywhere],
        out_specs=[whole] * (2 * SIDE),
        out_shape=[
            jax.ShapeDtypeStruct((BLK, width), half if distance else full)
            for block in (0, 1)
            for distance in range(SIDE)
        ],
        compiler_params=limit,
        cost_estimate=pl.CostEstimate(
            flops=4 * moves, bytes_accessed=16 * moves, transcendentals=0
        ),
    )(place, kept0, from_down0, from_up0, kept1, from_down1, from_up1, *order)
    results = []
    for block in (0, 1):
        mine = sums[SIDE * block : SIDE * block + SIDE]
        arrived = [
            step(mine[d], 0, d) if block == 0 else step(mine[d], d, 0) for d in range(1, SIDE)
        ]
        results.append([mine[0]] + arrived)
    return results


def total(values):
    result = values[0].astype(full)
    for value in values[1:]:
        result = result + value.astype(full)
    return result


def backward_kernel(dy, down, gate, up, order, grad_gate, grad_up, dh):
    del order
    rows = 8
    for chunk in range(2):
        columns = pl.ds(chunk * (down.shape[1] // 2), down.shape[1] // 2)
        value = jnp.dot(dy[...], down[:, columns], preferred_element_type=full)
        for index in range(value.shape[0] // rows):
            to = (index % 2) * BLK + (index // 2) * rows
            dh[pl.ds(to, rows), columns] = value[index * rows : index * rows + rows]
    gate_val = gate[...]
    sigma = jax.nn.sigmoid(gate_val)
    grad_gate[...] = (dh[...] * up[...] * sigma * (1.0 + gate_val * (1.0 - sigma))).astype(half)
    grad_up[...] = (dh[...] * (gate_val * sigma)).astype(half)


def backward(dy, down, gate, up, order):
    whole = pl.BlockSpec(memory_space=pltpu.VMEM)
    shape = jax.ShapeDtypeStruct(gate.shape, half)
    return pl.pallas_call(
        backward_kernel,
        in_specs=[whole] * 4 + [pl.BlockSpec(memory_space=pl.ANY)],
        out_specs=[whole, whole],
        out_shape=[shape, shape],
        scratch_shapes=[pltpu.VMEM(gate.shape, full)],
        compiler_params=pltpu.CompilerParams(vmem_limit_bytes=56 * 1024 * 1024),
        cost_estimate=pl.CostEstimate(
            flops=2 * dy.shape[0] * down.size,
            bytes_accessed=2 * (down.size + dy.size) + 16 * gate.size,
            transcendentals=gate.size,
        ),
    )(dy, down, gate, up, order)


def spread_kernel(piece, out, sems):
    copies = [
        pltpu.make_async_copy(piece, out.at[to], sems.at[to]) for to in range(out.shape[0])
    ]
    for copy in copies:
        copy.start()
    for copy in copies:
        copy.wait()


def spread(piece, count):
    whole = pl.BlockSpec(memory_space=pltpu.VMEM)
    return pl.pallas_call(
        spread_kernel,
        in_specs=[whole],
        out_specs=pl.BlockSpec(memory_space=pltpu.HBM),
        scratch_shapes=[pltpu.SemaphoreType.DMA((count,))],
        out_shape=jax.ShapeDtypeStruct((count,) + piece.shape, piece.dtype),
        compiler_params=pltpu.CompilerParams(vmem_limit_bytes=16 * 1024 * 1024),
        cost_estimate=pl.CostEstimate(
            flops=0, bytes_accessed=4 * count * piece.size, transcendentals=0
        ),
    )(piece)


def home_kernel(terms, state, out):
    value = state[...].astype(full)
    for source in range(terms.shape[0]):
        value = value + terms[source].astype(full)
    rows = state.shape[0]
    out[pl.ds(0, rows), :] = value.astype(half)
    out[pl.ds(rows, rows), :] = jnp.zeros(state.shape, half)


def home(terms, state):
    rows, width = state.shape
    whole = pl.BlockSpec(memory_space=pltpu.VMEM)
    return pl.pallas_call(
        home_kernel,
        in_specs=[whole, whole],
        out_specs=whole,
        out_shape=jax.ShapeDtypeStruct((2 * rows, width), half),
        compiler_params=pltpu.CompilerParams(vmem_limit_bytes=16 * 1024 * 1024),
        cost_estimate=pl.CostEstimate(
            flops=17 * rows * width, bytes_accessed=40 * rows * width, transcendentals=0
        ),
    )(terms, state)


def pool_kernel(place, message, token_slot, out, inverse, sh, weights, state, sems):
    sources, _, cols = message.shape
    rows = BLK // sources
    token_proj = message[0, :BLK].astype(full)
    for source in range(1, sources):
        token_proj = token_proj + message[source, :BLK].astype(full)
    squares = jnp.zeros((rows, cols), full)
    for source in range(sources):
        tail = message[source, BLK:].astype(full)
        sh[pl.ds(source * rows, rows), :] = tail[:rows]
        squares = squares + tail[rows:]
    tokens = token_slot.shape[1]
    squares = jnp.sum(squares, axis=0, keepdims=True)[:, :tokens]
    inverse[...] = lax.rsqrt(squares / place[1].astype(full) + epsilon)
    slots = jnp.where(place[0] == 0, token_slot[:, :BLK], token_slot[:, BLK:])
    scale = jnp.where(place[0] == 0, inverse[:, :BLK], inverse[:, BLK:])
    hits = slots == lax.broadcasted_iota(jnp.int32, (BLK, BLK), 0)
    counts = jnp.maximum(jnp.sum(hits.astype(full), axis=1, keepdims=True), 1.0)
    weights[...] = jnp.where(hits, scale, 0.0)
    first = weights[...].astype(half)
    second = (weights[...] - lax.reduce_precision(weights[...], 8, 7)).astype(half)
    token_proj = token_proj.astype(half)
    placed = jnp.dot(first, token_proj, preferred_element_type=full)
    placed = placed + jnp.dot(second, token_proj, preferred_element_type=full)
    placed = (placed / counts).astype(half).astype(full)
    state[...] = (sh[...] + placed).astype(half)
    copies = [
        pltpu.make_async_copy(state, out.at[to], sems.at[to]) for to in range(sources)
    ]
    for copy in copies:
        copy.start()
    for copy in copies:
        copy.wait()


def pool(message, token_slot, block, width_full):
    sources, _, cols = message.shape
    whole = pl.BlockSpec(memory_space=pltpu.VMEM)
    tokens = token_slot.shape[0]
    place = jnp.stack([block, jnp.full_like(block, width_full)]).astype(jnp.int32)
    return pl.pallas_call(
        pool_kernel,
        in_specs=[pl.BlockSpec(memory_space=pltpu.SMEM), whole, whole],
        out_specs=[pl.BlockSpec(memory_space=pltpu.HBM), whole],
        out_shape=[
            jax.ShapeDtypeStruct((sources, BLK, cols), half),
            jax.ShapeDtypeStruct((1, tokens), full),
        ],
        scratch_shapes=[
            pltpu.VMEM((BLK, cols), full),
            pltpu.VMEM((BLK, BLK), full),
            pltpu.VMEM((BLK, cols), half),
            pltpu.SemaphoreType.DMA((sources,)),
        ],
        compiler_params=pltpu.CompilerParams(vmem_limit_bytes=40 * 1024 * 1024),
        cost_estimate=pl.CostEstimate(
            flops=6 * message.size, bytes_accessed=4 * message.size, transcendentals=tokens
        ),
    )(place, message, token_slot[None])


def forward_kernel(
    pieces, gain, order, gate_hbm, up_hbm, down_hbm, state, gate, up, out, normed, act, held, sems
):
    del order
    parts = 3
    part = gate_hbm.shape[0] // parts

    def load(which, source, third):
        at = pl.ds(third * part, part)
        return pltpu.make_async_copy(
            source.at[at], held.at[which, at], sems.at[parts * which + third]
        )

    for third in range(parts):
        load(0, gate_hbm, third).start()
        load(1, up_hbm, third).start()
    cols = pieces.shape[2]
    groups = state.shape[1] // cols
    for block in range(state.shape[0] // BLK):
        rows = pl.ds(block * BLK, BLK)
        squares = jnp.zeros((BLK, 128), full)
        for group in range(groups):
            value = pieces[block * groups + group]
            state[rows, pl.ds(group * cols, cols)] = value
            wide = value.astype(full)
            wide = wide * wide
            for lane in range(0, cols, 128):
                squares = squares + wide[:, lane : lane + 128]
        mean = jnp.sum(squares, axis=1, keepdims=True) / state.shape[1]
        inverse = lax.rsqrt(mean + epsilon)
        for group in range(groups):
            at = pl.ds(group * cols, cols)
            wide = pieces[block * groups + group].astype(full)
            normed[rows, at] = (wide * inverse * gain[:, at]).astype(normed.dtype)
    half_hidden = gate.shape[1] // 2
    for third in range(parts):
        load(0, gate_hbm, third).wait()
        load(1, up_hbm, third).wait()
        load(2, down_hbm, third).start()
        depth = pl.ds(third * part, part)
        for index in range(2):
            at = pl.ds(index * half_hidden, half_hidden)
            for which, total_ref in ((0, gate), (1, up)):
                value = jnp.dot(
                    normed[:, depth], held[which, depth, at], preferred_element_type=full
                )
                total_ref[:, at] = value if third == 0 else total_ref[:, at] + value
    gate_val = gate[...]
    act[...] = (gate_val * jax.nn.sigmoid(gate_val) * up[...]).astype(half)
    for third in range(parts):
        load(2, down_hbm, third).wait()
    down_w = held.at[2]
    rows = out.shape[1] // 2
    wide_chunk = 512

    @pl.loop(0, state.shape[1] // wide_chunk)
    def _(index):
        at = pl.ds(pl.multiple_of(index * wide_chunk, wide_chunk), wide_chunk)
        value = times_rows(act[...], down_w[at, :])
        for to in range(out.shape[0]):
            first = value[to * rows : to * rows + rows]
            second = value[BLK + to * rows : BLK + to * rows + rows]
            out[to, :, at] = jnp.concatenate([first, second], axis=0).astype(half)


def forward(pieces, gain, gate_w, up_w, down_w, order):
    width, hidden = gate_w.shape
    n_mp = pieces.shape[0]
    rows = 2 * BLK
    whole = pl.BlockSpec(memory_space=pltpu.VMEM)
    return pl.pallas_call(
        forward_kernel,
        in_specs=[whole, whole, pl.BlockSpec(memory_space=pl.ANY)]
        + [pl.BlockSpec(memory_space=pltpu.HBM)] * 3,
        out_specs=[whole] * 4,
        out_shape=[
            jax.ShapeDtypeStruct((rows, width), half),
            jax.ShapeDtypeStruct((rows, hidden), full),
            jax.ShapeDtypeStruct((rows, hidden), full),
            jax.ShapeDtypeStruct((n_mp, rows // n_mp, width), half),
        ],
        scratch_shapes=[
            pltpu.VMEM((rows, width), half),
            pltpu.VMEM((rows, hidden), half),
            pltpu.VMEM((3, width, hidden), half),
            pltpu.SemaphoreType.DMA((9,)),
        ],
        compiler_params=pltpu.CompilerParams(vmem_limit_bytes=56 * 1024 * 1024),
        cost_estimate=pl.CostEstimate(
            flops=6 * rows * width * hidden,
            bytes_accessed=6 * width * hidden + 10 * rows * width,
            transcendentals=rows * hidden,
        ),
    )(pieces, gain[None], order, gate_w, up_w, down_w)


def slope_kernel(terms, dy, state, gain, order, out):
    del order
    rows, width = dy.shape
    cols = out.shape[2]
    wide = state[...].astype(full)
    inverse = lax.rsqrt(jnp.mean(wide * wide, axis=1, keepdims=True) + epsilon)
    dn = terms[0].astype(full)
    for source in range(1, terms.shape[0]):
        dn = dn + terms[source].astype(full)
    gained = gain[...] * dn
    mean = jnp.mean(gained * wide, axis=1, keepdims=True)
    dx = dy[...].astype(full) + inverse * gained - wide * (inverse * inverse * inverse) * mean
    for group in range(out.shape[0]):
        out[group] = dx[:, group * cols : (group + 1) * cols].astype(out.dtype)


def slope(terms, dy, state, gain, groups, order):
    rows, width = dy.shape
    whole = pl.BlockSpec(memory_space=pltpu.VMEM)
    return pl.pallas_call(
        slope_kernel,
        in_specs=[whole] * 4 + [pl.BlockSpec(memory_space=pl.ANY)],
        out_specs=whole,
        out_shape=jax.ShapeDtypeStruct((groups, rows, width // groups), half),
        compiler_params=pltpu.CompilerParams(vmem_limit_bytes=16 * 1024 * 1024),
        cost_estimate=pl.CostEstimate(
            flops=30 * rows * width, bytes_accessed=40 * rows * width, transcendentals=rows
        ),
    )(terms, dy, state, gain[None], order)


def on_device(
    attention,
    out_proj,
    residual,
    final_gain,
    adapter_weight,
    token_slot,
    block_owner,
    student_hidden,
    cotangent,
    student_gain,
    gate_weight,
    up_weight,
    down_weight,
):
    tokens, width_here = attention.shape
    width_full = out_proj.shape[1]
    student_width = adapter_weight.shape[1]
    blocks = tokens // BLK
    n_mp = lax.axis_size("mp")
    n_dp = lax.axis_size("dp")
    dp = lax.axis_index("dp")
    mp = lax.axis_index("mp")
    slots = student_hidden.shape[2]
    rows = BLK // n_mp
    groups = n_mp // blocks
    cols = student_width // groups
    out_cols = student_width // n_dp
    mine_rows = blocks * rows

    ids = jnp.arange(block_owner.shape[0], dtype=jnp.int32)
    my_ids = dp * blocks + jnp.arange(blocks, dtype=jnp.int32)
    my_owner = lax.dynamic_slice_in_dim(block_owner, dp * blocks, blocks)
    my_slot = jnp.sum(
        (block_owner[None, :] == my_owner[:, None]) & (ids[None, :] < my_ids[:, None]),
        axis=1,
        dtype=jnp.int32,
    )

    def fetch(array):
        everyone = lax.all_gather(array[0], "dp", axis=0, tiled=False)
        picked = []
        for k in range(blocks):
            at = (my_owner[k], 0, my_slot[k], 0)
            piece = lax.dynamic_slice(everyone, at, (1, rows, 1, student_width))
            picked.append(piece.reshape(rows, student_width))
        return jnp.stack(picked)

    sh_rows = fetch(student_hidden)
    dy_rows = fetch(cotangent)
    dy = lax.all_gather(dy_rows, "mp", axis=0, tiled=False)

    hidden = residual.astype(full) + jnp.concatenate(
        [total(v) for v in teacher_terms(attention, out_proj, mp, (sh_rows,))], axis=0
    )
    squares = jnp.sum(hidden * hidden, axis=1)
    gained_hidden = hidden * final_gain
    parts = jnp.einsum(
        "ktd,dce->kcte",
        gained_hidden.astype(half).reshape(blocks, BLK, width_here),
        adapter_weight.reshape(width_here, groups, cols),
        preferred_element_type=full,
    ).astype(half)
    sh_parts = jnp.swapaxes(sh_rows.reshape(blocks, rows, groups, cols), 1, 2)
    sq_parts = jnp.zeros((8, cols), half).at[:3, :tokens].set(three_parts(squares))
    message = jnp.concatenate(
        [
            parts,
            sh_parts,
            jnp.broadcast_to(sq_parts[None, None], (blocks, groups) + sq_parts.shape),
        ],
        axis=2,
    )
    message = exchange(message.reshape(n_mp, BLK + rows + 8, cols), "mp")
    states, inverse_rms = pool(message, token_slot, mp // groups, width_full)
    states = exchange(states, "mp")

    slots_block = token_slot.reshape(blocks, BLK)
    onehot = slots_block[:, None, :] == jnp.arange(BLK, dtype=jnp.int32)[None, :, None]
    counts = jnp.maximum(jnp.sum(onehot.astype(full), axis=2), 1.0)
    onehot = onehot.astype(half)
    normed = (gained_hidden * inverse_rms.reshape(tokens, 1)).astype(half).reshape(blocks, BLK, width_here)
    pooled = jnp.einsum("krt,ktd->krd", onehot, normed, preferred_element_type=full)
    pooled = (pooled / counts[:, :, None]).astype(half)
    pooled_all = lax.all_gather(pooled.reshape(n_mp, mine_rows, width_here), "dp", axis=0, tiled=False)
    pooled_all = jnp.swapaxes(pooled_all, 0, 1).reshape(n_dp * tokens, width_here)

    state, gate, up, output = forward(
        states, student_gain, gate_weight, up_weight, down_weight, pooled
    )
    grad_gate, grad_up = backward(dy.reshape(tokens, student_width), down_weight, gate, up, output)
    dn = (times_rows(grad_gate, gate_weight) + times_rows(grad_up, up_weight)).astype(half)
    output = exchange(output, "mp")
    dn, output = lax.optimization_barrier((dn, output))
    dn = exchange(dn.reshape(n_mp, mine_rows, student_width), "mp")
    here = mp * mine_rows
    state_rows = lax.dynamic_slice_in_dim(
        state.reshape(blocks, BLK, student_width), mp * rows, rows, 1
    )
    out_rows = home(output, state_rows.reshape(mine_rows, student_width))
    dproj = slope(
        dn,
        lax.dynamic_slice(
            dy, ((mp % groups) * blocks, mp // groups, 0, 0), (blocks, 1, rows, student_width)
        ).reshape(mine_rows, student_width),
        lax.dynamic_slice_in_dim(state, here, mine_rows, 0),
        student_gain,
        n_dp,
        out_rows,
    )
    dproj = exchange(spread(exchange(dproj, "dp"), n_mp), "mp")
    adapter_grad = lax.dot_general(
        pooled_all,
        dproj.reshape(n_dp * tokens, out_cols),
        (((0,), (0,)), ((), ())),
        preferred_element_type=full,
    )

    back = lax.all_gather(out_rows, "dp", axis=0, tiled=False)
    before = (block_owner[None, :] == block_owner[:, None]) & (ids[None, :] < ids[:, None])
    ranks = jnp.sum(before, axis=1, dtype=jnp.int32)
    mine = block_owner == dp
    picks = []
    for slot in range(slots):
        chosen = mine & (ranks == slot)
        index = jnp.sum(jnp.where(chosen, ids, 0))
        at = (index // blocks, (index % blocks) * rows, 0)
        piece = lax.dynamic_slice(back, at, (1, rows, student_width))[0]
        picks.append(jnp.where(jnp.any(chosen), piece, jnp.zeros((), half)))
    student_out = jnp.stack(picks, axis=1)
    return (student_out[None], adapter_grad)


def solution(mesh):
    return jax.shard_map(
        on_device,
        mesh=mesh,
        in_specs=(
            P("dp", "mp"),
            P("mp", None),
            P("dp", "mp"),
            P("mp"),
            P("mp", None),
            P("dp"),
            P(),
            P("dp", "mp", None, None),
            P("dp", "mp", None, None),
            P(),
            P(None, "mp"),
            P(None, "mp"),
            P(None, "mp"),
        ),
        out_specs=(P("dp", "mp", None, None), P("mp", "dp")),
        check_vma=False,
    )
```

```python
import jax
import jax.numpy as jnp
from jax import lax
from jax.experimental import pallas as pl
from jax.experimental.pallas import tpu as pltpu
from jax.sharding import PartitionSpec as P

BLK = 128
epsilon = 1e-06
half = jnp.bfloat16
full = jnp.float32


def exchange(pieces, axis):
    return lax.all_to_all(pieces, axis, split_axis=0, concat_axis=0, tiled=True)


def take(array, starts, sizes):
    return lax.dynamic_slice(array, starts, sizes, allow_negative_indices=False)


def three_parts(value):
    first = lax.reduce_precision(value, 8, 7)
    rest = value - first
    second = lax.reduce_precision(rest, 8, 7)
    return jnp.stack([first, second, rest - second]).astype(half)


def times_rows(left, right):
    return lax.dot_general(left, right, (((1,), (1,)), ((), ())), preferred_element_type=full)


SIDE = 4


def step(value, along_y, along_z):
    pairs = []
    for y in range(SIDE):
        for z in range(SIDE):
            to = ((y + along_y) % SIDE) * SIDE + (z + along_z) % SIDE
            pairs.append((y * SIDE + z, to))
    return lax.ppermute(value, "mp", pairs)


def far_kernel(place, left, right, lower0, upper0, lower1, upper1, held, sems):
    width = held.shape[2]
    y, z = lax.rem(place[0] + 2, SIDE), lax.rem(place[1] + 2, SIDE)
    middle = BLK // 2
    loads = []
    for index in range(2 * SIDE):
        piece = y * SIDE + index if index < SIDE else (index - SIDE) * SIDE + z
        columns = pl.ds(pl.multiple_of(piece * width, width), width)
        load = pltpu.make_async_copy(right.at[:, columns], held.at[index], sems.at[index])
        load.start()
        loads.append(load)
    for index in range(2 * SIDE):
        loads[index].wait()
        block, at = index // SIDE, index % SIDE
        value = jnp.dot(
            left[pl.ds(block * BLK, BLK), :], held[index], preferred_element_type=full
        ).astype(half)
        lower, upper = (lower0, upper0) if block == 0 else (lower1, upper1)
        lower[at] = value[:middle]
        upper[at] = value[middle:]


def near_kernel(place, left, right, kept0, up0, down0, kept1, up1, down1, held, sems):
    outs = {0: (kept0, kept1), 1: (up0, up1), 3: (down0, down1)}
    width = held.shape[2]
    y, z = place[0], place[1]

    def load(index):
        piece = lax.rem(y + index // SIDE, SIDE) * SIDE + lax.rem(index, SIDE)
        columns = pl.ds(pl.multiple_of(piece * width, width), width)
        return pltpu.make_async_copy(right.at[:, columns], held.at[index], sems.at[index])

    for index in range(SIDE * SIDE):
        load(index).start()

    @pl.loop(0, SIDE * SIDE)
    def _(index):
        load(index).wait()
        value = jnp.dot(left[...], held[index], preferred_element_type=full).astype(half)
        along_y, at_z = index // SIDE, lax.rem(index, SIDE)
        at_y, along_z = lax.rem(y + along_y, SIDE), lax.rem(at_z - z + SIDE, SIDE)
        for distance, (first, second) in outs.items():

            @pl.when(along_y == distance)
            def _():
                first[at_z] = value[:BLK]

            @pl.when(along_z == distance)
            def _():
                second[at_y] = value[BLK:]


def merge_kernel(*refs):
    ins, outs = refs[:8], refs[8:]
    middle = BLK // 2
    for block in (0, 1):
        up, down, lower, upper = ins[4 * block : 4 * block + 4]
        to_up, to_down = outs[2 * block], outs[2 * block + 1]
        to_up[0, :middle] = (up[0, :middle].astype(full) + lower[0].astype(full)).astype(half)
        to_up[0, middle:] = up[0, middle:]
        to_down[0, :middle] = down[0, :middle]
        to_down[0, middle:] = (down[0, middle:].astype(full) + upper[0].astype(full)).astype(half)


def gather_kernel(place, *refs):
    ins, outs = refs[:6], refs[7:]
    for block in (0, 1):
        kept, from_down, from_up = ins[3 * block : 3 * block + 3]
        here = place[1 - block]
        for distance in range(SIDE):
            at = lax.rem(here + distance, SIDE)
            value = kept[at].astype(full) + from_down[at].astype(full) + from_up[at].astype(full)
            out = outs[SIDE * block + distance]
            out[...] = value.astype(out.dtype)


def teacher_terms(attention, out_proj, mp, order):
    width = attention.shape[1]
    whole = pl.BlockSpec(memory_space=pltpu.VMEM)
    scalars = pl.BlockSpec(memory_space=pltpu.SMEM)
    anywhere = pl.BlockSpec(memory_space=pl.ANY)
    limit = pltpu.CompilerParams(vmem_limit_bytes=40 * 1024 * 1024)
    place = jnp.stack([mp // SIDE, mp % SIDE]).astype(jnp.int32)
    full_piece = jax.ShapeDtypeStruct((SIDE, BLK, width), half)
    half_piece = jax.ShapeDtypeStruct((SIDE, BLK // 2, width), half)
    moves = full_piece.size
    one_piece = pl.BlockSpec((1, BLK, width), lambda i: (i, 0, 0))
    one_half = pl.BlockSpec((1, BLK // 2, width), lambda i: (i, 0, 0))

    def terms(kernel, pieces, count, blocks):
        return pl.pallas_call(
            kernel,
            in_specs=[scalars, whole, pl.BlockSpec(memory_space=pltpu.HBM)],
            out_specs=[whole] * len(pieces),
            out_shape=pieces,
            scratch_shapes=[
                pltpu.VMEM((count, width, width), half),
                pltpu.SemaphoreType.DMA((count,)),
            ],
            compiler_params=pltpu.CompilerParams(vmem_limit_bytes=48 * 1024 * 1024),
            cost_estimate=pl.CostEstimate(
                flops=2 * blocks * BLK * count * width * width,
                bytes_accessed=2 * count * width * width,
                transcendentals=0,
            ),
        )(place, attention, out_proj)

    lower0, upper0, lower1, upper1 = terms(far_kernel, [half_piece] * 4, 2 * SIDE, 1)
    kept0, up0, down0, kept1, up1, down1 = terms(near_kernel, [full_piece] * 6, SIDE * SIDE, 2)
    lower0, upper0 = step(lower0, 1, 0), step(upper0, -1, 0)
    lower1, upper1 = step(lower1, 0, 1), step(upper1, 0, -1)
    up0, down0, up1, down1 = pl.pallas_call(
        merge_kernel,
        grid=(SIDE,),
        in_specs=[one_piece, one_piece, one_half, one_half] * 2,
        out_specs=[one_piece] * 4,
        out_shape=[full_piece] * 4,
        compiler_params=limit,
        cost_estimate=pl.CostEstimate(
            flops=4 * moves, bytes_accessed=20 * moves, transcendentals=0
        ),
    )(up0, down0, lower0, upper0, up1, down1, lower1, upper1)
    from_down0, from_up0 = step(up0, 1, 0), step(down0, -1, 0)
    from_down1, from_up1 = step(up1, 0, 1), step(down1, 0, -1)
    sums = pl.pallas_call(
        gather_kernel,
        in_specs=[scalars] + [whole] * 6 + [anywhere],
        out_specs=[whole] * (2 * SIDE),
        out_shape=[
            jax.ShapeDtypeStruct((BLK, width), half if distance else full)
            for block in (0, 1)
            for distance in range(SIDE)
        ],
        compiler_params=limit,
        cost_estimate=pl.CostEstimate(
            flops=4 * moves, bytes_accessed=16 * moves, transcendentals=0
        ),
    )(place, kept0, from_down0, from_up0, kept1, from_down1, from_up1, *order)
    results = []
    for block in (0, 1):
        mine = sums[SIDE * block : SIDE * block + SIDE]
        arrived = [
            step(mine[d], 0, d) if block == 0 else step(mine[d], d, 0) for d in range(1, SIDE)
        ]
        results.append([mine[0]] + arrived)
    return results


def total(values):
    result = values[0].astype(full)
    for value in values[1:]:
        result = result + value.astype(full)
    return result


def backward_kernel(dy, down, gate, up, order, grad_gate, grad_up, dh):
    del order
    rows = 8
    for chunk in range(2):
        columns = pl.ds(chunk * (down.shape[1] // 2), down.shape[1] // 2)
        value = jnp.dot(dy[...], down[:, columns], preferred_element_type=full)
        for index in range(value.shape[0] // rows):
            to = (index % 2) * BLK + (index // 2) * rows
            dh[pl.ds(to, rows), columns] = value[index * rows : index * rows + rows]
    gate_val = gate[...]
    sigma = jax.nn.sigmoid(gate_val)
    grad_gate[...] = (dh[...] * up[...] * sigma * (1.0 + gate_val * (1.0 - sigma))).astype(half)
    grad_up[...] = (dh[...] * (gate_val * sigma)).astype(half)


def backward(dy, down, gate, up, order):
    whole = pl.BlockSpec(memory_space=pltpu.VMEM)
    shape = jax.ShapeDtypeStruct(gate.shape, half)
    return pl.pallas_call(
        backward_kernel,
        in_specs=[whole] * 4 + [pl.BlockSpec(memory_space=pl.ANY)],
        out_specs=[whole, whole],
        out_shape=[shape, shape],
        scratch_shapes=[pltpu.VMEM(gate.shape, full)],
        compiler_params=pltpu.CompilerParams(vmem_limit_bytes=56 * 1024 * 1024),
        cost_estimate=pl.CostEstimate(
            flops=2 * dy.shape[0] * down.size,
            bytes_accessed=2 * (down.size + dy.size) + 16 * gate.size,
            transcendentals=gate.size,
        ),
    )(dy, down, gate, up, order)


def spread_kernel(piece, out, sems):
    copies = [
        pltpu.make_async_copy(piece, out.at[to], sems.at[to]) for to in range(out.shape[0])
    ]
    for copy in copies:
        copy.start()
    for copy in copies:
        copy.wait()


def spread(piece, count):
    whole = pl.BlockSpec(memory_space=pltpu.VMEM)
    return pl.pallas_call(
        spread_kernel,
        in_specs=[whole],
        out_specs=pl.BlockSpec(memory_space=pltpu.HBM),
        scratch_shapes=[pltpu.SemaphoreType.DMA((count,))],
        out_shape=jax.ShapeDtypeStruct((count,) + piece.shape, piece.dtype),
        compiler_params=pltpu.CompilerParams(vmem_limit_bytes=16 * 1024 * 1024),
        cost_estimate=pl.CostEstimate(
            flops=0, bytes_accessed=4 * count * piece.size, transcendentals=0
        ),
    )(piece)


def home_kernel(terms, state, out):
    value = state[...].astype(full)
    for source in range(terms.shape[0]):
        value = value + terms[source].astype(full)
    rows = state.shape[0]
    out[pl.ds(0, rows), :] = value.astype(half)
    out[pl.ds(rows, rows), :] = jnp.zeros(state.shape, half)


def home(terms, state):
    rows, width = state.shape
    whole = pl.BlockSpec(memory_space=pltpu.VMEM)
    return pl.pallas_call(
        home_kernel,
        in_specs=[whole, whole],
        out_specs=whole,
        out_shape=jax.ShapeDtypeStruct((2 * rows, width), half),
        compiler_params=pltpu.CompilerParams(vmem_limit_bytes=16 * 1024 * 1024),
        cost_estimate=pl.CostEstimate(
            flops=17 * rows * width, bytes_accessed=40 * rows * width, transcendentals=0
        ),
    )(terms, state)


def pool_kernel(place, message, token_slot, out, inverse, sh, weights, state, sems):
    sources, _, cols = message.shape
    rows = BLK // sources
    token_proj = message[0, :BLK].astype(full)
    for source in range(1, sources):
        token_proj = token_proj + message[source, :BLK].astype(full)
    squares = jnp.zeros((rows, cols), full)
    for source in range(sources):
        tail = message[source, BLK:].astype(full)
        sh[pl.ds(source * rows, rows), :] = tail[:rows]
        squares = squares + tail[rows:]
    tokens = token_slot.shape[1]
    squares = jnp.sum(squares, axis=0, keepdims=True)[:, :tokens]
    inverse[...] = lax.rsqrt(squares / place[1].astype(full) + epsilon)
    slots = jnp.where(place[0] == 0, token_slot[:, :BLK], token_slot[:, BLK:])
    scale = jnp.where(place[0] == 0, inverse[:, :BLK], inverse[:, BLK:])
    hits = slots == lax.broadcasted_iota(jnp.int32, (BLK, BLK), 0)
    counts = jnp.maximum(jnp.sum(hits.astype(full), axis=1, keepdims=True), 1.0)
    weights[...] = jnp.where(hits, scale, 0.0)
    first = weights[...].astype(half)
    second = (weights[...] - lax.reduce_precision(weights[...], 8, 7)).astype(half)
    token_proj = token_proj.astype(half)
    placed = jnp.dot(first, token_proj, preferred_element_type=full)
    placed = placed + jnp.dot(second, token_proj, preferred_element_type=full)
    placed = (placed / counts).astype(half).astype(full)
    state[...] = (sh[...] + placed).astype(half)
    copies = [
        pltpu.make_async_copy(state, out.at[to], sems.at[to]) for to in range(sources)
    ]
    for copy in copies:
        copy.start()
    for copy in copies:
        copy.wait()


def pool(message, token_slot, block, width_full):
    sources, _, cols = message.shape
    whole = pl.BlockSpec(memory_space=pltpu.VMEM)
    tokens = token_slot.shape[0]
    place = jnp.stack([block, jnp.full_like(block, width_full)]).astype(jnp.int32)
    return pl.pallas_call(
        pool_kernel,
        in_specs=[pl.BlockSpec(memory_space=pltpu.SMEM), whole, whole],
        out_specs=[pl.BlockSpec(memory_space=pltpu.HBM), whole],
        out_shape=[
            jax.ShapeDtypeStruct((sources, BLK, cols), half),
            jax.ShapeDtypeStruct((1, tokens), full),
        ],
        scratch_shapes=[
            pltpu.VMEM((BLK, cols), full),
            pltpu.VMEM((BLK, BLK), full),
            pltpu.VMEM((BLK, cols), half),
            pltpu.SemaphoreType.DMA((sources,)),
        ],
        compiler_params=pltpu.CompilerParams(vmem_limit_bytes=40 * 1024 * 1024),
        cost_estimate=pl.CostEstimate(
            flops=6 * message.size, bytes_accessed=4 * message.size, transcendentals=tokens
        ),
    )(place, message, token_slot[None])


def forward_kernel(
    place, pieces, gain, order, gate_hbm, up_hbm, down_hbm,
    home_state, here_state, gate, up, out_hbm, normed, act, held, out, sems, out_sems,
):
    del order
    parts = 3
    part = gate_hbm.shape[0] // parts

    def load(which, source, third):
        at = pl.ds(third * part, part)
        return pltpu.make_async_copy(
            source.at[at], held.at[which, at], sems.at[parts * which + third]
        )

    for third in range(parts):
        load(0, gate_hbm, third).start()
        load(1, up_hbm, third).start()
    cols = pieces.shape[2]
    width = normed.shape[1]
    groups = width // cols
    mine = here_state.shape[0]
    mp = place[0]
    rows = pl.multiple_of(lax.rem(mp, groups) * mine, mine)
    pair = pl.multiple_of((mp // 2) * mine, mine)
    for group in range(groups):
        at = pl.ds(group * cols, cols)
        here_state[:, at] = pieces[(mp // groups) * groups + group, pl.ds(rows, mine), :]
        halves = []
        for block in range(2):
            two = pieces[block * groups + group, pl.ds(pair, mine), :].astype(full)
            halves.append(jnp.where(lax.rem(mp, 2) == 0, two[: mine // 2], two[mine // 2 :]))
        home_state[:, at] = jnp.concatenate(halves, axis=0).astype(half)
    for block in range(normed.shape[0] // BLK):
        rows = pl.ds(block * BLK, BLK)
        squares = jnp.zeros((BLK, 128), full)
        for group in range(groups):
            wide = pieces[block * groups + group].astype(full)
            wide = wide * wide
            for lane in range(0, cols, 128):
                squares = squares + wide[:, lane : lane + 128]
        mean = jnp.sum(squares, axis=1, keepdims=True) / width
        inverse = lax.rsqrt(mean + epsilon)
        for group in range(groups):
            at = pl.ds(group * cols, cols)
            wide = pieces[block * groups + group].astype(full)
            normed[rows, at] = (wide * inverse * gain[:, at]).astype(normed.dtype)
    half_hidden = gate.shape[1] // 2
    for third in range(parts):
        load(0, gate_hbm, third).wait()
        load(1, up_hbm, third).wait()
        load(2, down_hbm, third).start()
        depth = pl.ds(third * part, part)
        for index in range(2):
            at = pl.ds(index * half_hidden, half_hidden)
            for which, total_ref in ((0, gate), (1, up)):
                value = jnp.dot(
                    normed[:, depth], held[which, depth, at], preferred_element_type=full
                )
                total_ref[:, at] = value if third == 0 else total_ref[:, at] + value
    gate_val = gate[...]
    act[...] = (gate_val * jax.nn.sigmoid(gate_val) * up[...]).astype(half)
    for third in range(parts):
        load(2, down_hbm, third).wait()
    down_w = held.at[2]
    rows = out.shape[1] // 2
    wide_chunk = 512

    def leave(index):
        at = pl.ds(pl.multiple_of(index * wide_chunk, wide_chunk), wide_chunk)
        return pltpu.make_async_copy(out.at[:, :, at], out_hbm.at[:, :, at], out_sems.at[index])

    @pl.loop(0, width // wide_chunk)
    def _(index):
        at = pl.ds(pl.multiple_of(index * wide_chunk, wide_chunk), wide_chunk)
        value = times_rows(act[...], down_w[at, :])
        for to in range(out.shape[0]):
            first = value[to * rows : to * rows + rows]
            second = value[BLK + to * rows : BLK + to * rows + rows]
            out[to, :, at] = jnp.concatenate([first, second], axis=0).astype(half)
        leave(index).start()

    for index in range(width // wide_chunk):
        leave(index).wait()


def forward(pieces, gain, gate_w, up_w, down_w, mp, order):
    width, hidden = gate_w.shape
    n_mp = pieces.shape[0]
    rows = 2 * BLK
    mine = rows // n_mp
    whole = pl.BlockSpec(memory_space=pltpu.VMEM)
    far = pl.BlockSpec(memory_space=pltpu.HBM)
    return pl.pallas_call(
        forward_kernel,
        in_specs=[pl.BlockSpec(memory_space=pltpu.SMEM), whole, whole]
        + [pl.BlockSpec(memory_space=pl.ANY), far, far, far],
        out_specs=[whole] * 4 + [far],
        out_shape=[
            jax.ShapeDtypeStruct((mine, width), half),
            jax.ShapeDtypeStruct((mine, width), half),
            jax.ShapeDtypeStruct((rows, hidden), full),
            jax.ShapeDtypeStruct((rows, hidden), full),
            jax.ShapeDtypeStruct((n_mp, mine, width), half),
        ],
        scratch_shapes=[
            pltpu.VMEM((rows, width), half),
            pltpu.VMEM((rows, hidden), half),
            pltpu.VMEM((3, width, hidden), half),
            pltpu.VMEM((n_mp, mine, width), half),
            pltpu.SemaphoreType.DMA((9,)),
            pltpu.SemaphoreType.DMA((width // 512,)),
        ],
        compiler_params=pltpu.CompilerParams(vmem_limit_bytes=56 * 1024 * 1024),
        cost_estimate=pl.CostEstimate(
            flops=6 * rows * width * hidden,
            bytes_accessed=6 * width * hidden + 10 * rows * width,
            transcendentals=rows * hidden,
        ),
    )(mp[None].astype(jnp.int32), pieces, gain[None], order, gate_w, up_w, down_w)


def slope_kernel(terms, dy, state, gain, order, out):
    del order
    rows, width = dy.shape
    cols = out.shape[2]
    wide = state[...].astype(full)
    inverse = lax.rsqrt(jnp.mean(wide * wide, axis=1, keepdims=True) + epsilon)
    dn = terms[0].astype(full)
    for source in range(1, terms.shape[0]):
        dn = dn + terms[source].astype(full)
    gained = gain[...] * dn
    mean = jnp.mean(gained * wide, axis=1, keepdims=True)
    dx = dy[...].astype(full) + inverse * gained - wide * (inverse * inverse * inverse) * mean
    for group in range(out.shape[0]):
        out[group] = dx[:, group * cols : (group + 1) * cols].astype(out.dtype)


def slope(terms, dy, state, gain, groups, order):
    rows, width = dy.shape
    whole = pl.BlockSpec(memory_space=pltpu.VMEM)
    return pl.pallas_call(
        slope_kernel,
        in_specs=[whole] * 4 + [pl.BlockSpec(memory_space=pl.ANY)],
        out_specs=whole,
        out_shape=jax.ShapeDtypeStruct((groups, rows, width // groups), half),
        compiler_params=pltpu.CompilerParams(vmem_limit_bytes=16 * 1024 * 1024),
        cost_estimate=pl.CostEstimate(
            flops=30 * rows * width, bytes_accessed=40 * rows * width, transcendentals=rows
        ),
    )(terms, dy, state, gain[None], order)


def on_device(
    attention,
    out_proj,
    residual,
    final_gain,
    adapter_weight,
    token_slot,
    block_owner,
    student_hidden,
    cotangent,
    student_gain,
    gate_weight,
    up_weight,
    down_weight,
):
    tokens, width_here = attention.shape
    width_full = out_proj.shape[1]
    student_width = adapter_weight.shape[1]
    blocks = tokens // BLK
    n_mp = lax.axis_size("mp")
    n_dp = lax.axis_size("dp")
    dp = lax.axis_index("dp")
    mp = lax.axis_index("mp")
    slots = student_hidden.shape[2]
    rows = BLK // n_mp
    groups = n_mp // blocks
    cols = student_width // groups
    out_cols = student_width // n_dp
    mine_rows = blocks * rows

    ids = jnp.arange(block_owner.shape[0], dtype=jnp.int32)
    my_ids = dp * blocks + jnp.arange(blocks, dtype=jnp.int32)
    my_owner = take(block_owner, (dp * blocks,), (blocks,))
    my_slot = jnp.sum(
        (block_owner[None, :] == my_owner[:, None]) & (ids[None, :] < my_ids[:, None]),
        axis=1,
        dtype=jnp.int32,
    )

    def fetch(array):
        everyone = lax.all_gather(array[0], "dp", axis=0, tiled=False)
        picked = []
        for k in range(blocks):
            at = (my_owner[k], 0, my_slot[k], 0)
            piece = take(everyone, at, (1, rows, 1, student_width))
            picked.append(piece.reshape(rows, student_width))
        return jnp.stack(picked)

    sh_rows = fetch(student_hidden)
    dy_rows = fetch(cotangent)
    dy = lax.all_gather(dy_rows, "mp", axis=0, tiled=False)

    hidden = residual.astype(full) + jnp.concatenate(
        [total(v) for v in teacher_terms(attention, out_proj, mp, (sh_rows,))], axis=0
    )
    squares = jnp.sum(hidden * hidden, axis=1)
    gained_hidden = hidden * final_gain
    parts = jnp.einsum(
        "ktd,dce->kcte",
        gained_hidden.astype(half).reshape(blocks, BLK, width_here),
        adapter_weight.reshape(width_here, groups, cols),
        preferred_element_type=full,
    ).astype(half)
    sh_parts = jnp.swapaxes(sh_rows.reshape(blocks, rows, groups, cols), 1, 2)
    sq_parts = jnp.zeros((8, cols), half).at[:3, :tokens].set(three_parts(squares))
    message = jnp.concatenate(
        [
            parts,
            sh_parts,
            jnp.broadcast_to(sq_parts[None, None], (blocks, groups) + sq_parts.shape),
        ],
        axis=2,
    )
    message = exchange(message.reshape(n_mp, BLK + rows + 8, cols), "mp")
    states, inverse_rms = pool(message, token_slot, mp // groups, width_full)
    states = exchange(states, "mp")

    slots_block = token_slot.reshape(blocks, BLK)
    onehot = slots_block[:, None, :] == jnp.arange(BLK, dtype=jnp.int32)[None, :, None]
    counts = jnp.maximum(jnp.sum(onehot.astype(full), axis=2), 1.0)
    onehot = onehot.astype(half)
    normed = (gained_hidden * inverse_rms.reshape(tokens, 1)).astype(half).reshape(blocks, BLK, width_here)
    pooled = jnp.einsum("krt,ktd->krd", onehot, normed, preferred_element_type=full)
    pooled = (pooled / counts[:, :, None]).astype(half)
    pooled_all = lax.all_gather(pooled.reshape(n_mp, mine_rows, width_here), "dp", axis=0, tiled=False)
    pooled_all = jnp.swapaxes(pooled_all, 0, 1).reshape(n_dp * tokens, width_here)

    home_state, here_state, gate, up, output = forward(
        states, student_gain, gate_weight, up_weight, down_weight, mp, pooled
    )
    grad_gate, grad_up = backward(dy.reshape(tokens, student_width), down_weight, gate, up, output)
    dn = (times_rows(grad_gate, gate_weight) + times_rows(grad_up, up_weight)).astype(half)
    output = exchange(output, "mp")
    dn, output = lax.optimization_barrier((dn, output))
    dn = exchange(dn.reshape(n_mp, mine_rows, student_width), "mp")
    out_rows = home(output, home_state)
    dproj = slope(
        dn,
        take(
            dy, ((mp % groups) * blocks, mp // groups, 0, 0), (blocks, 1, rows, student_width)
        ).reshape(mine_rows, student_width),
        here_state,
        student_gain,
        n_dp,
        out_rows,
    )
    dproj = exchange(spread(exchange(dproj, "dp"), n_mp), "mp")
    adapter_grad = lax.dot_general(
        pooled_all,
        dproj.reshape(n_dp * tokens, out_cols),
        (((0,), (0,)), ((), ())),
        preferred_element_type=full,
    )

    back = lax.all_gather(out_rows, "dp", axis=0, tiled=False)
    before = (block_owner[None, :] == block_owner[:, None]) & (ids[None, :] < ids[:, None])
    ranks = jnp.sum(before, axis=1, dtype=jnp.int32)
    mine = block_owner == dp
    picks = []
    for slot in range(slots):
        chosen = mine & (ranks == slot)
        index = jnp.sum(jnp.where(chosen, ids, 0))
        at = (index // blocks, (index % blocks) * rows, 0)
        piece = take(back, at, (1, rows, student_width))[0]
        picks.append(jnp.where(jnp.any(chosen), piece, jnp.zeros((), half)))
    student_out = jnp.stack(picks, axis=1)
    return (student_out[None], adapter_grad)


def solution(mesh):
    return jax.shard_map(
        on_device,
        mesh=mesh,
        in_specs=(
            P("dp", "mp"),
            P("mp", None),
            P("dp", "mp"),
            P("mp"),
            P("mp", None),
            P("dp"),
            P(),
            P("dp", "mp", None, None),
            P("dp", "mp", None, None),
            P(),
            P(None, "mp"),
            P(None, "mp"),
            P(None, "mp"),
        ),
        out_specs=(P("dp", "mp", None, None), P("mp", "dp")),
        check_vma=False,
    )
```

```python
import jax
import jax.numpy as jnp
from jax import lax
from jax.experimental import pallas as pl
from jax.experimental.pallas import tpu as pltpu
from jax.sharding import PartitionSpec as P

BLK = 128
epsilon = 1e-06
half = jnp.bfloat16
full = jnp.float32


def exchange(pieces, axis):
    return lax.all_to_all(pieces, axis, split_axis=0, concat_axis=0, tiled=True)


def take(array, starts, sizes):
    return lax.dynamic_slice(array, starts, sizes, allow_negative_indices=False)


def three_parts(value):
    first = lax.reduce_precision(value, 8, 7)
    rest = value - first
    second = lax.reduce_precision(rest, 8, 7)
    return jnp.stack([first, second, rest - second]).astype(half)


def times_rows(left, right):
    return lax.dot_general(left, right, (((1,), (1,)), ((), ())), preferred_element_type=full)


SIDE = 4


def step(value, along_y, along_z):
    pairs = []
    for y in range(SIDE):
        for z in range(SIDE):
            to = ((y + along_y) % SIDE) * SIDE + (z + along_z) % SIDE
            pairs.append((y * SIDE + z, to))
    return lax.ppermute(value, "mp", pairs)


def far_kernel(place, left, right, lower0, upper0, lower1, upper1, held, sems):
    width = held.shape[2]
    y, z = lax.rem(place[0] + 2, SIDE), lax.rem(place[1] + 2, SIDE)
    middle = BLK // 2
    loads = []
    for index in range(2 * SIDE):
        piece = y * SIDE + index if index < SIDE else (index - SIDE) * SIDE + z
        columns = pl.ds(pl.multiple_of(piece * width, width), width)
        load = pltpu.make_async_copy(right.at[:, columns], held.at[index], sems.at[index])
        load.start()
        loads.append(load)
    for index in range(2 * SIDE):
        loads[index].wait()
        block, at = index // SIDE, index % SIDE
        value = jnp.dot(
            left[pl.ds(block * BLK, BLK), :], held[index], preferred_element_type=full
        ).astype(half)
        lower, upper = (lower0, upper0) if block == 0 else (lower1, upper1)
        lower[at] = value[:middle]
        upper[at] = value[middle:]


def near_kernel(place, left, right, kept0, up0, down0, kept1, up1, down1, held, sems):
    outs = {0: (kept0, kept1), 1: (up0, up1), 3: (down0, down1)}
    width = held.shape[2]
    y, z = place[0], place[1]

    def load(index):
        piece = lax.rem(y + index // SIDE, SIDE) * SIDE + lax.rem(index, SIDE)
        columns = pl.ds(pl.multiple_of(piece * width, width), width)
        return pltpu.make_async_copy(right.at[:, columns], held.at[index], sems.at[index])

    for index in range(SIDE * SIDE):
        load(index).start()

    @pl.loop(0, SIDE * SIDE)
    def _(index):
        load(index).wait()
        value = jnp.dot(left[...], held[index], preferred_element_type=full).astype(half)
        along_y, at_z = index // SIDE, lax.rem(index, SIDE)
        at_y, along_z = lax.rem(y + along_y, SIDE), lax.rem(at_z - z + SIDE, SIDE)
        for distance, (first, second) in outs.items():

            @pl.when(along_y == distance)
            def _():
                first[at_z] = value[:BLK]

            @pl.when(along_z == distance)
            def _():
                second[at_y] = value[BLK:]


def merge_kernel(*refs):
    ins, outs = refs[:8], refs[8:]
    middle = BLK // 2
    for block in (0, 1):
        up, down, lower, upper = ins[4 * block : 4 * block + 4]
        to_up, to_down = outs[2 * block], outs[2 * block + 1]
        to_up[0, :middle] = (up[0, :middle].astype(full) + lower[0].astype(full)).astype(half)
        to_up[0, middle:] = up[0, middle:]
        to_down[0, :middle] = down[0, :middle]
        to_down[0, middle:] = (down[0, middle:].astype(full) + upper[0].astype(full)).astype(half)


def gather_kernel(place, *refs):
    ins, outs = refs[:6], refs[7:]
    for block in (0, 1):
        kept, from_down, from_up = ins[3 * block : 3 * block + 3]
        here = place[1 - block]
        for distance in range(SIDE):
            at = lax.rem(here + distance, SIDE)
            value = kept[at].astype(full) + from_down[at].astype(full) + from_up[at].astype(full)
            out = outs[SIDE * block + distance]
            out[...] = value.astype(out.dtype)


def teacher_terms(attention, out_proj, mp, order):
    width = attention.shape[1]
    whole = pl.BlockSpec(memory_space=pltpu.VMEM)
    scalars = pl.BlockSpec(memory_space=pltpu.SMEM)
    anywhere = pl.BlockSpec(memory_space=pl.ANY)
    limit = pltpu.CompilerParams(vmem_limit_bytes=40 * 1024 * 1024)
    place = jnp.stack([mp // SIDE, mp % SIDE]).astype(jnp.int32)
    full_piece = jax.ShapeDtypeStruct((SIDE, BLK, width), half)
    half_piece = jax.ShapeDtypeStruct((SIDE, BLK // 2, width), half)
    moves = full_piece.size
    one_piece = pl.BlockSpec((1, BLK, width), lambda i: (i, 0, 0))
    one_half = pl.BlockSpec((1, BLK // 2, width), lambda i: (i, 0, 0))

    def terms(kernel, pieces, count, blocks):
        return pl.pallas_call(
            kernel,
            in_specs=[scalars, whole, pl.BlockSpec(memory_space=pltpu.HBM)],
            out_specs=[whole] * len(pieces),
            out_shape=pieces,
            scratch_shapes=[
                pltpu.VMEM((count, width, width), half),
                pltpu.SemaphoreType.DMA((count,)),
            ],
            compiler_params=pltpu.CompilerParams(vmem_limit_bytes=48 * 1024 * 1024),
            cost_estimate=pl.CostEstimate(
                flops=2 * blocks * BLK * count * width * width,
                bytes_accessed=2 * count * width * width,
                transcendentals=0,
            ),
        )(place, attention, out_proj)

    lower0, upper0, lower1, upper1 = terms(far_kernel, [half_piece] * 4, 2 * SIDE, 1)
    kept0, up0, down0, kept1, up1, down1 = terms(near_kernel, [full_piece] * 6, SIDE * SIDE, 2)
    lower0, upper0 = step(lower0, 1, 0), step(upper0, -1, 0)
    lower1, upper1 = step(lower1, 0, 1), step(upper1, 0, -1)
    up0, down0, up1, down1 = pl.pallas_call(
        merge_kernel,
        grid=(SIDE,),
        in_specs=[one_piece, one_piece, one_half, one_half] * 2,
        out_specs=[one_piece] * 4,
        out_shape=[full_piece] * 4,
        compiler_params=limit,
        cost_estimate=pl.CostEstimate(
            flops=4 * moves, bytes_accessed=20 * moves, transcendentals=0
        ),
    )(up0, down0, lower0, upper0, up1, down1, lower1, upper1)
    from_down0, from_up0 = step(up0, 1, 0), step(down0, -1, 0)
    from_down1, from_up1 = step(up1, 0, 1), step(down1, 0, -1)
    sums = pl.pallas_call(
        gather_kernel,
        in_specs=[scalars] + [whole] * 6 + [anywhere],
        out_specs=[whole] * (2 * SIDE),
        out_shape=[
            jax.ShapeDtypeStruct((BLK, width), half if distance else full)
            for block in (0, 1)
            for distance in range(SIDE)
        ],
        compiler_params=limit,
        cost_estimate=pl.CostEstimate(
            flops=4 * moves, bytes_accessed=16 * moves, transcendentals=0
        ),
    )(place, kept0, from_down0, from_up0, kept1, from_down1, from_up1, *order)
    results = []
    for block in (0, 1):
        mine = sums[SIDE * block : SIDE * block + SIDE]
        arrived = [
            step(mine[d], 0, d) if block == 0 else step(mine[d], d, 0) for d in range(1, SIDE)
        ]
        results.append([mine[0]] + arrived)
    return results


def total(values):
    result = values[0].astype(full)
    for value in values[1:]:
        result = result + value.astype(full)
    return result


def backward_kernel(dy, down, gate, up, order, grad_gate, grad_up, dh):
    del order
    rows = 8
    for chunk in range(2):
        columns = pl.ds(chunk * (down.shape[1] // 2), down.shape[1] // 2)
        value = jnp.dot(dy[...], down[:, columns], preferred_element_type=full)
        for index in range(value.shape[0] // rows):
            to = (index % 2) * BLK + (index // 2) * rows
            dh[pl.ds(to, rows), columns] = value[index * rows : index * rows + rows]
    gate_val = gate[...]
    sigma = jax.nn.sigmoid(gate_val)
    grad_gate[...] = (dh[...] * up[...] * sigma * (1.0 + gate_val * (1.0 - sigma))).astype(half)
    grad_up[...] = (dh[...] * (gate_val * sigma)).astype(half)


def backward(dy, down, gate, up, order):
    whole = pl.BlockSpec(memory_space=pltpu.VMEM)
    shape = jax.ShapeDtypeStruct(gate.shape, half)
    return pl.pallas_call(
        backward_kernel,
        in_specs=[whole] * 4 + [pl.BlockSpec(memory_space=pl.ANY)],
        out_specs=[whole, whole],
        out_shape=[shape, shape],
        scratch_shapes=[pltpu.VMEM(gate.shape, full)],
        compiler_params=pltpu.CompilerParams(vmem_limit_bytes=56 * 1024 * 1024),
        cost_estimate=pl.CostEstimate(
            flops=2 * dy.shape[0] * down.size,
            bytes_accessed=2 * (down.size + dy.size) + 16 * gate.size,
            transcendentals=gate.size,
        ),
    )(dy, down, gate, up, order)


def spread_kernel(piece, out, sems):
    copies = [
        pltpu.make_async_copy(piece, out.at[to], sems.at[to]) for to in range(out.shape[0])
    ]
    for copy in copies:
        copy.start()
    for copy in copies:
        copy.wait()


def spread(piece, count):
    whole = pl.BlockSpec(memory_space=pltpu.VMEM)
    return pl.pallas_call(
        spread_kernel,
        in_specs=[whole],
        out_specs=pl.BlockSpec(memory_space=pltpu.HBM),
        scratch_shapes=[pltpu.SemaphoreType.DMA((count,))],
        out_shape=jax.ShapeDtypeStruct((count,) + piece.shape, piece.dtype),
        compiler_params=pltpu.CompilerParams(vmem_limit_bytes=16 * 1024 * 1024),
        cost_estimate=pl.CostEstimate(
            flops=0, bytes_accessed=4 * count * piece.size, transcendentals=0
        ),
    )(piece)


def home_kernel(terms, state, out):
    value = state[...].astype(full)
    for source in range(terms.shape[0]):
        value = value + terms[source].astype(full)
    rows = state.shape[0]
    out[pl.ds(0, rows), :] = value.astype(half)
    out[pl.ds(rows, rows), :] = jnp.zeros(state.shape, half)


def home(terms, state):
    rows, width = state.shape
    whole = pl.BlockSpec(memory_space=pltpu.VMEM)
    return pl.pallas_call(
        home_kernel,
        in_specs=[whole, whole],
        out_specs=whole,
        out_shape=jax.ShapeDtypeStruct((2 * rows, width), half),
        compiler_params=pltpu.CompilerParams(vmem_limit_bytes=16 * 1024 * 1024),
        cost_estimate=pl.CostEstimate(
            flops=17 * rows * width, bytes_accessed=40 * rows * width, transcendentals=0
        ),
    )(terms, state)


def pool_kernel(place, message, token_slot, out, inverse, sh, weights, state, sems):
    sources, _, cols = message.shape
    rows = BLK // sources
    token_proj = message[0, :BLK].astype(full)
    for source in range(1, sources):
        token_proj = token_proj + message[source, :BLK].astype(full)
    squares = jnp.zeros((rows, cols), full)
    for source in range(sources):
        tail = message[source, BLK:].astype(full)
        sh[pl.ds(source * rows, rows), :] = tail[:rows]
        squares = squares + tail[rows:]
    tokens = token_slot.shape[1]
    squares = jnp.sum(squares, axis=0, keepdims=True)[:, :tokens]
    inverse[...] = lax.rsqrt(squares / place[1].astype(full) + epsilon)
    slots = jnp.where(place[0] == 0, token_slot[:, :BLK], token_slot[:, BLK:])
    scale = jnp.where(place[0] == 0, inverse[:, :BLK], inverse[:, BLK:])
    hits = slots == lax.broadcasted_iota(jnp.int32, (BLK, BLK), 0)
    counts = jnp.maximum(jnp.sum(hits.astype(full), axis=1, keepdims=True), 1.0)
    weights[...] = jnp.where(hits, scale, 0.0)
    first = weights[...].astype(half)
    second = (weights[...] - lax.reduce_precision(weights[...], 8, 7)).astype(half)
    token_proj = token_proj.astype(half)
    placed = jnp.dot(first, token_proj, preferred_element_type=full)
    placed = placed + jnp.dot(second, token_proj, preferred_element_type=full)
    placed = (placed / counts).astype(half).astype(full)
    state[...] = (sh[...] + placed).astype(half)
    copies = [
        pltpu.make_async_copy(state, out.at[to], sems.at[to]) for to in range(sources)
    ]
    for copy in copies:
        copy.start()
    for copy in copies:
        copy.wait()


def pool(message, token_slot, block, width_full):
    sources, _, cols = message.shape
    whole = pl.BlockSpec(memory_space=pltpu.VMEM)
    tokens = token_slot.shape[0]
    place = jnp.stack([block, jnp.full_like(block, width_full)]).astype(jnp.int32)
    return pl.pallas_call(
        pool_kernel,
        in_specs=[pl.BlockSpec(memory_space=pltpu.SMEM), whole, whole],
        out_specs=[pl.BlockSpec(memory_space=pltpu.HBM), whole],
        out_shape=[
            jax.ShapeDtypeStruct((sources, BLK, cols), half),
            jax.ShapeDtypeStruct((1, tokens), full),
        ],
        scratch_shapes=[
            pltpu.VMEM((BLK, cols), full),
            pltpu.VMEM((BLK, BLK), full),
            pltpu.VMEM((BLK, cols), half),
            pltpu.SemaphoreType.DMA((sources,)),
        ],
        compiler_params=pltpu.CompilerParams(vmem_limit_bytes=40 * 1024 * 1024),
        cost_estimate=pl.CostEstimate(
            flops=6 * message.size, bytes_accessed=4 * message.size, transcendentals=tokens
        ),
    )(place, message, token_slot[None])


def bring_kernel(order, *refs):
    del order
    count = len(refs) // 2
    sources, outs, sems = refs[:count], refs[count : 2 * count], refs[2 * count]
    copies = [
        pltpu.make_async_copy(source, out, sems.at[index])
        for index, (source, out) in enumerate(zip(sources, outs))
    ]
    for copy in copies:
        copy.start()
    for copy in copies:
        copy.wait()


def bring(arrays, order):
    return pl.pallas_call(
        bring_kernel,
        in_specs=[pl.BlockSpec(memory_space=pl.ANY)] + [pl.BlockSpec(memory_space=pltpu.HBM)] * len(arrays),
        out_specs=[pl.BlockSpec(memory_space=pltpu.VMEM)] * len(arrays),
        out_shape=[jax.ShapeDtypeStruct(a.shape, a.dtype) for a in arrays],
        scratch_shapes=[pltpu.SemaphoreType.DMA((len(arrays),))],
        compiler_params=pltpu.CompilerParams(vmem_limit_bytes=48 * 1024 * 1024),
        cost_estimate=pl.CostEstimate(
            flops=0, bytes_accessed=12 * arrays[0].size, transcendentals=0
        ),
    )(order, *arrays)


def forward_kernel(
    place, pieces, gain, order, gate_w, up_w, down_hbm,
    home_state, here_state, gate_hbm, up_hbm, out_hbm,
    normed, act, out, down_w, gate, up, out_sems, sems,
):
    del order
    down_load = pltpu.make_async_copy(down_hbm, down_w, sems.at[0])
    down_load.start()
    cols = pieces.shape[2]
    width = normed.shape[1]
    groups = width // cols
    mine = here_state.shape[0]
    mp = place[0]
    rows = pl.multiple_of(lax.rem(mp, groups) * mine, mine)
    pair = pl.multiple_of((mp // 2) * mine, mine)
    for group in range(groups):
        at = pl.ds(group * cols, cols)
        here_state[:, at] = pieces[(mp // groups) * groups + group, pl.ds(rows, mine), :]
        halves = []
        for block in range(2):
            two = pieces[block * groups + group, pl.ds(pair, mine), :].astype(full)
            halves.append(jnp.where(lax.rem(mp, 2) == 0, two[: mine // 2], two[mine // 2 :]))
        home_state[:, at] = jnp.concatenate(halves, axis=0).astype(half)
    for block in range(normed.shape[0] // BLK):
        rows = pl.ds(block * BLK, BLK)
        squares = jnp.zeros((BLK, 128), full)
        for group in range(groups):
            wide = pieces[block * groups + group].astype(full)
            wide = wide * wide
            for lane in range(0, cols, 128):
                squares = squares + wide[:, lane : lane + 128]
        mean = jnp.sum(squares, axis=1, keepdims=True) / width
        inverse = lax.rsqrt(mean + epsilon)
        for group in range(groups):
            at = pl.ds(group * cols, cols)
            wide = pieces[block * groups + group].astype(full)
            normed[rows, at] = (wide * inverse * gain[:, at]).astype(normed.dtype)
    half_hidden = gate.shape[1] // 2
    for index in range(2):
        at = pl.ds(index * half_hidden, half_hidden)
        gate[:, at] = jnp.dot(normed[...], gate_w[:, at], preferred_element_type=full)
        up[:, at] = jnp.dot(normed[...], up_w[:, at], preferred_element_type=full)
    gate_leaves = pltpu.make_async_copy(gate, gate_hbm, sems.at[1])
    up_leaves = pltpu.make_async_copy(up, up_hbm, sems.at[2])
    gate_leaves.start()
    up_leaves.start()
    gate_val = gate[...]
    act[...] = (gate_val * jax.nn.sigmoid(gate_val) * up[...]).astype(half)
    down_load.wait()
    rows = out.shape[1] // 2
    wide_chunk = 512

    def leave(index):
        at = pl.ds(pl.multiple_of(index * wide_chunk, wide_chunk), wide_chunk)
        return pltpu.make_async_copy(out.at[:, :, at], out_hbm.at[:, :, at], out_sems.at[index])

    @pl.loop(0, width // wide_chunk)
    def _(index):
        at = pl.ds(pl.multiple_of(index * wide_chunk, wide_chunk), wide_chunk)
        value = times_rows(act[...], down_w[at, :])
        for to in range(out.shape[0]):
            first = value[to * rows : to * rows + rows]
            second = value[BLK + to * rows : BLK + to * rows + rows]
            out[to, :, at] = jnp.concatenate([first, second], axis=0).astype(half)
        leave(index).start()

    for index in range(width // wide_chunk):
        leave(index).wait()
    gate_leaves.wait()
    up_leaves.wait()


def forward(pieces, gain, gate_w, up_w, down_w, mp, order):
    width, hidden = gate_w.shape
    n_mp = pieces.shape[0]
    rows = 2 * BLK
    mine = rows // n_mp
    whole = pl.BlockSpec(memory_space=pltpu.VMEM)
    far = pl.BlockSpec(memory_space=pltpu.HBM)
    return pl.pallas_call(
        forward_kernel,
        in_specs=[pl.BlockSpec(memory_space=pltpu.SMEM), whole, whole]
        + [pl.BlockSpec(memory_space=pl.ANY), whole, whole, far],
        out_specs=[whole, whole, far, far, far],
        out_shape=[
            jax.ShapeDtypeStruct((mine, width), half),
            jax.ShapeDtypeStruct((mine, width), half),
            jax.ShapeDtypeStruct((rows, hidden), full),
            jax.ShapeDtypeStruct((rows, hidden), full),
            jax.ShapeDtypeStruct((n_mp, mine, width), half),
        ],
        scratch_shapes=[
            pltpu.VMEM((rows, width), half),
            pltpu.VMEM((rows, hidden), half),
            pltpu.VMEM((n_mp, mine, width), half),
            pltpu.VMEM((width, hidden), half),
            pltpu.VMEM((rows, hidden), full),
            pltpu.VMEM((rows, hidden), full),
            pltpu.SemaphoreType.DMA((width // 512,)),
            pltpu.SemaphoreType.DMA((3,)),
        ],
        compiler_params=pltpu.CompilerParams(vmem_limit_bytes=48 * 1024 * 1024),
        cost_estimate=pl.CostEstimate(
            flops=6 * rows * width * hidden,
            bytes_accessed=6 * width * hidden + 10 * rows * width,
            transcendentals=rows * hidden,
        ),
    )(mp[None].astype(jnp.int32), pieces, gain[None], order, gate_w, up_w, down_w)


def slope_kernel(terms, dy, state, gain, order, out):
    del order
    rows, width = dy.shape
    cols = out.shape[2]
    wide = state[...].astype(full)
    inverse = lax.rsqrt(jnp.mean(wide * wide, axis=1, keepdims=True) + epsilon)
    dn = terms[0].astype(full)
    for source in range(1, terms.shape[0]):
        dn = dn + terms[source].astype(full)
    gained = gain[...] * dn
    mean = jnp.mean(gained * wide, axis=1, keepdims=True)
    dx = dy[...].astype(full) + inverse * gained - wide * (inverse * inverse * inverse) * mean
    for group in range(out.shape[0]):
        out[group] = dx[:, group * cols : (group + 1) * cols].astype(out.dtype)


def slope(terms, dy, state, gain, groups, order):
    rows, width = dy.shape
    whole = pl.BlockSpec(memory_space=pltpu.VMEM)
    return pl.pallas_call(
        slope_kernel,
        in_specs=[whole] * 4 + [pl.BlockSpec(memory_space=pl.ANY)],
        out_specs=whole,
        out_shape=jax.ShapeDtypeStruct((groups, rows, width // groups), half),
        compiler_params=pltpu.CompilerParams(vmem_limit_bytes=16 * 1024 * 1024),
        cost_estimate=pl.CostEstimate(
            flops=30 * rows * width, bytes_accessed=40 * rows * width, transcendentals=rows
        ),
    )(terms, dy, state, gain[None], order)


def on_device(
    attention,
    out_proj,
    residual,
    final_gain,
    adapter_weight,
    token_slot,
    block_owner,
    student_hidden,
    cotangent,
    student_gain,
    gate_weight,
    up_weight,
    down_weight,
):
    tokens, width_here = attention.shape
    width_full = out_proj.shape[1]
    student_width = adapter_weight.shape[1]
    blocks = tokens // BLK
    n_mp = lax.axis_size("mp")
    n_dp = lax.axis_size("dp")
    dp = lax.axis_index("dp")
    mp = lax.axis_index("mp")
    slots = student_hidden.shape[2]
    rows = BLK // n_mp
    groups = n_mp // blocks
    cols = student_width // groups
    out_cols = student_width // n_dp
    mine_rows = blocks * rows

    ids = jnp.arange(block_owner.shape[0], dtype=jnp.int32)
    my_ids = dp * blocks + jnp.arange(blocks, dtype=jnp.int32)
    my_owner = take(block_owner, (dp * blocks,), (blocks,))
    my_slot = jnp.sum(
        (block_owner[None, :] == my_owner[:, None]) & (ids[None, :] < my_ids[:, None]),
        axis=1,
        dtype=jnp.int32,
    )

    def fetch(array):
        everyone = lax.all_gather(array[0], "dp", axis=0, tiled=False)
        picked = []
        for k in range(blocks):
            at = (my_owner[k], 0, my_slot[k], 0)
            piece = take(everyone, at, (1, rows, 1, student_width))
            picked.append(piece.reshape(rows, student_width))
        return jnp.stack(picked)

    sh_rows = fetch(student_hidden)
    dy_rows = fetch(cotangent)
    dy = lax.all_gather(dy_rows, "mp", axis=0, tiled=False)

    hidden = residual.astype(full) + jnp.concatenate(
        [total(v) for v in teacher_terms(attention, out_proj, mp, (sh_rows,))], axis=0
    )
    squares = jnp.sum(hidden * hidden, axis=1)
    gained_hidden = hidden * final_gain
    parts = jnp.einsum(
        "ktd,dce->kcte",
        gained_hidden.astype(half).reshape(blocks, BLK, width_here),
        adapter_weight.reshape(width_here, groups, cols),
        preferred_element_type=full,
    ).astype(half)
    sh_parts = jnp.swapaxes(sh_rows.reshape(blocks, rows, groups, cols), 1, 2)
    sq_parts = jnp.zeros((8, cols), half).at[:3, :tokens].set(three_parts(squares))
    message = jnp.concatenate(
        [
            parts,
            sh_parts,
            jnp.broadcast_to(sq_parts[None, None], (blocks, groups) + sq_parts.shape),
        ],
        axis=2,
    )
    message = exchange(message.reshape(n_mp, BLK + rows + 8, cols), "mp")
    states, inverse_rms = pool(message, token_slot, mp // groups, width_full)
    states = exchange(states, "mp")

    slots_block = token_slot.reshape(blocks, BLK)
    onehot = slots_block[:, None, :] == jnp.arange(BLK, dtype=jnp.int32)[None, :, None]
    counts = jnp.maximum(jnp.sum(onehot.astype(full), axis=2), 1.0)
    onehot = onehot.astype(half)
    normed = (gained_hidden * inverse_rms.reshape(tokens, 1)).astype(half).reshape(blocks, BLK, width_here)
    pooled = jnp.einsum("krt,ktd->krd", onehot, normed, preferred_element_type=full)
    pooled = (pooled / counts[:, :, None]).astype(half)
    pooled_all = lax.all_gather(pooled.reshape(n_mp, mine_rows, width_here), "dp", axis=0, tiled=False)
    pooled_all = jnp.swapaxes(pooled_all, 0, 1).reshape(n_dp * tokens, width_here)

    weights = bring((gate_weight, up_weight), inverse_rms)
    home_state, here_state, gate, up, output = forward(
        states, student_gain, *weights, down_weight, mp, pooled
    )
    grad_gate, grad_up = backward(dy.reshape(tokens, student_width), down_weight, gate, up, output)
    dn = (times_rows(grad_gate, gate_weight) + times_rows(grad_up, up_weight)).astype(half)
    output = exchange(output, "mp")
    dn, output = lax.optimization_barrier((dn, output))
    dn = exchange(dn.reshape(n_mp, mine_rows, student_width), "mp")
    out_rows = home(output, home_state)
    dproj = slope(
        dn,
        take(
            dy, ((mp % groups) * blocks, mp // groups, 0, 0), (blocks, 1, rows, student_width)
        ).reshape(mine_rows, student_width),
        here_state,
        student_gain,
        n_dp,
        out_rows,
    )
    dproj = exchange(spread(exchange(dproj, "dp"), n_mp), "mp")
    adapter_grad = lax.dot_general(
        pooled_all,
        dproj.reshape(n_dp * tokens, out_cols),
        (((0,), (0,)), ((), ())),
        preferred_element_type=full,
    )

    back = lax.all_gather(out_rows, "dp", axis=0, tiled=False)
    before = (block_owner[None, :] == block_owner[:, None]) & (ids[None, :] < ids[:, None])
    ranks = jnp.sum(before, axis=1, dtype=jnp.int32)
    mine = block_owner == dp
    picks = []
    for slot in range(slots):
        chosen = mine & (ranks == slot)
        index = jnp.sum(jnp.where(chosen, ids, 0))
        at = (index // blocks, (index % blocks) * rows, 0)
        piece = take(back, at, (1, rows, student_width))[0]
        picks.append(jnp.where(jnp.any(chosen), piece, jnp.zeros((), half)))
    student_out = jnp.stack(picks, axis=1)
    return (student_out[None], adapter_grad)


def solution(mesh):
    return jax.shard_map(
        on_device,
        mesh=mesh,
        in_specs=(
            P("dp", "mp"),
            P("mp", None),
            P("dp", "mp"),
            P("mp"),
            P("mp", None),
            P("dp"),
            P(),
            P("dp", "mp", None, None),
            P("dp", "mp", None, None),
            P(),
            P(None, "mp"),
            P(None, "mp"),
            P(None, "mp"),
        ),
        out_specs=(P("dp", "mp", None, None), P("mp", "dp")),
        check_vma=False,
    )
```

```python
import jax
import jax.numpy as jnp
from jax import lax
from jax.experimental import pallas as pl
from jax.experimental.pallas import tpu as pltpu
from jax.sharding import PartitionSpec as P

BLK = 128
epsilon = 1e-06
half = jnp.bfloat16
full = jnp.float32


def exchange(pieces, axis):
    return lax.all_to_all(pieces, axis, split_axis=0, concat_axis=0, tiled=True)


def take(array, starts, sizes):
    return lax.dynamic_slice(array, starts, sizes, allow_negative_indices=False)


def three_parts(value):
    first = lax.reduce_precision(value, 8, 7)
    rest = value - first
    second = lax.reduce_precision(rest, 8, 7)
    return jnp.stack([first, second, rest - second]).astype(half)


def times_rows(left, right):
    return lax.dot_general(left, right, (((1,), (1,)), ((), ())), preferred_element_type=full)


SIDE = 4


def step(value, along_y, along_z):
    pairs = []
    for y in range(SIDE):
        for z in range(SIDE):
            to = ((y + along_y) % SIDE) * SIDE + (z + along_z) % SIDE
            pairs.append((y * SIDE + z, to))
    return lax.ppermute(value, "mp", pairs)


def far_kernel(place, left, right, lower0, upper0, lower1, upper1, held, sems):
    width = held.shape[2]
    y, z = lax.rem(place[0] + 2, SIDE), lax.rem(place[1] + 2, SIDE)
    middle = BLK // 2
    loads = []
    for index in range(2 * SIDE):
        piece = y * SIDE + index if index < SIDE else (index - SIDE) * SIDE + z
        columns = pl.ds(pl.multiple_of(piece * width, width), width)
        load = pltpu.make_async_copy(right.at[:, columns], held.at[index], sems.at[index])
        load.start()
        loads.append(load)
    for index in range(2 * SIDE):
        loads[index].wait()
        block, at = index // SIDE, index % SIDE
        value = jnp.dot(
            left[pl.ds(block * BLK, BLK), :], held[index], preferred_element_type=full
        ).astype(half)
        lower, upper = (lower0, upper0) if block == 0 else (lower1, upper1)
        lower[at] = value[:middle]
        upper[at] = value[middle:]


def near_kernel(place, left, right, kept0, up0, down0, kept1, up1, down1, held, sems):
    outs = {0: (kept0, kept1), 1: (up0, up1), 3: (down0, down1)}
    width = held.shape[2]
    y, z = place[0], place[1]

    def load(index):
        piece = lax.rem(y + index // SIDE, SIDE) * SIDE + lax.rem(index, SIDE)
        columns = pl.ds(pl.multiple_of(piece * width, width), width)
        return pltpu.make_async_copy(right.at[:, columns], held.at[index], sems.at[index])

    for index in range(SIDE * SIDE):
        load(index).start()

    @pl.loop(0, SIDE * SIDE)
    def _(index):
        load(index).wait()
        value = jnp.dot(left[...], held[index], preferred_element_type=full).astype(half)
        along_y, at_z = index // SIDE, lax.rem(index, SIDE)
        at_y, along_z = lax.rem(y + along_y, SIDE), lax.rem(at_z - z + SIDE, SIDE)
        for distance, (first, second) in outs.items():

            @pl.when(along_y == distance)
            def _():
                first[at_z] = value[:BLK]

            @pl.when(along_z == distance)
            def _():
                second[at_y] = value[BLK:]


def merge_kernel(*refs):
    ins, outs = refs[:8], refs[8:]
    middle = BLK // 2
    for block in (0, 1):
        up, down, lower, upper = ins[4 * block : 4 * block + 4]
        to_up, to_down = outs[2 * block], outs[2 * block + 1]
        to_up[0, :middle] = (up[0, :middle].astype(full) + lower[0].astype(full)).astype(half)
        to_up[0, middle:] = up[0, middle:]
        to_down[0, :middle] = down[0, :middle]
        to_down[0, middle:] = (down[0, middle:].astype(full) + upper[0].astype(full)).astype(half)


def gather_kernel(place, *refs):
    ins, outs = refs[:6], refs[8:]
    for block in (0, 1):
        kept, from_down, from_up = ins[3 * block : 3 * block + 3]
        here = place[1 - block]
        for distance in range(SIDE):
            at = lax.rem(here + distance, SIDE)
            value = kept[at].astype(full) + from_down[at].astype(full) + from_up[at].astype(full)
            out = outs[SIDE * block + distance]
            out[...] = value.astype(out.dtype)


def teacher_terms(attention, out_proj, mp, order):
    width = attention.shape[1]
    whole = pl.BlockSpec(memory_space=pltpu.VMEM)
    scalars = pl.BlockSpec(memory_space=pltpu.SMEM)
    anywhere = pl.BlockSpec(memory_space=pl.ANY)
    limit = pltpu.CompilerParams(vmem_limit_bytes=40 * 1024 * 1024)
    place = jnp.stack([mp // SIDE, mp % SIDE]).astype(jnp.int32)
    full_piece = jax.ShapeDtypeStruct((SIDE, BLK, width), half)
    half_piece = jax.ShapeDtypeStruct((SIDE, BLK // 2, width), half)
    moves = full_piece.size
    one_piece = pl.BlockSpec((1, BLK, width), lambda i: (i, 0, 0))
    one_half = pl.BlockSpec((1, BLK // 2, width), lambda i: (i, 0, 0))

    def terms(kernel, pieces, count, blocks):
        return pl.pallas_call(
            kernel,
            in_specs=[scalars, whole, pl.BlockSpec(memory_space=pltpu.HBM)],
            out_specs=[whole] * len(pieces),
            out_shape=pieces,
            scratch_shapes=[
                pltpu.VMEM((count, width, width), half),
                pltpu.SemaphoreType.DMA((count,)),
            ],
            compiler_params=pltpu.CompilerParams(vmem_limit_bytes=48 * 1024 * 1024),
            cost_estimate=pl.CostEstimate(
                flops=2 * blocks * BLK * count * width * width,
                bytes_accessed=2 * count * width * width,
                transcendentals=0,
            ),
        )(place, attention, out_proj)

    lower0, upper0, lower1, upper1 = terms(far_kernel, [half_piece] * 4, 2 * SIDE, 1)
    kept0, up0, down0, kept1, up1, down1 = terms(near_kernel, [full_piece] * 6, SIDE * SIDE, 2)
    lower0, upper0 = step(lower0, 1, 0), step(upper0, -1, 0)
    lower1, upper1 = step(lower1, 0, 1), step(upper1, 0, -1)
    up0, down0, up1, down1 = pl.pallas_call(
        merge_kernel,
        grid=(SIDE,),
        in_specs=[one_piece, one_piece, one_half, one_half] * 2,
        out_specs=[one_piece] * 4,
        out_shape=[full_piece] * 4,
        compiler_params=limit,
        cost_estimate=pl.CostEstimate(
            flops=4 * moves, bytes_accessed=20 * moves, transcendentals=0
        ),
    )(up0, down0, lower0, upper0, up1, down1, lower1, upper1)
    from_down0, from_up0 = step(up0, 1, 0), step(down0, -1, 0)
    from_down1, from_up1 = step(up1, 0, 1), step(down1, 0, -1)
    sums = pl.pallas_call(
        gather_kernel,
        in_specs=[scalars] + [whole] * 6 + [anywhere] * 2,
        out_specs=[whole] * (2 * SIDE),
        out_shape=[
            jax.ShapeDtypeStruct((BLK, width), half if distance else full)
            for block in (0, 1)
            for distance in range(SIDE)
        ],
        compiler_params=limit,
        cost_estimate=pl.CostEstimate(
            flops=4 * moves, bytes_accessed=16 * moves, transcendentals=0
        ),
    )(place, kept0, from_down0, from_up0, kept1, from_down1, from_up1, *order)
    results = []
    for block in (0, 1):
        mine = sums[SIDE * block : SIDE * block + SIDE]
        arrived = [
            step(mine[d], 0, d) if block == 0 else step(mine[d], d, 0) for d in range(1, SIDE)
        ]
        results.append([mine[0]] + arrived)
    return results


def total(values):
    result = values[0].astype(full)
    for value in values[1:]:
        result = result + value.astype(full)
    return result


def backward_kernel(dy, down, gate, up, order, grad_gate, grad_up, dh):
    del order
    rows = 8
    for chunk in range(2):
        columns = pl.ds(chunk * (down.shape[1] // 2), down.shape[1] // 2)
        value = jnp.dot(dy[...], down[:, columns], preferred_element_type=full)
        for index in range(value.shape[0] // rows):
            to = (index % 2) * BLK + (index // 2) * rows
            dh[pl.ds(to, rows), columns] = value[index * rows : index * rows + rows]
    gate_val = gate[...]
    sigma = jax.nn.sigmoid(gate_val)
    grad_gate[...] = (dh[...] * up[...] * sigma * (1.0 + gate_val * (1.0 - sigma))).astype(half)
    grad_up[...] = (dh[...] * (gate_val * sigma)).astype(half)


def backward(dy, down, gate, up, order):
    whole = pl.BlockSpec(memory_space=pltpu.VMEM)
    shape = jax.ShapeDtypeStruct(gate.shape, half)
    return pl.pallas_call(
        backward_kernel,
        in_specs=[whole] * 4 + [pl.BlockSpec(memory_space=pl.ANY)],
        out_specs=[whole, whole],
        out_shape=[shape, shape],
        scratch_shapes=[pltpu.VMEM(gate.shape, full)],
        compiler_params=pltpu.CompilerParams(vmem_limit_bytes=56 * 1024 * 1024),
        cost_estimate=pl.CostEstimate(
            flops=2 * dy.shape[0] * down.size,
            bytes_accessed=2 * (down.size + dy.size) + 16 * gate.size,
            transcendentals=gate.size,
        ),
    )(dy, down, gate, up, order)


def spread_kernel(piece, out, sems):
    copies = [
        pltpu.make_async_copy(piece, out.at[to], sems.at[to]) for to in range(out.shape[0])
    ]
    for copy in copies:
        copy.start()
    for copy in copies:
        copy.wait()


def spread(piece, count):
    whole = pl.BlockSpec(memory_space=pltpu.VMEM)
    return pl.pallas_call(
        spread_kernel,
        in_specs=[whole],
        out_specs=pl.BlockSpec(memory_space=pltpu.HBM),
        scratch_shapes=[pltpu.SemaphoreType.DMA((count,))],
        out_shape=jax.ShapeDtypeStruct((count,) + piece.shape, piece.dtype),
        compiler_params=pltpu.CompilerParams(vmem_limit_bytes=16 * 1024 * 1024),
        cost_estimate=pl.CostEstimate(
            flops=0, bytes_accessed=4 * count * piece.size, transcendentals=0
        ),
    )(piece)


def home_kernel(terms, state, out):
    value = state[...].astype(full)
    for source in range(terms.shape[0]):
        value = value + terms[source].astype(full)
    rows = state.shape[0]
    out[pl.ds(0, rows), :] = value.astype(half)
    out[pl.ds(rows, rows), :] = jnp.zeros(state.shape, half)


def home(terms, state):
    rows, width = state.shape
    whole = pl.BlockSpec(memory_space=pltpu.VMEM)
    return pl.pallas_call(
        home_kernel,
        in_specs=[whole, whole],
        out_specs=whole,
        out_shape=jax.ShapeDtypeStruct((2 * rows, width), half),
        compiler_params=pltpu.CompilerParams(vmem_limit_bytes=16 * 1024 * 1024),
        cost_estimate=pl.CostEstimate(
            flops=17 * rows * width, bytes_accessed=40 * rows * width, transcendentals=0
        ),
    )(terms, state)


def pool_kernel(place, message, token_slot, out, inverse, sh, weights, state, sems):
    sources, _, cols = message.shape
    rows = BLK // sources
    token_proj = message[0, :BLK].astype(full)
    for source in range(1, sources):
        token_proj = token_proj + message[source, :BLK].astype(full)
    squares = jnp.zeros((rows, cols), full)
    for source in range(sources):
        tail = message[source, BLK:].astype(full)
        sh[pl.ds(source * rows, rows), :] = tail[:rows]
        squares = squares + tail[rows:]
    tokens = token_slot.shape[1]
    squares = jnp.sum(squares, axis=0, keepdims=True)[:, :tokens]
    inverse[...] = lax.rsqrt(squares / place[1].astype(full) + epsilon)
    slots = jnp.where(place[0] == 0, token_slot[:, :BLK], token_slot[:, BLK:])
    scale = jnp.where(place[0] == 0, inverse[:, :BLK], inverse[:, BLK:])
    hits = slots == lax.broadcasted_iota(jnp.int32, (BLK, BLK), 0)
    counts = jnp.maximum(jnp.sum(hits.astype(full), axis=1, keepdims=True), 1.0)
    weights[...] = jnp.where(hits, scale, 0.0)
    first = weights[...].astype(half)
    second = (weights[...] - lax.reduce_precision(weights[...], 8, 7)).astype(half)
    token_proj = token_proj.astype(half)
    placed = jnp.dot(first, token_proj, preferred_element_type=full)
    placed = placed + jnp.dot(second, token_proj, preferred_element_type=full)
    placed = (placed / counts).astype(half).astype(full)
    state[...] = (sh[...] + placed).astype(half)
    copies = [
        pltpu.make_async_copy(state, out.at[to], sems.at[to]) for to in range(sources)
    ]
    for copy in copies:
        copy.start()
    for copy in copies:
        copy.wait()


def pool(message, token_slot, block, width_full):
    sources, _, cols = message.shape
    whole = pl.BlockSpec(memory_space=pltpu.VMEM)
    tokens = token_slot.shape[0]
    place = jnp.stack([block, jnp.full_like(block, width_full)]).astype(jnp.int32)
    return pl.pallas_call(
        pool_kernel,
        in_specs=[pl.BlockSpec(memory_space=pltpu.SMEM), whole, whole],
        out_specs=[pl.BlockSpec(memory_space=pltpu.HBM), whole],
        out_shape=[
            jax.ShapeDtypeStruct((sources, BLK, cols), half),
            jax.ShapeDtypeStruct((1, tokens), full),
        ],
        scratch_shapes=[
            pltpu.VMEM((BLK, cols), full),
            pltpu.VMEM((BLK, BLK), full),
            pltpu.VMEM((BLK, cols), half),
            pltpu.SemaphoreType.DMA((sources,)),
        ],
        compiler_params=pltpu.CompilerParams(vmem_limit_bytes=40 * 1024 * 1024),
        cost_estimate=pl.CostEstimate(
            flops=6 * message.size, bytes_accessed=4 * message.size, transcendentals=tokens
        ),
    )(place, message, token_slot[None])


def forward_kernel(
    pieces, gain, order, other, gate_hbm, up_hbm, down_hbm, state, gate, up, out, normed, act, held, sems
):
    del order, other
    parts = 3
    part = gate_hbm.shape[0] // parts

    def load(which, source, third):
        at = pl.ds(third * part, part)
        return pltpu.make_async_copy(
            source.at[at], held.at[which, at], sems.at[parts * which + third]
        )

    for third in range(parts):
        load(0, gate_hbm, third).start()
        load(1, up_hbm, third).start()
    cols = pieces.shape[2]
    groups = state.shape[1] // cols
    for block in range(state.shape[0] // BLK):
        rows = pl.ds(block * BLK, BLK)
        squares = jnp.zeros((BLK, 128), full)
        for group in range(groups):
            value = pieces[block * groups + group]
            state[rows, pl.ds(group * cols, cols)] = value
            wide = value.astype(full)
            wide = wide * wide
            for lane in range(0, cols, 128):
                squares = squares + wide[:, lane : lane + 128]
        mean = jnp.sum(squares, axis=1, keepdims=True) / state.shape[1]
        inverse = lax.rsqrt(mean + epsilon)
        for group in range(groups):
            at = pl.ds(group * cols, cols)
            wide = pieces[block * groups + group].astype(full)
            normed[rows, at] = (wide * inverse * gain[:, at]).astype(normed.dtype)
    half_hidden = gate.shape[1] // 2
    for third in range(parts):
        load(0, gate_hbm, third).wait()
        load(1, up_hbm, third).wait()
        load(2, down_hbm, third).start()
        depth = pl.ds(third * part, part)
        for index in range(2):
            at = pl.ds(index * half_hidden, half_hidden)
            for which, total_ref in ((0, gate), (1, up)):
                value = jnp.dot(
                    normed[:, depth], held[which, depth, at], preferred_element_type=full
                )
                total_ref[:, at] = value if third == 0 else total_ref[:, at] + value
    gate_val = gate[...]
    act[...] = (gate_val * jax.nn.sigmoid(gate_val) * up[...]).astype(half)
    for third in range(parts):
        load(2, down_hbm, third).wait()
    down_w = held.at[2]
    rows = out.shape[1] // 2
    wide_chunk = 512

    @pl.loop(0, state.shape[1] // wide_chunk)
    def _(index):
        at = pl.ds(pl.multiple_of(index * wide_chunk, wide_chunk), wide_chunk)
        value = times_rows(act[...], down_w[at, :])
        for to in range(out.shape[0]):
            first = value[to * rows : to * rows + rows]
            second = value[BLK + to * rows : BLK + to * rows + rows]
            out[to, :, at] = jnp.concatenate([first, second], axis=0).astype(half)


def forward(pieces, gain, gate_w, up_w, down_w, order, other):
    width, hidden = gate_w.shape
    n_mp = pieces.shape[0]
    rows = 2 * BLK
    whole = pl.BlockSpec(memory_space=pltpu.VMEM)
    return pl.pallas_call(
        forward_kernel,
        in_specs=[whole, whole] + [pl.BlockSpec(memory_space=pl.ANY)] * 2
        + [pl.BlockSpec(memory_space=pltpu.HBM)] * 3,
        out_specs=[whole] * 4,
        out_shape=[
            jax.ShapeDtypeStruct((rows, width), half),
            jax.ShapeDtypeStruct((rows, hidden), full),
            jax.ShapeDtypeStruct((rows, hidden), full),
            jax.ShapeDtypeStruct((n_mp, rows // n_mp, width), half),
        ],
        scratch_shapes=[
            pltpu.VMEM((rows, width), half),
            pltpu.VMEM((rows, hidden), half),
            pltpu.VMEM((3, width, hidden), half),
            pltpu.SemaphoreType.DMA((9,)),
        ],
        compiler_params=pltpu.CompilerParams(vmem_limit_bytes=56 * 1024 * 1024),
        cost_estimate=pl.CostEstimate(
            flops=6 * rows * width * hidden,
            bytes_accessed=6 * width * hidden + 10 * rows * width,
            transcendentals=rows * hidden,
        ),
    )(pieces, gain[None], order, other, gate_w, up_w, down_w)


def slope_kernel(terms, dy, state, gain, order, out):
    del order
    rows, width = dy.shape
    cols = out.shape[2]
    wide = state[...].astype(full)
    inverse = lax.rsqrt(jnp.mean(wide * wide, axis=1, keepdims=True) + epsilon)
    dn = terms[0].astype(full)
    for source in range(1, terms.shape[0]):
        dn = dn + terms[source].astype(full)
    gained = gain[...] * dn
    mean = jnp.mean(gained * wide, axis=1, keepdims=True)
    dx = dy[...].astype(full) + inverse * gained - wide * (inverse * inverse * inverse) * mean
    for group in range(out.shape[0]):
        out[group] = dx[:, group * cols : (group + 1) * cols].astype(out.dtype)


def slope(terms, dy, state, gain, groups, order):
    rows, width = dy.shape
    whole = pl.BlockSpec(memory_space=pltpu.VMEM)
    return pl.pallas_call(
        slope_kernel,
        in_specs=[whole] * 4 + [pl.BlockSpec(memory_space=pl.ANY)],
        out_specs=whole,
        out_shape=jax.ShapeDtypeStruct((groups, rows, width // groups), half),
        compiler_params=pltpu.CompilerParams(vmem_limit_bytes=16 * 1024 * 1024),
        cost_estimate=pl.CostEstimate(
            flops=30 * rows * width, bytes_accessed=40 * rows * width, transcendentals=rows
        ),
    )(terms, dy, state, gain[None], order)


def on_device(
    attention,
    out_proj,
    residual,
    final_gain,
    adapter_weight,
    token_slot,
    block_owner,
    student_hidden,
    cotangent,
    student_gain,
    gate_weight,
    up_weight,
    down_weight,
):
    tokens, width_here = attention.shape
    width_full = out_proj.shape[1]
    student_width = adapter_weight.shape[1]
    blocks = tokens // BLK
    n_mp = lax.axis_size("mp")
    n_dp = lax.axis_size("dp")
    dp = lax.axis_index("dp")
    mp = lax.axis_index("mp")
    slots = student_hidden.shape[2]
    rows = BLK // n_mp
    groups = n_mp // blocks
    cols = student_width // groups
    out_cols = student_width // n_dp
    mine_rows = blocks * rows

    ids = jnp.arange(block_owner.shape[0], dtype=jnp.int32)
    my_ids = dp * blocks + jnp.arange(blocks, dtype=jnp.int32)
    my_owner = take(block_owner, (dp * blocks,), (blocks,))
    my_slot = jnp.sum(
        (block_owner[None, :] == my_owner[:, None]) & (ids[None, :] < my_ids[:, None]),
        axis=1,
        dtype=jnp.int32,
    )

    both = jnp.concatenate([student_hidden[0], cotangent[0]], axis=1)
    everyone = lax.all_gather(both, "dp", axis=0, tiled=False)

    def fetch(offset):
        picked = []
        for k in range(blocks):
            at = (my_owner[k], 0, my_slot[k] + offset, 0)
            picked.append(
                take(everyone, at, (1, rows, 1, student_width)).reshape(rows, student_width)
            )
        return jnp.stack(picked)

    sh_rows = fetch(0)
    dy_rows = fetch(student_hidden.shape[2])
    dy = lax.all_gather(dy_rows, "mp", axis=0, tiled=False)

    hidden = residual.astype(full) + jnp.concatenate(
        [total(v) for v in teacher_terms(attention, out_proj, mp, (sh_rows, dy_rows))], axis=0
    )
    squares = jnp.sum(hidden * hidden, axis=1)
    gained_hidden = hidden * final_gain
    parts = jnp.einsum(
        "ktd,dce->kcte",
        gained_hidden.astype(half).reshape(blocks, BLK, width_here),
        adapter_weight.reshape(width_here, groups, cols),
        preferred_element_type=full,
    ).astype(half)
    sh_parts = jnp.swapaxes(sh_rows.reshape(blocks, rows, groups, cols), 1, 2)
    sq_parts = jnp.zeros((8, cols), half).at[:3, :tokens].set(three_parts(squares))
    message = jnp.concatenate(
        [
            parts,
            sh_parts,
            jnp.broadcast_to(sq_parts[None, None], (blocks, groups) + sq_parts.shape),
        ],
        axis=2,
    )
    message = exchange(message.reshape(n_mp, BLK + rows + 8, cols), "mp")
    states, inverse_rms = pool(message, token_slot, mp // groups, width_full)
    states = exchange(states, "mp")

    slots_block = token_slot.reshape(blocks, BLK)
    onehot = slots_block[:, None, :] == jnp.arange(BLK, dtype=jnp.int32)[None, :, None]
    counts = jnp.maximum(jnp.sum(onehot.astype(full), axis=2), 1.0)
    onehot = onehot.astype(half)
    normed = (gained_hidden * inverse_rms.reshape(tokens, 1)).astype(half).reshape(blocks, BLK, width_here)
    pooled = jnp.einsum("krt,ktd->krd", onehot, normed, preferred_element_type=full)
    pooled = (pooled / counts[:, :, None]).astype(half)
    pooled_all = lax.all_gather(pooled.reshape(n_mp, mine_rows, width_here), "dp", axis=0, tiled=False)
    pooled_all = jnp.swapaxes(pooled_all, 0, 1).reshape(n_dp * tokens, width_here)

    state, gate, up, output = forward(
        states, student_gain, gate_weight, up_weight, down_weight, pooled, dy[0, 0, :, :128]
    )
    grad_gate, grad_up = backward(dy.reshape(tokens, student_width), down_weight, gate, up, output)
    dn = (times_rows(grad_gate, gate_weight) + times_rows(grad_up, up_weight)).astype(half)
    output = exchange(output, "mp")
    dn, output = lax.optimization_barrier((dn, output))
    dn = exchange(dn.reshape(n_mp, mine_rows, student_width), "mp")
    here = mp * mine_rows
    state_rows = take(
        state.reshape(blocks, BLK, student_width),
        (0, mp * rows, 0),
        (blocks, rows, student_width),
    )
    out_rows = home(output, state_rows.reshape(mine_rows, student_width))
    dproj = slope(
        dn,
        take(
            dy, ((mp % groups) * blocks, mp // groups, 0, 0), (blocks, 1, rows, student_width)
        ).reshape(mine_rows, student_width),
        take(state, (here, 0), (mine_rows, student_width)),
        student_gain,
        n_dp,
        out_rows,
    )
    dproj = exchange(spread(exchange(dproj, "dp"), n_mp), "mp")
    adapter_grad = lax.dot_general(
        pooled_all,
        dproj.reshape(n_dp * tokens, out_cols),
        (((0,), (0,)), ((), ())),
        preferred_element_type=full,
    )

    back = lax.all_gather(out_rows, "dp", axis=0, tiled=False)
    before = (block_owner[None, :] == block_owner[:, None]) & (ids[None, :] < ids[:, None])
    ranks = jnp.sum(before, axis=1, dtype=jnp.int32)
    mine = block_owner == dp
    picks = []
    for slot in range(slots):
        chosen = mine & (ranks == slot)
        index = jnp.sum(jnp.where(chosen, ids, 0))
        at = (index // blocks, (index % blocks) * rows, 0)
        piece = take(back, at, (1, rows, student_width))[0]
        picks.append(jnp.where(jnp.any(chosen), piece, jnp.zeros((), half)))
    student_out = jnp.stack(picks, axis=1)
    return (student_out[None], adapter_grad)


def solution(mesh):
    return jax.shard_map(
        on_device,
        mesh=mesh,
        in_specs=(
            P("dp", "mp"),
            P("mp", None),
            P("dp", "mp"),
            P("mp"),
            P("mp", None),
            P("dp"),
            P(),
            P("dp", "mp", None, None),
            P("dp", "mp", None, None),
            P(),
            P(None, "mp"),
            P(None, "mp"),
            P(None, "mp"),
        ),
        out_specs=(P("dp", "mp", None, None), P("mp", "dp")),
        check_vma=False,
    )
```

```python
import jax
import jax.numpy as jnp
from jax import lax
from jax.experimental import pallas as pl
from jax.experimental.pallas import tpu as pltpu
from jax.sharding import PartitionSpec as P

BLK = 128
epsilon = 1e-06
half = jnp.bfloat16
full = jnp.float32


def exchange(pieces, axis):
    return lax.all_to_all(pieces, axis, split_axis=0, concat_axis=0, tiled=True)


def take(array, starts, sizes):
    return lax.dynamic_slice(array, starts, sizes, allow_negative_indices=False)


def three_parts(value):
    first = lax.reduce_precision(value, 8, 7)
    rest = value - first
    second = lax.reduce_precision(rest, 8, 7)
    return jnp.stack([first, second, rest - second]).astype(half)


def times_rows(left, right):
    return lax.dot_general(left, right, (((1,), (1,)), ((), ())), preferred_element_type=full)


SIDE = 4


def step(value, along_y, along_z):
    pairs = []
    for y in range(SIDE):
        for z in range(SIDE):
            to = ((y + along_y) % SIDE) * SIDE + (z + along_z) % SIDE
            pairs.append((y * SIDE + z, to))
    return lax.ppermute(value, "mp", pairs)


def far_kernel(place, left, right, lower0, upper0, lower1, upper1, held, sems):
    width = held.shape[2]
    y, z = lax.rem(place[0] + 2, SIDE), lax.rem(place[1] + 2, SIDE)
    middle = BLK // 2
    loads = []
    for index in range(2 * SIDE):
        piece = y * SIDE + index if index < SIDE else (index - SIDE) * SIDE + z
        columns = pl.ds(pl.multiple_of(piece * width, width), width)
        load = pltpu.make_async_copy(right.at[:, columns], held.at[index], sems.at[index])
        load.start()
        loads.append(load)
    for index in range(2 * SIDE):
        loads[index].wait()
        block, at = index // SIDE, index % SIDE
        value = jnp.dot(
            left[pl.ds(block * BLK, BLK), :], held[index], preferred_element_type=full
        ).astype(half)
        lower, upper = (lower0, upper0) if block == 0 else (lower1, upper1)
        lower[at] = value[:middle]
        upper[at] = value[middle:]


def near_kernel(place, left, right, kept0, up0, down0, kept1, up1, down1, held, sems):
    outs = {0: (kept0, kept1), 1: (up0, up1), 3: (down0, down1)}
    width = held.shape[2]
    y, z = place[0], place[1]

    def load(index):
        piece = lax.rem(y + index // SIDE, SIDE) * SIDE + lax.rem(index, SIDE)
        columns = pl.ds(pl.multiple_of(piece * width, width), width)
        return pltpu.make_async_copy(right.at[:, columns], held.at[index], sems.at[index])

    for index in range(SIDE * SIDE):
        load(index).start()

    @pl.loop(0, SIDE * SIDE)
    def _(index):
        load(index).wait()
        value = jnp.dot(left[...], held[index], preferred_element_type=full).astype(half)
        along_y, at_z = index // SIDE, lax.rem(index, SIDE)
        at_y, along_z = lax.rem(y + along_y, SIDE), lax.rem(at_z - z + SIDE, SIDE)
        for distance, (first, second) in outs.items():

            @pl.when(along_y == distance)
            def _():
                first[at_z] = value[:BLK]

            @pl.when(along_z == distance)
            def _():
                second[at_y] = value[BLK:]


def merge_kernel(*refs):
    ins, outs = refs[:8], refs[8:]
    middle = BLK // 2
    for block in (0, 1):
        up, down, lower, upper = ins[4 * block : 4 * block + 4]
        to_up, to_down = outs[2 * block], outs[2 * block + 1]
        to_up[0, :middle] = (up[0, :middle].astype(full) + lower[0].astype(full)).astype(half)
        to_up[0, middle:] = up[0, middle:]
        to_down[0, :middle] = down[0, :middle]
        to_down[0, middle:] = (down[0, middle:].astype(full) + upper[0].astype(full)).astype(half)


def gather_kernel(place, *refs):
    ins, outs = refs[:6], refs[7:]
    for block in (0, 1):
        kept, from_down, from_up = ins[3 * block : 3 * block + 3]
        here = place[1 - block]
        for distance in range(SIDE):
            at = lax.rem(here + distance, SIDE)
            value = kept[at].astype(full) + from_down[at].astype(full) + from_up[at].astype(full)
            out = outs[SIDE * block + distance]
            out[...] = value.astype(out.dtype)


def teacher_terms(attention, out_proj, mp, order):
    width = attention.shape[1]
    whole = pl.BlockSpec(memory_space=pltpu.VMEM)
    scalars = pl.BlockSpec(memory_space=pltpu.SMEM)
    anywhere = pl.BlockSpec(memory_space=pl.ANY)
    limit = pltpu.CompilerParams(vmem_limit_bytes=40 * 1024 * 1024)
    place = jnp.stack([mp // SIDE, mp % SIDE]).astype(jnp.int32)
    full_piece = jax.ShapeDtypeStruct((SIDE, BLK, width), half)
    half_piece = jax.ShapeDtypeStruct((SIDE, BLK // 2, width), half)
    moves = full_piece.size
    one_piece = pl.BlockSpec((1, BLK, width), lambda i: (i, 0, 0))
    one_half = pl.BlockSpec((1, BLK // 2, width), lambda i: (i, 0, 0))

    def terms(kernel, pieces, count, blocks):
        return pl.pallas_call(
            kernel,
            in_specs=[scalars, whole, pl.BlockSpec(memory_space=pltpu.HBM)],
            out_specs=[whole] * len(pieces),
            out_shape=pieces,
            scratch_shapes=[
                pltpu.VMEM((count, width, width), half),
                pltpu.SemaphoreType.DMA((count,)),
            ],
            compiler_params=pltpu.CompilerParams(vmem_limit_bytes=48 * 1024 * 1024),
            cost_estimate=pl.CostEstimate(
                flops=2 * blocks * BLK * count * width * width,
                bytes_accessed=2 * count * width * width,
                transcendentals=0,
            ),
        )(place, attention, out_proj)

    lower0, upper0, lower1, upper1 = terms(far_kernel, [half_piece] * 4, 2 * SIDE, 1)
    kept0, up0, down0, kept1, up1, down1 = terms(near_kernel, [full_piece] * 6, SIDE * SIDE, 2)
    lower0, upper0 = step(lower0, 1, 0), step(upper0, -1, 0)
    lower1, upper1 = step(lower1, 0, 1), step(upper1, 0, -1)
    up0, down0, up1, down1 = pl.pallas_call(
        merge_kernel,
        grid=(SIDE,),
        in_specs=[one_piece, one_piece, one_half, one_half] * 2,
        out_specs=[one_piece] * 4,
        out_shape=[full_piece] * 4,
        compiler_params=limit,
        cost_estimate=pl.CostEstimate(
            flops=4 * moves, bytes_accessed=20 * moves, transcendentals=0
        ),
    )(up0, down0, lower0, upper0, up1, down1, lower1, upper1)
    from_down0, from_up0 = step(up0, 1, 0), step(down0, -1, 0)
    from_down1, from_up1 = step(up1, 0, 1), step(down1, 0, -1)
    sums = pl.pallas_call(
        gather_kernel,
        in_specs=[scalars] + [whole] * 6 + [anywhere],
        out_specs=[whole] * (2 * SIDE),
        out_shape=[
            jax.ShapeDtypeStruct((BLK, width), half if distance else full)
            for block in (0, 1)
            for distance in range(SIDE)
        ],
        compiler_params=limit,
        cost_estimate=pl.CostEstimate(
            flops=4 * moves, bytes_accessed=16 * moves, transcendentals=0
        ),
    )(place, kept0, from_down0, from_up0, kept1, from_down1, from_up1, *order)
    results = []
    for block in (0, 1):
        mine = sums[SIDE * block : SIDE * block + SIDE]
        arrived = [
            step(mine[d], 0, d) if block == 0 else step(mine[d], d, 0) for d in range(1, SIDE)
        ]
        results.append([mine[0]] + arrived)
    return results


def total(values):
    result = values[0].astype(full)
    for value in values[1:]:
        result = result + value.astype(full)
    return result


def backward_kernel(dy, down, gate, up, order, grad_gate, grad_up, dh):
    del order
    rows = 8
    for chunk in range(2):
        columns = pl.ds(chunk * (down.shape[1] // 2), down.shape[1] // 2)
        value = jnp.dot(dy[...], down[:, columns], preferred_element_type=full)
        for index in range(value.shape[0] // rows):
            to = (index % 2) * BLK + (index // 2) * rows
            dh[pl.ds(to, rows), columns] = value[index * rows : index * rows + rows]
    gate_val = gate[...]
    sigma = jax.nn.sigmoid(gate_val)
    grad_gate[...] = (dh[...] * up[...] * sigma * (1.0 + gate_val * (1.0 - sigma))).astype(half)
    grad_up[...] = (dh[...] * (gate_val * sigma)).astype(half)


def backward(dy, down, gate, up, order):
    whole = pl.BlockSpec(memory_space=pltpu.VMEM)
    shape = jax.ShapeDtypeStruct(gate.shape, half)
    return pl.pallas_call(
        backward_kernel,
        in_specs=[whole] * 4 + [pl.BlockSpec(memory_space=pl.ANY)],
        out_specs=[whole, whole],
        out_shape=[shape, shape],
        scratch_shapes=[pltpu.VMEM(gate.shape, full)],
        compiler_params=pltpu.CompilerParams(vmem_limit_bytes=56 * 1024 * 1024),
        cost_estimate=pl.CostEstimate(
            flops=2 * dy.shape[0] * down.size,
            bytes_accessed=2 * (down.size + dy.size) + 16 * gate.size,
            transcendentals=gate.size,
        ),
    )(dy, down, gate, up, order)


def spread_kernel(piece, out, sems):
    copies = [
        pltpu.make_async_copy(piece, out.at[to], sems.at[to]) for to in range(out.shape[0])
    ]
    for copy in copies:
        copy.start()
    for copy in copies:
        copy.wait()


def spread(piece, count):
    whole = pl.BlockSpec(memory_space=pltpu.VMEM)
    return pl.pallas_call(
        spread_kernel,
        in_specs=[whole],
        out_specs=pl.BlockSpec(memory_space=pltpu.HBM),
        scratch_shapes=[pltpu.SemaphoreType.DMA((count,))],
        out_shape=jax.ShapeDtypeStruct((count,) + piece.shape, piece.dtype),
        compiler_params=pltpu.CompilerParams(vmem_limit_bytes=16 * 1024 * 1024),
        cost_estimate=pl.CostEstimate(
            flops=0, bytes_accessed=4 * count * piece.size, transcendentals=0
        ),
    )(piece)


def home_kernel(terms, state, out):
    value = state[...].astype(full)
    for source in range(terms.shape[0]):
        value = value + terms[source].astype(full)
    rows = state.shape[0]
    out[pl.ds(0, rows), :] = value.astype(half)
    out[pl.ds(rows, rows), :] = jnp.zeros(state.shape, half)


def home(terms, state):
    rows, width = state.shape
    whole = pl.BlockSpec(memory_space=pltpu.VMEM)
    return pl.pallas_call(
        home_kernel,
        in_specs=[whole, whole],
        out_specs=whole,
        out_shape=jax.ShapeDtypeStruct((2 * rows, width), half),
        compiler_params=pltpu.CompilerParams(vmem_limit_bytes=16 * 1024 * 1024),
        cost_estimate=pl.CostEstimate(
            flops=17 * rows * width, bytes_accessed=40 * rows * width, transcendentals=0
        ),
    )(terms, state)


def pool_kernel(place, message, token_slot, out, inverse, sh, weights, state, sems):
    sources, _, cols = message.shape
    rows = BLK // sources
    token_proj = message[0, :BLK].astype(full)
    for source in range(1, sources):
        token_proj = token_proj + message[source, :BLK].astype(full)
    squares = jnp.zeros((rows, cols), full)
    for source in range(sources):
        tail = message[source, BLK:].astype(full)
        sh[pl.ds(source * rows, rows), :] = tail[:rows]
        squares = squares + tail[rows:]
    tokens = token_slot.shape[1]
    squares = jnp.sum(squares, axis=0, keepdims=True)[:, :tokens]
    inverse[...] = lax.rsqrt(squares / place[1].astype(full) + epsilon)
    slots = jnp.where(place[0] == 0, token_slot[:, :BLK], token_slot[:, BLK:])
    scale = jnp.where(place[0] == 0, inverse[:, :BLK], inverse[:, BLK:])
    hits = slots == lax.broadcasted_iota(jnp.int32, (BLK, BLK), 0)
    counts = jnp.maximum(jnp.sum(hits.astype(full), axis=1, keepdims=True), 1.0)
    weights[...] = jnp.where(hits, scale, 0.0)
    first = weights[...].astype(half)
    second = (weights[...] - lax.reduce_precision(weights[...], 8, 7)).astype(half)
    token_proj = token_proj.astype(half)
    placed = jnp.dot(first, token_proj, preferred_element_type=full)
    placed = placed + jnp.dot(second, token_proj, preferred_element_type=full)
    placed = (placed / counts).astype(half).astype(full)
    state[...] = (sh[...] + placed).astype(half)
    copies = [
        pltpu.make_async_copy(state, out.at[to], sems.at[to]) for to in range(sources)
    ]
    for copy in copies:
        copy.start()
    for copy in copies:
        copy.wait()


def pool(message, token_slot, block, width_full):
    sources, _, cols = message.shape
    whole = pl.BlockSpec(memory_space=pltpu.VMEM)
    tokens = token_slot.shape[0]
    place = jnp.stack([block, jnp.full_like(block, width_full)]).astype(jnp.int32)
    return pl.pallas_call(
        pool_kernel,
        in_specs=[pl.BlockSpec(memory_space=pltpu.SMEM), whole, whole],
        out_specs=[pl.BlockSpec(memory_space=pltpu.HBM), whole],
        out_shape=[
            jax.ShapeDtypeStruct((sources, BLK, cols), half),
            jax.ShapeDtypeStruct((1, tokens), full),
        ],
        scratch_shapes=[
            pltpu.VMEM((BLK, cols), full),
            pltpu.VMEM((BLK, BLK), full),
            pltpu.VMEM((BLK, cols), half),
            pltpu.SemaphoreType.DMA((sources,)),
        ],
        compiler_params=pltpu.CompilerParams(vmem_limit_bytes=40 * 1024 * 1024),
        cost_estimate=pl.CostEstimate(
            flops=6 * message.size, bytes_accessed=4 * message.size, transcendentals=tokens
        ),
    )(place, message, token_slot[None])


def forward_kernel(
    pieces, gain, order, gate_hbm, up_hbm, down_hbm, state, gate, up, out, normed, act, held, sems
):
    del order
    parts = 3
    part = gate_hbm.shape[0] // parts

    def load(which, source, third):
        at = pl.ds(third * part, part)
        return pltpu.make_async_copy(
            source.at[at], held.at[which, at], sems.at[parts * which + third]
        )

    for third in range(parts):
        load(0, gate_hbm, third).start()
        load(1, up_hbm, third).start()
    cols = pieces.shape[2]
    groups = state.shape[1] // cols
    for block in range(state.shape[0] // BLK):
        rows = pl.ds(block * BLK, BLK)
        squares = jnp.zeros((BLK, 128), full)
        for group in range(groups):
            value = pieces[block * groups + group]
            state[rows, pl.ds(group * cols, cols)] = value
            wide = value.astype(full)
            wide = wide * wide
            for lane in range(0, cols, 128):
                squares = squares + wide[:, lane : lane + 128]
        mean = jnp.sum(squares, axis=1, keepdims=True) / state.shape[1]
        inverse = lax.rsqrt(mean + epsilon)
        for group in range(groups):
            at = pl.ds(group * cols, cols)
            wide = pieces[block * groups + group].astype(full)
            normed[rows, at] = (wide * inverse * gain[:, at]).astype(normed.dtype)
    half_hidden = gate.shape[1] // 2
    for third in range(parts):
        load(0, gate_hbm, third).wait()
        load(1, up_hbm, third).wait()
        load(2, down_hbm, third).start()
        depth = pl.ds(third * part, part)
        for index in range(2):
            at = pl.ds(index * half_hidden, half_hidden)
            for which, total_ref in ((0, gate), (1, up)):
                value = jnp.dot(
                    normed[:, depth], held[which, depth, at], preferred_element_type=full
                )
                total_ref[:, at] = value if third == 0 else total_ref[:, at] + value
    gate_val = gate[...]
    act[...] = (gate_val * jax.nn.sigmoid(gate_val) * up[...]).astype(half)
    for third in range(parts):
        load(2, down_hbm, third).wait()
    down_w = held.at[2]
    rows = out.shape[1] // 2
    wide_chunk = 512

    @pl.loop(0, state.shape[1] // wide_chunk)
    def _(index):
        at = pl.ds(pl.multiple_of(index * wide_chunk, wide_chunk), wide_chunk)
        value = times_rows(act[...], down_w[at, :])
        for to in range(out.shape[0]):
            first = value[to * rows : to * rows + rows]
            second = value[BLK + to * rows : BLK + to * rows + rows]
            out[to, :, at] = jnp.concatenate([first, second], axis=0).astype(half)


def forward(pieces, gain, gate_w, up_w, down_w, order):
    width, hidden = gate_w.shape
    n_mp = pieces.shape[0]
    rows = 2 * BLK
    whole = pl.BlockSpec(memory_space=pltpu.VMEM)
    return pl.pallas_call(
        forward_kernel,
        in_specs=[whole, whole, pl.BlockSpec(memory_space=pl.ANY)]
        + [pl.BlockSpec(memory_space=pltpu.HBM)] * 3,
        out_specs=[whole] * 4,
        out_shape=[
            jax.ShapeDtypeStruct((rows, width), half),
            jax.ShapeDtypeStruct((rows, hidden), full),
            jax.ShapeDtypeStruct((rows, hidden), full),
            jax.ShapeDtypeStruct((n_mp, rows // n_mp, width), half),
        ],
        scratch_shapes=[
            pltpu.VMEM((rows, width), half),
            pltpu.VMEM((rows, hidden), half),
            pltpu.VMEM((3, width, hidden), half),
            pltpu.SemaphoreType.DMA((9,)),
        ],
        compiler_params=pltpu.CompilerParams(vmem_limit_bytes=56 * 1024 * 1024),
        cost_estimate=pl.CostEstimate(
            flops=6 * rows * width * hidden,
            bytes_accessed=6 * width * hidden + 10 * rows * width,
            transcendentals=rows * hidden,
        ),
    )(pieces, gain[None], order, gate_w, up_w, down_w)


def slope_kernel(terms, dy, state, gain, order, out):
    del order
    rows, width = dy.shape
    cols = out.shape[2]
    wide = state[...].astype(full)
    inverse = lax.rsqrt(jnp.mean(wide * wide, axis=1, keepdims=True) + epsilon)
    dn = terms[0].astype(full)
    for source in range(1, terms.shape[0]):
        dn = dn + terms[source].astype(full)
    gained = gain[...] * dn
    mean = jnp.mean(gained * wide, axis=1, keepdims=True)
    dx = dy[...].astype(full) + inverse * gained - wide * (inverse * inverse * inverse) * mean
    for group in range(out.shape[0]):
        out[group] = dx[:, group * cols : (group + 1) * cols].astype(out.dtype)


def slope(terms, dy, state, gain, groups, order):
    rows, width = dy.shape
    whole = pl.BlockSpec(memory_space=pltpu.VMEM)
    return pl.pallas_call(
        slope_kernel,
        in_specs=[whole] * 4 + [pl.BlockSpec(memory_space=pl.ANY)],
        out_specs=whole,
        out_shape=jax.ShapeDtypeStruct((groups, rows, width // groups), half),
        compiler_params=pltpu.CompilerParams(vmem_limit_bytes=16 * 1024 * 1024),
        cost_estimate=pl.CostEstimate(
            flops=30 * rows * width, bytes_accessed=40 * rows * width, transcendentals=rows
        ),
    )(terms, dy, state, gain[None], order)


def on_device(
    attention,
    out_proj,
    residual,
    final_gain,
    adapter_weight,
    token_slot,
    block_owner,
    student_hidden,
    cotangent,
    student_gain,
    gate_weight,
    up_weight,
    down_weight,
):
    tokens, width_here = attention.shape
    width_full = out_proj.shape[1]
    student_width = adapter_weight.shape[1]
    blocks = tokens // BLK
    n_mp = lax.axis_size("mp")
    n_dp = lax.axis_size("dp")
    dp = lax.axis_index("dp")
    mp = lax.axis_index("mp")
    slots = student_hidden.shape[2]
    rows = BLK // n_mp
    groups = n_mp // blocks
    cols = student_width // groups
    out_cols = student_width // n_dp
    mine_rows = blocks * rows

    ids = jnp.arange(block_owner.shape[0], dtype=jnp.int32)
    my_ids = dp * blocks + jnp.arange(blocks, dtype=jnp.int32)
    my_owner = take(block_owner, (dp * blocks,), (blocks,))
    my_slot = jnp.sum(
        (block_owner[None, :] == my_owner[:, None]) & (ids[None, :] < my_ids[:, None]),
        axis=1,
        dtype=jnp.int32,
    )

    def fetch(array):
        everyone = lax.all_gather(array[0], "dp", axis=0, tiled=False)
        picked = []
        for k in range(blocks):
            at = (my_owner[k], 0, my_slot[k], 0)
            piece = take(everyone, at, (1, rows, 1, student_width))
            picked.append(piece.reshape(rows, student_width))
        return jnp.stack(picked)

    sh_rows = fetch(student_hidden)
    dy_rows = fetch(cotangent)
    dy = lax.all_gather(dy_rows, "mp", axis=0, tiled=False)

    hidden = residual.astype(full) + jnp.concatenate(
        [total(v) for v in teacher_terms(attention, out_proj, mp, (sh_rows,))], axis=0
    )
    squares = jnp.sum(hidden * hidden, axis=1)
    gained_hidden = hidden * final_gain
    parts = jnp.einsum(
        "ktd,dce->kcte",
        gained_hidden.astype(half).reshape(blocks, BLK, width_here),
        adapter_weight.reshape(width_here, groups, cols),
        preferred_element_type=full,
    ).astype(half)
    sh_parts = jnp.swapaxes(sh_rows.reshape(blocks, rows, groups, cols), 1, 2)
    sq_parts = jnp.zeros((8, cols), half).at[:3, :tokens].set(three_parts(squares))
    message = jnp.concatenate(
        [
            parts,
            sh_parts,
            jnp.broadcast_to(sq_parts[None, None], (blocks, groups) + sq_parts.shape),
        ],
        axis=2,
    )
    message = exchange(message.reshape(n_mp, BLK + rows + 8, cols), "mp")
    states, inverse_rms = pool(message, token_slot, mp // groups, width_full)
    states = exchange(states, "mp")

    slots_block = token_slot.reshape(blocks, BLK)
    onehot = slots_block[:, None, :] == jnp.arange(BLK, dtype=jnp.int32)[None, :, None]
    counts = jnp.maximum(jnp.sum(onehot.astype(full), axis=2), 1.0)
    onehot = onehot.astype(half)
    normed = (gained_hidden * inverse_rms.reshape(tokens, 1)).astype(half).reshape(blocks, BLK, width_here)
    pooled = jnp.einsum("krt,ktd->krd", onehot, normed, preferred_element_type=full)
    pooled = (pooled / counts[:, :, None]).astype(half)
    pooled_all = lax.all_gather(pooled.reshape(n_mp, mine_rows, width_here), "dp", axis=0, tiled=False)
    pooled_all = jnp.swapaxes(pooled_all, 0, 1).reshape(n_dp * tokens, width_here)

    state, gate, up, output = forward(
        states, student_gain, gate_weight, up_weight, down_weight, pooled
    )
    grad_gate, grad_up = backward(dy.reshape(tokens, student_width), down_weight, gate, up, output)
    dn = (times_rows(grad_gate, gate_weight) + times_rows(grad_up, up_weight)).astype(half)
    output = exchange(output, "mp")
    dn, output = lax.optimization_barrier((dn, output))
    dn = exchange(dn.reshape(n_mp, mine_rows, student_width), "mp")
    here = mp * mine_rows
    state_rows = take(
        state.reshape(blocks, BLK, student_width),
        (0, mp * rows, 0),
        (blocks, rows, student_width),
    )
    out_rows = home(output, state_rows.reshape(mine_rows, student_width))
    dproj = slope(
        dn,
        take(
            dy, ((mp % groups) * blocks, mp // groups, 0, 0), (blocks, 1, rows, student_width)
        ).reshape(mine_rows, student_width),
        take(state, (here, 0), (mine_rows, student_width)),
        student_gain,
        n_dp,
        out_rows,
    )
    dproj = exchange(spread(exchange(dproj, "dp"), n_mp), "mp")
    adapter_grad = lax.dot_general(
        pooled_all,
        dproj.reshape(n_dp * tokens, out_cols),
        (((0,), (0,)), ((), ())),
        preferred_element_type=full,
    )

    back = lax.all_gather(out_rows, "dp", axis=0, tiled=False)
    before = (block_owner[None, :] == block_owner[:, None]) & (ids[None, :] < ids[:, None])
    ranks = jnp.sum(before, axis=1, dtype=jnp.int32)
    mine = block_owner == dp
    picks = []
    for slot in range(slots):
        chosen = mine & (ranks == slot)
        index = jnp.sum(jnp.where(chosen, ids, 0))
        at = (index // blocks, (index % blocks) * rows, 0)
        piece = take(back, at, (1, rows, student_width))[0]
        picks.append(jnp.where(jnp.any(chosen), piece, jnp.zeros((), half)))
    student_out = jnp.stack(picks, axis=1)
    return (student_out[None], adapter_grad)


def solution(mesh):
    return jax.shard_map(
        on_device,
        mesh=mesh,
        in_specs=(
            P("dp", "mp"),
            P("mp", None),
            P("dp", "mp"),
            P("mp"),
            P("mp", None),
            P("dp"),
            P(),
            P("dp", "mp", None, None),
            P("dp", "mp", None, None),
            P(),
            P(None, "mp"),
            P(None, "mp"),
            P(None, "mp"),
        ),
        out_specs=(P("dp", "mp", None, None), P("mp", "dp")),
        check_vma=False,
    )
```

```python
import jax
import jax.numpy as jnp
from jax import lax
from jax.experimental import pallas as pl
from jax.experimental.pallas import tpu as pltpu
from jax.sharding import PartitionSpec as P

BLK = 128
epsilon = 1e-06
half = jnp.bfloat16
full = jnp.float32


def exchange(pieces, axis):
    return lax.all_to_all(pieces, axis, split_axis=0, concat_axis=0, tiled=True)


def take(array, starts, sizes):
    return lax.dynamic_slice(array, starts, sizes, allow_negative_indices=False)


def three_parts(value):
    first = lax.reduce_precision(value, 8, 7)
    rest = value - first
    second = lax.reduce_precision(rest, 8, 7)
    return jnp.stack([first, second, rest - second]).astype(half)


def times_rows(left, right):
    return lax.dot_general(left, right, (((1,), (1,)), ((), ())), preferred_element_type=full)


SIDE = 4


def partner(value):
    return lax.ppermute(value, "dp", [(d, d ^ 1) for d in range(lax.axis_size("dp"))])


def step(value, along_y, along_z):
    pairs = []
    for y in range(SIDE):
        for z in range(SIDE):
            to = ((y + along_y) % SIDE) * SIDE + (z + along_z) % SIDE
            pairs.append((y * SIDE + z, to))
    return lax.ppermute(value, "mp", pairs)


def far_kernel(place, left, right, lower0, upper0, lower1, upper1, held, sems):
    width = held.shape[2]
    y, z = lax.rem(place[0] + 2, SIDE), lax.rem(place[1] + 2, SIDE)
    middle = BLK // 2
    loads = []
    for index in range(2 * SIDE):
        piece = y * SIDE + index if index < SIDE else (index - SIDE) * SIDE + z
        columns = pl.ds(pl.multiple_of(piece * width, width), width)
        load = pltpu.make_async_copy(right.at[:, columns], held.at[index], sems.at[index])
        load.start()
        loads.append(load)
    for index in range(2 * SIDE):
        loads[index].wait()
        block, at = index // SIDE, index % SIDE
        value = jnp.dot(
            left[pl.ds(block * BLK, BLK), :], held[index], preferred_element_type=full
        ).astype(half)
        lower, upper = (lower0, upper0) if block == 0 else (lower1, upper1)
        lower[at] = value[:middle]
        upper[at] = value[middle:]


def near_kernel(place, left, right, kept0, up0, down0, kept1, up1, down1, held, sems):
    outs = {0: (kept0, kept1), 1: (up0, up1), 3: (down0, down1)}
    width = held.shape[2]
    y, z = place[0], place[1]

    def load(index):
        piece = lax.rem(y + index // SIDE, SIDE) * SIDE + lax.rem(index, SIDE)
        columns = pl.ds(pl.multiple_of(piece * width, width), width)
        return pltpu.make_async_copy(right.at[:, columns], held.at[index], sems.at[index])

    for index in range(SIDE * SIDE):
        load(index).start()

    @pl.loop(0, SIDE * SIDE)
    def _(index):
        load(index).wait()
        value = jnp.dot(left[...], held[index], preferred_element_type=full).astype(half)
        along_y, at_z = index // SIDE, lax.rem(index, SIDE)
        at_y, along_z = lax.rem(y + along_y, SIDE), lax.rem(at_z - z + SIDE, SIDE)
        for distance, (first, second) in outs.items():

            @pl.when(along_y == distance)
            def _():
                first[at_z] = value[:BLK]

            @pl.when(along_z == distance)
            def _():
                second[at_y] = value[BLK:]


def merge_kernel(*refs):
    ins, outs = refs[:8], refs[8:]
    middle = BLK // 2
    for block in (0, 1):
        up, down, lower, upper = ins[4 * block : 4 * block + 4]
        to_up, to_down = outs[2 * block], outs[2 * block + 1]
        to_up[0, :middle] = (up[0, :middle].astype(full) + lower[0].astype(full)).astype(half)
        to_up[0, middle:] = up[0, middle:]
        to_down[0, :middle] = down[0, :middle]
        to_down[0, middle:] = (down[0, middle:].astype(full) + upper[0].astype(full)).astype(half)


def gather_kernel(place, *refs):
    ins, outs = refs[:6], refs[7:]
    for block in (0, 1):
        kept, from_down, from_up = ins[3 * block : 3 * block + 3]
        here = place[1 - block]
        for distance in range(SIDE):
            at = lax.rem(here + distance, SIDE)
            value = kept[at].astype(full) + from_down[at].astype(full) + from_up[at].astype(full)
            out = outs[SIDE * block + distance]
            out[...] = value.astype(out.dtype)


def teacher_terms(attention, out_proj, mp, order):
    width = attention.shape[1]
    whole = pl.BlockSpec(memory_space=pltpu.VMEM)
    scalars = pl.BlockSpec(memory_space=pltpu.SMEM)
    anywhere = pl.BlockSpec(memory_space=pl.ANY)
    limit = pltpu.CompilerParams(vmem_limit_bytes=40 * 1024 * 1024)
    place = jnp.stack([mp // SIDE, mp % SIDE]).astype(jnp.int32)
    full_piece = jax.ShapeDtypeStruct((SIDE, BLK, width), half)
    half_piece = jax.ShapeDtypeStruct((SIDE, BLK // 2, width), half)
    moves = full_piece.size
    one_piece = pl.BlockSpec((1, BLK, width), lambda i: (i, 0, 0))
    one_half = pl.BlockSpec((1, BLK // 2, width), lambda i: (i, 0, 0))

    def terms(kernel, pieces, count, blocks):
        return pl.pallas_call(
            kernel,
            in_specs=[scalars, whole, pl.BlockSpec(memory_space=pltpu.HBM)],
            out_specs=[whole] * len(pieces),
            out_shape=pieces,
            scratch_shapes=[
                pltpu.VMEM((count, width, width), half),
                pltpu.SemaphoreType.DMA((count,)),
            ],
            compiler_params=pltpu.CompilerParams(vmem_limit_bytes=48 * 1024 * 1024),
            cost_estimate=pl.CostEstimate(
                flops=2 * blocks * BLK * count * width * width,
                bytes_accessed=2 * count * width * width,
                transcendentals=0,
            ),
        )(place, attention, out_proj)

    lower0, upper0, lower1, upper1 = terms(far_kernel, [half_piece] * 4, 2 * SIDE, 1)
    kept0, up0, down0, kept1, up1, down1 = terms(near_kernel, [full_piece] * 6, SIDE * SIDE, 2)
    lower0, upper0 = step(lower0, 1, 0), step(upper0, -1, 0)
    lower1, upper1 = step(lower1, 0, 1), step(upper1, 0, -1)
    up0, down0, up1, down1 = pl.pallas_call(
        merge_kernel,
        grid=(SIDE,),
        in_specs=[one_piece, one_piece, one_half, one_half] * 2,
        out_specs=[one_piece] * 4,
        out_shape=[full_piece] * 4,
        compiler_params=limit,
        cost_estimate=pl.CostEstimate(
            flops=4 * moves, bytes_accessed=20 * moves, transcendentals=0
        ),
    )(up0, down0, lower0, upper0, up1, down1, lower1, upper1)
    from_down0, from_up0 = step(up0, 1, 0), step(down0, -1, 0)
    from_down1, from_up1 = step(up1, 0, 1), step(down1, 0, -1)
    sums = pl.pallas_call(
        gather_kernel,
        in_specs=[scalars] + [whole] * 6 + [anywhere],
        out_specs=[whole] * (2 * SIDE),
        out_shape=[
            jax.ShapeDtypeStruct((BLK, width), half if distance else full)
            for block in (0, 1)
            for distance in range(SIDE)
        ],
        compiler_params=limit,
        cost_estimate=pl.CostEstimate(
            flops=4 * moves, bytes_accessed=16 * moves, transcendentals=0
        ),
    )(place, kept0, from_down0, from_up0, kept1, from_down1, from_up1, *order)
    results = []
    for block in (0, 1):
        mine = sums[SIDE * block : SIDE * block + SIDE]
        arrived = [
            step(mine[d], 0, d) if block == 0 else step(mine[d], d, 0) for d in range(1, SIDE)
        ]
        results.append([mine[0]] + arrived)
    return results


def total(values):
    result = values[0].astype(full)
    for value in values[1:]:
        result = result + value.astype(full)
    return result


def backward_kernel(dy, down, gate, up, order, grad_gate, grad_up, dh):
    del order
    rows = 8
    for chunk in range(2):
        columns = pl.ds(chunk * (down.shape[1] // 2), down.shape[1] // 2)
        value = jnp.dot(dy[...], down[:, columns], preferred_element_type=full)
        for index in range(value.shape[0] // rows):
            to = (index % 2) * BLK + (index // 2) * rows
            dh[pl.ds(to, rows), columns] = value[index * rows : index * rows + rows]
    gate_val = gate[...]
    sigma = jax.nn.sigmoid(gate_val)
    grad_gate[...] = (dh[...] * up[...] * sigma * (1.0 + gate_val * (1.0 - sigma))).astype(half)
    grad_up[...] = (dh[...] * (gate_val * sigma)).astype(half)


def backward(dy, down, gate, up, order):
    whole = pl.BlockSpec(memory_space=pltpu.VMEM)
    shape = jax.ShapeDtypeStruct(gate.shape, half)
    return pl.pallas_call(
        backward_kernel,
        in_specs=[whole] * 4 + [pl.BlockSpec(memory_space=pl.ANY)],
        out_specs=[whole, whole],
        out_shape=[shape, shape],
        scratch_shapes=[pltpu.VMEM(gate.shape, full)],
        compiler_params=pltpu.CompilerParams(vmem_limit_bytes=56 * 1024 * 1024),
        cost_estimate=pl.CostEstimate(
            flops=2 * dy.shape[0] * down.size,
            bytes_accessed=2 * (down.size + dy.size) + 16 * gate.size,
            transcendentals=gate.size,
        ),
    )(dy, down, gate, up, order)


def spread_kernel(piece, out, sems):
    copies = [
        pltpu.make_async_copy(piece, out.at[to], sems.at[to]) for to in range(out.shape[0])
    ]
    for copy in copies:
        copy.start()
    for copy in copies:
        copy.wait()


def spread(piece, count):
    whole = pl.BlockSpec(memory_space=pltpu.VMEM)
    return pl.pallas_call(
        spread_kernel,
        in_specs=[whole],
        out_specs=pl.BlockSpec(memory_space=pltpu.HBM),
        scratch_shapes=[pltpu.SemaphoreType.DMA((count,))],
        out_shape=jax.ShapeDtypeStruct((count,) + piece.shape, piece.dtype),
        compiler_params=pltpu.CompilerParams(vmem_limit_bytes=16 * 1024 * 1024),
        cost_estimate=pl.CostEstimate(
            flops=0, bytes_accessed=4 * count * piece.size, transcendentals=0
        ),
    )(piece)


def home_kernel(terms, state, out):
    value = state[...].astype(full)
    for source in range(terms.shape[0]):
        value = value + terms[source].astype(full)
    rows = state.shape[0]
    out[pl.ds(0, rows), :] = value.astype(half)
    out[pl.ds(rows, rows), :] = jnp.zeros(state.shape, half)


def home(terms, state):
    rows, width = state.shape
    whole = pl.BlockSpec(memory_space=pltpu.VMEM)
    return pl.pallas_call(
        home_kernel,
        in_specs=[whole, whole],
        out_specs=whole,
        out_shape=jax.ShapeDtypeStruct((2 * rows, width), half),
        compiler_params=pltpu.CompilerParams(vmem_limit_bytes=16 * 1024 * 1024),
        cost_estimate=pl.CostEstimate(
            flops=17 * rows * width, bytes_accessed=40 * rows * width, transcendentals=0
        ),
    )(terms, state)


def pool_kernel(place, message, token_slot, out, inverse, sh, weights, state, sems):
    sources, _, cols = message.shape
    rows = BLK // sources
    token_proj = message[0, :BLK].astype(full)
    for source in range(1, sources):
        token_proj = token_proj + message[source, :BLK].astype(full)
    squares = jnp.zeros((rows, cols), full)
    for source in range(sources):
        tail = message[source, BLK:].astype(full)
        sh[pl.ds(source * rows, rows), :] = tail[:rows]
        squares = squares + tail[rows:]
    tokens = token_slot.shape[1]
    squares = jnp.sum(squares[:3], axis=0, keepdims=True)[:, :tokens]
    inverse[...] = lax.rsqrt(squares / place[1].astype(full) + epsilon)
    slots = jnp.where(place[0] == 0, token_slot[:, :BLK], token_slot[:, BLK:])
    scale = jnp.where(place[0] == 0, inverse[:, :BLK], inverse[:, BLK:])
    hits = slots == lax.broadcasted_iota(jnp.int32, (BLK, BLK), 0)
    counts = jnp.maximum(jnp.sum(hits.astype(full), axis=1, keepdims=True), 1.0)
    weights[...] = jnp.where(hits, scale, 0.0)
    first = weights[...].astype(half)
    second = (weights[...] - lax.reduce_precision(weights[...], 8, 7)).astype(half)
    token_proj = token_proj.astype(half)
    placed = jnp.dot(first, token_proj, preferred_element_type=full)
    placed = placed + jnp.dot(second, token_proj, preferred_element_type=full)
    placed = (placed / counts).astype(half).astype(full)
    state[...] = (sh[...] + placed).astype(half)
    copies = [
        pltpu.make_async_copy(state, out.at[to], sems.at[to]) for to in range(sources)
    ]
    for copy in copies:
        copy.start()
    for copy in copies:
        copy.wait()


def pool(message, token_slot, block, width_full):
    sources, _, cols = message.shape
    whole = pl.BlockSpec(memory_space=pltpu.VMEM)
    tokens = token_slot.shape[0]
    place = jnp.stack([block, jnp.full_like(block, width_full)]).astype(jnp.int32)
    return pl.pallas_call(
        pool_kernel,
        in_specs=[pl.BlockSpec(memory_space=pltpu.SMEM), whole, whole],
        out_specs=[pl.BlockSpec(memory_space=pltpu.HBM), whole],
        out_shape=[
            jax.ShapeDtypeStruct((sources, BLK, cols), half),
            jax.ShapeDtypeStruct((1, tokens), full),
        ],
        scratch_shapes=[
            pltpu.VMEM((BLK, cols), full),
            pltpu.VMEM((BLK, BLK), full),
            pltpu.VMEM((BLK, cols), half),
            pltpu.SemaphoreType.DMA((sources,)),
        ],
        compiler_params=pltpu.CompilerParams(vmem_limit_bytes=40 * 1024 * 1024),
        cost_estimate=pl.CostEstimate(
            flops=6 * message.size, bytes_accessed=4 * message.size, transcendentals=tokens
        ),
    )(place, message, token_slot[None])


def forward_kernel(
    pieces, gain, order, other, gate_hbm, up_hbm, down_hbm, state, gate, up, out, normed, act, held, sems
):
    del order, other
    parts = 3
    part = gate_hbm.shape[0] // parts

    def load(which, source, third):
        at = pl.ds(third * part, part)
        return pltpu.make_async_copy(
            source.at[at], held.at[which, at], sems.at[parts * which + third]
        )

    for third in range(parts):
        load(0, gate_hbm, third).start()
        load(1, up_hbm, third).start()
    cols = pieces.shape[2]
    groups = state.shape[1] // cols
    for block in range(state.shape[0] // BLK):
        rows = pl.ds(block * BLK, BLK)
        squares = jnp.zeros((BLK, 128), full)
        for group in range(groups):
            value = pieces[block * groups + group]
            state[rows, pl.ds(group * cols, cols)] = value
            wide = value.astype(full)
            wide = wide * wide
            for lane in range(0, cols, 128):
                squares = squares + wide[:, lane : lane + 128]
        mean = jnp.sum(squares, axis=1, keepdims=True) / state.shape[1]
        inverse = lax.rsqrt(mean + epsilon)
        for group in range(groups):
            at = pl.ds(group * cols, cols)
            wide = pieces[block * groups + group].astype(full)
            normed[rows, at] = (wide * inverse * gain[:, at]).astype(normed.dtype)
    half_hidden = gate.shape[1] // 2
    for third in range(parts):
        load(0, gate_hbm, third).wait()
        load(1, up_hbm, third).wait()
        load(2, down_hbm, third).start()
        depth = pl.ds(third * part, part)
        for index in range(2):
            at = pl.ds(index * half_hidden, half_hidden)
            for which, total_ref in ((0, gate), (1, up)):
                value = jnp.dot(
                    normed[:, depth], held[which, depth, at], preferred_element_type=full
                )
                total_ref[:, at] = value if third == 0 else total_ref[:, at] + value
    gate_val = gate[...]
    act[...] = (gate_val * jax.nn.sigmoid(gate_val) * up[...]).astype(half)
    for third in range(parts):
        load(2, down_hbm, third).wait()
    down_w = held.at[2]
    rows = out.shape[1] // 2
    wide_chunk = 512

    @pl.loop(0, state.shape[1] // wide_chunk)
    def _(index):
        at = pl.ds(pl.multiple_of(index * wide_chunk, wide_chunk), wide_chunk)
        value = times_rows(act[...], down_w[at, :])
        for to in range(out.shape[0]):
            first = value[to * rows : to * rows + rows]
            second = value[BLK + to * rows : BLK + to * rows + rows]
            out[to, :, at] = jnp.concatenate([first, second], axis=0).astype(half)


def forward(pieces, gain, gate_w, up_w, down_w, order, other):
    width, hidden = gate_w.shape
    n_mp = pieces.shape[0]
    rows = 2 * BLK
    whole = pl.BlockSpec(memory_space=pltpu.VMEM)
    return pl.pallas_call(
        forward_kernel,
        in_specs=[whole, whole] + [pl.BlockSpec(memory_space=pl.ANY)] * 2
        + [pl.BlockSpec(memory_space=pltpu.HBM)] * 3,
        out_specs=[whole] * 4,
        out_shape=[
            jax.ShapeDtypeStruct((rows, width), half),
            jax.ShapeDtypeStruct((rows, hidden), full),
            jax.ShapeDtypeStruct((rows, hidden), full),
            jax.ShapeDtypeStruct((n_mp, rows // n_mp, width), half),
        ],
        scratch_shapes=[
            pltpu.VMEM((rows, width), half),
            pltpu.VMEM((rows, hidden), half),
            pltpu.VMEM((3, width, hidden), half),
            pltpu.SemaphoreType.DMA((9,)),
        ],
        compiler_params=pltpu.CompilerParams(vmem_limit_bytes=56 * 1024 * 1024),
        cost_estimate=pl.CostEstimate(
            flops=6 * rows * width * hidden,
            bytes_accessed=6 * width * hidden + 10 * rows * width,
            transcendentals=rows * hidden,
        ),
    )(pieces, gain[None], order, other, gate_w, up_w, down_w)


def slope_kernel(terms, dy, state, gain, order, out):
    del order
    rows, width = dy.shape
    cols = out.shape[2]
    wide = state[...].astype(full)
    inverse = lax.rsqrt(jnp.mean(wide * wide, axis=1, keepdims=True) + epsilon)
    dn = terms[0].astype(full)
    for source in range(1, terms.shape[0]):
        dn = dn + terms[source].astype(full)
    gained = gain[...] * dn
    mean = jnp.mean(gained * wide, axis=1, keepdims=True)
    dx = dy[...].astype(full) + inverse * gained - wide * (inverse * inverse * inverse) * mean
    for group in range(out.shape[0]):
        out[group] = dx[:, group * cols : (group + 1) * cols].astype(out.dtype)


def slope(terms, dy, state, gain, groups, order):
    rows, width = dy.shape
    whole = pl.BlockSpec(memory_space=pltpu.VMEM)
    return pl.pallas_call(
        slope_kernel,
        in_specs=[whole] * 4 + [pl.BlockSpec(memory_space=pl.ANY)],
        out_specs=whole,
        out_shape=jax.ShapeDtypeStruct((groups, rows, width // groups), half),
        compiler_params=pltpu.CompilerParams(vmem_limit_bytes=16 * 1024 * 1024),
        cost_estimate=pl.CostEstimate(
            flops=30 * rows * width, bytes_accessed=40 * rows * width, transcendentals=rows
        ),
    )(terms, dy, state, gain[None], order)


def on_device(
    attention,
    out_proj,
    residual,
    final_gain,
    adapter_weight,
    token_slot,
    block_owner,
    student_hidden,
    cotangent,
    student_gain,
    gate_weight,
    up_weight,
    down_weight,
):
    tokens, width_here = attention.shape
    width_full = out_proj.shape[1]
    student_width = adapter_weight.shape[1]
    blocks = tokens // BLK
    n_mp = lax.axis_size("mp")
    n_dp = lax.axis_size("dp")
    dp = lax.axis_index("dp")
    mp = lax.axis_index("mp")
    slots = student_hidden.shape[2]
    rows = BLK // n_mp
    groups = n_mp // blocks
    cols = student_width // groups
    out_cols = student_width // n_dp
    mine_rows = blocks * rows

    ids = jnp.arange(block_owner.shape[0], dtype=jnp.int32)
    my_ids = dp * blocks + jnp.arange(blocks, dtype=jnp.int32)
    my_owner = take(block_owner, (dp * blocks,), (blocks,))
    my_slot = jnp.sum(
        (block_owner[None, :] == my_owner[:, None]) & (ids[None, :] < my_ids[:, None]),
        axis=1,
        dtype=jnp.int32,
    )

    def fetch(array):
        everyone = lax.all_gather(array[0], "dp", axis=0, tiled=False)
        picked = []
        for k in range(blocks):
            at = (my_owner[k], 0, my_slot[k], 0)
            piece = take(everyone, at, (1, rows, 1, student_width))
            picked.append(piece.reshape(rows, student_width))
        return jnp.stack(picked)

    sh_rows = fetch(student_hidden)
    dy_rows = fetch(cotangent)
    dy = lax.all_gather(dy_rows, "mp", axis=0, tiled=False)

    hidden = residual.astype(full) + jnp.concatenate(
        [total(v) for v in teacher_terms(attention, out_proj, mp, (sh_rows,))], axis=0
    )
    squares = jnp.sum(hidden * hidden, axis=1)
    gained_hidden = hidden * final_gain
    parts = jnp.einsum(
        "ktd,dce->kcte",
        gained_hidden.astype(half).reshape(blocks, BLK, width_here),
        adapter_weight.reshape(width_here, groups, cols),
        preferred_element_type=full,
    ).astype(half)
    sh_parts = jnp.swapaxes(sh_rows.reshape(blocks, rows, groups, cols), 1, 2)
    sq_parts = three_parts(squares)
    sq_parts = jnp.pad(
        jnp.concatenate([sq_parts, partner(sq_parts)], axis=0), ((0, 2), (0, cols - tokens))
    )
    message = jnp.concatenate(
        [
            parts,
            sh_parts,
            jnp.broadcast_to(sq_parts[None, None], (blocks, groups) + sq_parts.shape),
        ],
        axis=2,
    )
    message = exchange(message.reshape(n_mp, BLK + rows + 8, cols), "mp")
    states, inverse_rms = pool(message, token_slot, mp // groups, width_full)
    states = exchange(states, "mp")

    slots_block = token_slot.reshape(blocks, BLK)
    onehot = slots_block[:, None, :] == jnp.arange(BLK, dtype=jnp.int32)[None, :, None]
    counts = jnp.maximum(jnp.sum(onehot.astype(full), axis=2), 1.0)
    onehot = onehot.astype(half)
    normed = (gained_hidden * inverse_rms.reshape(tokens, 1)).astype(half).reshape(blocks, BLK, width_here)
    pooled = jnp.einsum("krt,ktd->krd", onehot, normed, preferred_element_type=full)
    pooled = (pooled / counts[:, :, None]).astype(half)
    pooled_all = lax.all_gather(pooled.reshape(n_mp, mine_rows, width_here), "dp", axis=0, tiled=False)
    pooled_all = jnp.swapaxes(pooled_all, 0, 1).reshape(n_dp * tokens, width_here)

    state, gate, up, output = forward(
        states, student_gain, gate_weight, up_weight, down_weight, pooled, partner(states[0, :8, :128])
    )
    grad_gate, grad_up = backward(dy.reshape(tokens, student_width), down_weight, gate, up, output)
    dn = (times_rows(grad_gate, gate_weight) + times_rows(grad_up, up_weight)).astype(half)
    output = exchange(output, "mp")
    dn, output = lax.optimization_barrier((dn, output))
    dn = exchange(dn.reshape(n_mp, mine_rows, student_width), "mp")
    here = mp * mine_rows
    state_rows = take(
        state.reshape(blocks, BLK, student_width),
        (0, mp * rows, 0),
        (blocks, rows, student_width),
    )
    out_rows = home(output, state_rows.reshape(mine_rows, student_width))
    dproj = slope(
        dn,
        take(
            dy, ((mp % groups) * blocks, mp // groups, 0, 0), (blocks, 1, rows, student_width)
        ).reshape(mine_rows, student_width),
        take(state, (here, 0), (mine_rows, student_width)),
        student_gain,
        n_dp,
        out_rows,
    )
    dproj = exchange(spread(exchange(dproj, "dp"), n_mp), "mp")
    adapter_grad = lax.dot_general(
        pooled_all,
        dproj.reshape(n_dp * tokens, out_cols),
        (((0,), (0,)), ((), ())),
        preferred_element_type=full,
    )

    back = lax.all_gather(out_rows, "dp", axis=0, tiled=False)
    before = (block_owner[None, :] == block_owner[:, None]) & (ids[None, :] < ids[:, None])
    ranks = jnp.sum(before, axis=1, dtype=jnp.int32)
    mine = block_owner == dp
    picks = []
    for slot in range(slots):
        chosen = mine & (ranks == slot)
        index = jnp.sum(jnp.where(chosen, ids, 0))
        at = (index // blocks, (index % blocks) * rows, 0)
        piece = take(back, at, (1, rows, student_width))[0]
        picks.append(jnp.where(jnp.any(chosen), piece, jnp.zeros((), half)))
    student_out = jnp.stack(picks, axis=1)
    return (student_out[None], adapter_grad)


def solution(mesh):
    return jax.shard_map(
        on_device,
        mesh=mesh,
        in_specs=(
            P("dp", "mp"),
            P("mp", None),
            P("dp", "mp"),
            P("mp"),
            P("mp", None),
            P("dp"),
            P(),
            P("dp", "mp", None, None),
            P("dp", "mp", None, None),
            P(),
            P(None, "mp"),
            P(None, "mp"),
            P(None, "mp"),
        ),
        out_specs=(P("dp", "mp", None, None), P("mp", "dp")),
        check_vma=False,
    )
```

```python
import jax
import jax.numpy as jnp
from jax import lax
from jax.experimental import pallas as pl
from jax.experimental.pallas import tpu as pltpu
from jax.sharding import PartitionSpec as P

BLK = 128
epsilon = 1e-06
half = jnp.bfloat16
full = jnp.float32


def exchange(pieces, axis):
    return lax.all_to_all(pieces, axis, split_axis=0, concat_axis=0, tiled=True)


def take(array, starts, sizes):
    return lax.dynamic_slice(array, starts, sizes, allow_negative_indices=False)


def three_parts(value):
    first = lax.reduce_precision(value, 8, 7)
    rest = value - first
    second = lax.reduce_precision(rest, 8, 7)
    return jnp.stack([first, second, rest - second]).astype(half)


def times_rows(left, right):
    return lax.dot_general(left, right, (((1,), (1,)), ((), ())), preferred_element_type=full)


SIDE = 4


def step(value, along_y, along_z):
    pairs = []
    for y in range(SIDE):
        for z in range(SIDE):
            to = ((y + along_y) % SIDE) * SIDE + (z + along_z) % SIDE
            pairs.append((y * SIDE + z, to))
    return lax.ppermute(value, "mp", pairs)


def far_kernel(place, left, right, lower0, upper0, lower1, upper1, held, sems):
    width = held.shape[2]
    y, z = lax.rem(place[0] + 2, SIDE), lax.rem(place[1] + 2, SIDE)
    middle = BLK // 2
    loads = []
    for index in range(2 * SIDE):
        piece = y * SIDE + index if index < SIDE else (index - SIDE) * SIDE + z
        columns = pl.ds(pl.multiple_of(piece * width, width), width)
        load = pltpu.make_async_copy(right.at[:, columns], held.at[index], sems.at[index])
        load.start()
        loads.append(load)
    for index in range(2 * SIDE):
        loads[index].wait()
        block, at = index // SIDE, index % SIDE
        value = jnp.dot(
            left[pl.ds(block * BLK, BLK), :], held[index], preferred_element_type=full
        ).astype(half)
        lower, upper = (lower0, upper0) if block == 0 else (lower1, upper1)
        lower[at] = value[:middle]
        upper[at] = value[middle:]


def near_kernel(place, left, right, kept0, up0, down0, kept1, up1, down1, held, sems):
    outs = {0: (kept0, kept1), 1: (up0, up1), 3: (down0, down1)}
    width = held.shape[2]
    y, z = place[0], place[1]

    def load(index):
        piece = lax.rem(y + index // SIDE, SIDE) * SIDE + lax.rem(index, SIDE)
        columns = pl.ds(pl.multiple_of(piece * width, width), width)
        return pltpu.make_async_copy(right.at[:, columns], held.at[index], sems.at[index])

    for index in range(SIDE * SIDE):
        load(index).start()

    @pl.loop(0, SIDE * SIDE)
    def _(index):
        load(index).wait()
        value = jnp.dot(left[...], held[index], preferred_element_type=full).astype(half)
        along_y, at_z = index // SIDE, lax.rem(index, SIDE)
        at_y, along_z = lax.rem(y + along_y, SIDE), lax.rem(at_z - z + SIDE, SIDE)
        for distance, (first, second) in outs.items():

            @pl.when(along_y == distance)
            def _():
                first[at_z] = value[:BLK]

            @pl.when(along_z == distance)
            def _():
                second[at_y] = value[BLK:]


def merge_kernel(*refs):
    ins, outs = refs[:8], refs[8:]
    middle = BLK // 2
    for block in (0, 1):
        up, down, lower, upper = ins[4 * block : 4 * block + 4]
        to_up, to_down = outs[2 * block], outs[2 * block + 1]
        to_up[0, :middle] = (up[0, :middle].astype(full) + lower[0].astype(full)).astype(half)
        to_up[0, middle:] = up[0, middle:]
        to_down[0, :middle] = down[0, :middle]
        to_down[0, middle:] = (down[0, middle:].astype(full) + upper[0].astype(full)).astype(half)


def gather_kernel(place, *refs):
    ins, outs = refs[:6], refs[8:]
    for block in (0, 1):
        kept, from_down, from_up = ins[3 * block : 3 * block + 3]
        here = place[1 - block]
        for distance in range(SIDE):
            at = lax.rem(here + distance, SIDE)
            value = kept[at].astype(full) + from_down[at].astype(full) + from_up[at].astype(full)
            out = outs[SIDE * block + distance]
            out[...] = value.astype(out.dtype)


def teacher_terms(attention, out_proj, mp, order):
    width = attention.shape[1]
    whole = pl.BlockSpec(memory_space=pltpu.VMEM)
    scalars = pl.BlockSpec(memory_space=pltpu.SMEM)
    anywhere = pl.BlockSpec(memory_space=pl.ANY)
    limit = pltpu.CompilerParams(vmem_limit_bytes=40 * 1024 * 1024)
    place = jnp.stack([mp // SIDE, mp % SIDE]).astype(jnp.int32)
    full_piece = jax.ShapeDtypeStruct((SIDE, BLK, width), half)
    half_piece = jax.ShapeDtypeStruct((SIDE, BLK // 2, width), half)
    moves = full_piece.size
    one_piece = pl.BlockSpec((1, BLK, width), lambda i: (i, 0, 0))
    one_half = pl.BlockSpec((1, BLK // 2, width), lambda i: (i, 0, 0))

    def terms(kernel, pieces, count, blocks):
        return pl.pallas_call(
            kernel,
            in_specs=[scalars, whole, pl.BlockSpec(memory_space=pltpu.HBM)],
            out_specs=[whole] * len(pieces),
            out_shape=pieces,
            scratch_shapes=[
                pltpu.VMEM((count, width, width), half),
                pltpu.SemaphoreType.DMA((count,)),
            ],
            compiler_params=pltpu.CompilerParams(vmem_limit_bytes=48 * 1024 * 1024),
            cost_estimate=pl.CostEstimate(
                flops=2 * blocks * BLK * count * width * width,
                bytes_accessed=2 * count * width * width,
                transcendentals=0,
            ),
        )(place, attention, out_proj)

    lower0, upper0, lower1, upper1 = terms(far_kernel, [half_piece] * 4, 2 * SIDE, 1)
    kept0, up0, down0, kept1, up1, down1 = terms(near_kernel, [full_piece] * 6, SIDE * SIDE, 2)
    lower0, upper0 = step(lower0, 1, 0), step(upper0, -1, 0)
    lower1, upper1 = step(lower1, 0, 1), step(upper1, 0, -1)
    up0, down0, up1, down1 = pl.pallas_call(
        merge_kernel,
        grid=(SIDE,),
        in_specs=[one_piece, one_piece, one_half, one_half] * 2,
        out_specs=[one_piece] * 4,
        out_shape=[full_piece] * 4,
        compiler_params=limit,
        cost_estimate=pl.CostEstimate(
            flops=4 * moves, bytes_accessed=20 * moves, transcendentals=0
        ),
    )(up0, down0, lower0, upper0, up1, down1, lower1, upper1)
    from_down0, from_up0 = step(up0, 1, 0), step(down0, -1, 0)
    from_down1, from_up1 = step(up1, 0, 1), step(down1, 0, -1)
    sums = pl.pallas_call(
        gather_kernel,
        in_specs=[scalars] + [whole] * 6 + [anywhere] * 2,
        out_specs=[whole] * (2 * SIDE),
        out_shape=[
            jax.ShapeDtypeStruct((BLK, width), half if distance else full)
            for block in (0, 1)
            for distance in range(SIDE)
        ],
        compiler_params=limit,
        cost_estimate=pl.CostEstimate(
            flops=4 * moves, bytes_accessed=16 * moves, transcendentals=0
        ),
    )(place, kept0, from_down0, from_up0, kept1, from_down1, from_up1, *order)
    results = []
    for block in (0, 1):
        mine = sums[SIDE * block : SIDE * block + SIDE]
        arrived = [
            step(mine[d], 0, d) if block == 0 else step(mine[d], d, 0) for d in range(1, SIDE)
        ]
        results.append([mine[0]] + arrived)
    return results


def total(values):
    result = values[0].astype(full)
    for value in values[1:]:
        result = result + value.astype(full)
    return result


def backward_kernel(dy, down, gate, up, order, grad_gate, grad_up, dh):
    del order
    rows = 8
    for chunk in range(2):
        columns = pl.ds(chunk * (down.shape[1] // 2), down.shape[1] // 2)
        value = jnp.dot(dy[...], down[:, columns], preferred_element_type=full)
        for index in range(value.shape[0] // rows):
            to = (index % 2) * BLK + (index // 2) * rows
            dh[pl.ds(to, rows), columns] = value[index * rows : index * rows + rows]
    gate_val = gate[...]
    sigma = jax.nn.sigmoid(gate_val)
    grad_gate[...] = (dh[...] * up[...] * sigma * (1.0 + gate_val * (1.0 - sigma))).astype(half)
    grad_up[...] = (dh[...] * (gate_val * sigma)).astype(half)


def backward(dy, down, gate, up, order):
    whole = pl.BlockSpec(memory_space=pltpu.VMEM)
    shape = jax.ShapeDtypeStruct(gate.shape, half)
    return pl.pallas_call(
        backward_kernel,
        in_specs=[whole] * 4 + [pl.BlockSpec(memory_space=pl.ANY)],
        out_specs=[whole, whole],
        out_shape=[shape, shape],
        scratch_shapes=[pltpu.VMEM(gate.shape, full)],
        compiler_params=pltpu.CompilerParams(vmem_limit_bytes=56 * 1024 * 1024),
        cost_estimate=pl.CostEstimate(
            flops=2 * dy.shape[0] * down.size,
            bytes_accessed=2 * (down.size + dy.size) + 16 * gate.size,
            transcendentals=gate.size,
        ),
    )(dy, down, gate, up, order)


def spread_kernel(piece, out, sems):
    copies = [
        pltpu.make_async_copy(piece, out.at[to], sems.at[to]) for to in range(out.shape[0])
    ]
    for copy in copies:
        copy.start()
    for copy in copies:
        copy.wait()


def spread(piece, count):
    whole = pl.BlockSpec(memory_space=pltpu.VMEM)
    return pl.pallas_call(
        spread_kernel,
        in_specs=[whole],
        out_specs=pl.BlockSpec(memory_space=pltpu.HBM),
        scratch_shapes=[pltpu.SemaphoreType.DMA((count,))],
        out_shape=jax.ShapeDtypeStruct((count,) + piece.shape, piece.dtype),
        compiler_params=pltpu.CompilerParams(vmem_limit_bytes=16 * 1024 * 1024),
        cost_estimate=pl.CostEstimate(
            flops=0, bytes_accessed=4 * count * piece.size, transcendentals=0
        ),
    )(piece)


def home_kernel(terms, state, out):
    value = state[...].astype(full)
    for source in range(terms.shape[0]):
        value = value + terms[source].astype(full)
    rows = state.shape[0]
    out[pl.ds(0, rows), :] = value.astype(half)
    out[pl.ds(rows, rows), :] = jnp.zeros(state.shape, half)


def home(terms, state):
    rows, width = state.shape
    whole = pl.BlockSpec(memory_space=pltpu.VMEM)
    return pl.pallas_call(
        home_kernel,
        in_specs=[whole, whole],
        out_specs=whole,
        out_shape=jax.ShapeDtypeStruct((2 * rows, width), half),
        compiler_params=pltpu.CompilerParams(vmem_limit_bytes=16 * 1024 * 1024),
        cost_estimate=pl.CostEstimate(
            flops=17 * rows * width, bytes_accessed=40 * rows * width, transcendentals=0
        ),
    )(terms, state)


def pool_kernel(place, message, token_slot, out, inverse, sh, weights, state, sems):
    sources, _, cols = message.shape
    rows = BLK // sources
    token_proj = message[0, :BLK].astype(full)
    for source in range(1, sources):
        token_proj = token_proj + message[source, :BLK].astype(full)
    squares = jnp.zeros((rows, cols), full)
    for source in range(sources):
        tail = message[source, BLK:].astype(full)
        sh[pl.ds(source * rows, rows), :] = tail[:rows]
        squares = squares + tail[rows:]
    tokens = token_slot.shape[1]
    squares = jnp.sum(squares, axis=0, keepdims=True)[:, :tokens]
    inverse[...] = lax.rsqrt(squares / place[1].astype(full) + epsilon)
    slots = jnp.where(place[0] == 0, token_slot[:, :BLK], token_slot[:, BLK:])
    scale = jnp.where(place[0] == 0, inverse[:, :BLK], inverse[:, BLK:])
    hits = slots == lax.broadcasted_iota(jnp.int32, (BLK, BLK), 0)
    counts = jnp.maximum(jnp.sum(hits.astype(full), axis=1, keepdims=True), 1.0)
    weights[...] = jnp.where(hits, scale, 0.0)
    first = weights[...].astype(half)
    second = (weights[...] - lax.reduce_precision(weights[...], 8, 7)).astype(half)
    token_proj = token_proj.astype(half)
    placed = jnp.dot(first, token_proj, preferred_element_type=full)
    placed = placed + jnp.dot(second, token_proj, preferred_element_type=full)
    placed = (placed / counts).astype(half).astype(full)
    state[...] = (sh[...] + placed).astype(half)
    copies = [
        pltpu.make_async_copy(state, out.at[to], sems.at[to]) for to in range(sources)
    ]
    for copy in copies:
        copy.start()
    for copy in copies:
        copy.wait()


def pool(message, token_slot, block, width_full):
    sources, _, cols = message.shape
    whole = pl.BlockSpec(memory_space=pltpu.VMEM)
    tokens = token_slot.shape[0]
    place = jnp.stack([block, jnp.full_like(block, width_full)]).astype(jnp.int32)
    return pl.pallas_call(
        pool_kernel,
        in_specs=[pl.BlockSpec(memory_space=pltpu.SMEM), whole, whole],
        out_specs=[pl.BlockSpec(memory_space=pltpu.HBM), whole],
        out_shape=[
            jax.ShapeDtypeStruct((sources, BLK, cols), half),
            jax.ShapeDtypeStruct((1, tokens), full),
        ],
        scratch_shapes=[
            pltpu.VMEM((BLK, cols), full),
            pltpu.VMEM((BLK, BLK), full),
            pltpu.VMEM((BLK, cols), half),
            pltpu.SemaphoreType.DMA((sources,)),
        ],
        compiler_params=pltpu.CompilerParams(vmem_limit_bytes=40 * 1024 * 1024),
        cost_estimate=pl.CostEstimate(
            flops=6 * message.size, bytes_accessed=4 * message.size, transcendentals=tokens
        ),
    )(place, message, token_slot[None])


def forward_kernel(
    pieces, gain, order, gate_hbm, up_hbm, down_hbm, state, gate, up, out, normed, act, held, sems
):
    del order
    parts = 3
    part = gate_hbm.shape[0] // parts

    def load(which, source, third):
        at = pl.ds(third * part, part)
        return pltpu.make_async_copy(
            source.at[at], held.at[which, at], sems.at[parts * which + third]
        )

    for third in range(parts):
        load(0, gate_hbm, third).start()
        load(1, up_hbm, third).start()
    cols = pieces.shape[2]
    groups = state.shape[1] // cols
    for block in range(state.shape[0] // BLK):
        rows = pl.ds(block * BLK, BLK)
        squares = jnp.zeros((BLK, 128), full)
        for group in range(groups):
            value = pieces[block * groups + group]
            state[rows, pl.ds(group * cols, cols)] = value
            wide = value.astype(full)
            wide = wide * wide
            for lane in range(0, cols, 128):
                squares = squares + wide[:, lane : lane + 128]
        mean = jnp.sum(squares, axis=1, keepdims=True) / state.shape[1]
        inverse = lax.rsqrt(mean + epsilon)
        for group in range(groups):
            at = pl.ds(group * cols, cols)
            wide = pieces[block * groups + group].astype(full)
            normed[rows, at] = (wide * inverse * gain[:, at]).astype(normed.dtype)
    half_hidden = gate.shape[1] // 2
    for third in range(parts):
        load(0, gate_hbm, third).wait()
        load(1, up_hbm, third).wait()
        load(2, down_hbm, third).start()
        depth = pl.ds(third * part, part)
        for index in range(2):
            at = pl.ds(index * half_hidden, half_hidden)
            for which, total_ref in ((0, gate), (1, up)):
                value = jnp.dot(
                    normed[:, depth], held[which, depth, at], preferred_element_type=full
                )
                total_ref[:, at] = value if third == 0 else total_ref[:, at] + value
    gate_val = gate[...]
    act[...] = (gate_val * jax.nn.sigmoid(gate_val) * up[...]).astype(half)
    for third in range(parts):
        load(2, down_hbm, third).wait()
    down_w = held.at[2]
    rows = out.shape[1] // 2
    wide_chunk = 512

    @pl.loop(0, state.shape[1] // wide_chunk)
    def _(index):
        at = pl.ds(pl.multiple_of(index * wide_chunk, wide_chunk), wide_chunk)
        value = times_rows(act[...], down_w[at, :])
        for to in range(out.shape[0]):
            first = value[to * rows : to * rows + rows]
            second = value[BLK + to * rows : BLK + to * rows + rows]
            out[to, :, at] = jnp.concatenate([first, second], axis=0).astype(half)


def forward(pieces, gain, gate_w, up_w, down_w, order):
    width, hidden = gate_w.shape
    n_mp = pieces.shape[0]
    rows = 2 * BLK
    whole = pl.BlockSpec(memory_space=pltpu.VMEM)
    return pl.pallas_call(
        forward_kernel,
        in_specs=[whole, whole, pl.BlockSpec(memory_space=pl.ANY)]
        + [pl.BlockSpec(memory_space=pltpu.HBM)] * 3,
        out_specs=[whole] * 4,
        out_shape=[
            jax.ShapeDtypeStruct((rows, width), half),
            jax.ShapeDtypeStruct((rows, hidden), full),
            jax.ShapeDtypeStruct((rows, hidden), full),
            jax.ShapeDtypeStruct((n_mp, rows // n_mp, width), half),
        ],
        scratch_shapes=[
            pltpu.VMEM((rows, width), half),
            pltpu.VMEM((rows, hidden), half),
            pltpu.VMEM((3, width, hidden), half),
            pltpu.SemaphoreType.DMA((9,)),
        ],
        compiler_params=pltpu.CompilerParams(vmem_limit_bytes=56 * 1024 * 1024),
        cost_estimate=pl.CostEstimate(
            flops=6 * rows * width * hidden,
            bytes_accessed=6 * width * hidden + 10 * rows * width,
            transcendentals=rows * hidden,
        ),
    )(pieces, gain[None], order, gate_w, up_w, down_w)


def slope_kernel(terms, dy, state, gain, order, out):
    del order
    rows, width = dy.shape
    cols = out.shape[2]
    wide = state[...].astype(full)
    inverse = lax.rsqrt(jnp.mean(wide * wide, axis=1, keepdims=True) + epsilon)
    dn = terms[0].astype(full)
    for source in range(1, terms.shape[0]):
        dn = dn + terms[source].astype(full)
    gained = gain[...] * dn
    mean = jnp.mean(gained * wide, axis=1, keepdims=True)
    dx = dy[...].astype(full) + inverse * gained - wide * (inverse * inverse * inverse) * mean
    for group in range(out.shape[0]):
        out[group] = dx[:, group * cols : (group + 1) * cols].astype(out.dtype)


def slope(terms, dy, state, gain, groups, order):
    rows, width = dy.shape
    whole = pl.BlockSpec(memory_space=pltpu.VMEM)
    return pl.pallas_call(
        slope_kernel,
        in_specs=[whole] * 4 + [pl.BlockSpec(memory_space=pl.ANY)],
        out_specs=whole,
        out_shape=jax.ShapeDtypeStruct((groups, rows, width // groups), half),
        compiler_params=pltpu.CompilerParams(vmem_limit_bytes=16 * 1024 * 1024),
        cost_estimate=pl.CostEstimate(
            flops=30 * rows * width, bytes_accessed=40 * rows * width, transcendentals=rows
        ),
    )(terms, dy, state, gain[None], order)


def on_device(
    attention,
    out_proj,
    residual,
    final_gain,
    adapter_weight,
    token_slot,
    block_owner,
    student_hidden,
    cotangent,
    student_gain,
    gate_weight,
    up_weight,
    down_weight,
):
    tokens, width_here = attention.shape
    width_full = out_proj.shape[1]
    student_width = adapter_weight.shape[1]
    blocks = tokens // BLK
    n_mp = lax.axis_size("mp")
    n_dp = lax.axis_size("dp")
    dp = lax.axis_index("dp")
    mp = lax.axis_index("mp")
    slots = student_hidden.shape[2]
    rows = BLK // n_mp
    groups = n_mp // blocks
    cols = student_width // groups
    out_cols = student_width // n_dp
    mine_rows = blocks * rows

    ids = jnp.arange(block_owner.shape[0], dtype=jnp.int32)
    my_ids = dp * blocks + jnp.arange(blocks, dtype=jnp.int32)
    my_owner = take(block_owner, (dp * blocks,), (blocks,))
    my_slot = jnp.sum(
        (block_owner[None, :] == my_owner[:, None]) & (ids[None, :] < my_ids[:, None]),
        axis=1,
        dtype=jnp.int32,
    )

    both = jnp.concatenate([student_hidden[0], cotangent[0]], axis=1)
    everyone = lax.all_gather(both, "dp", axis=0, tiled=False)

    def fetch(offset):
        picked = []
        for k in range(blocks):
            at = (my_owner[k], 0, my_slot[k] + offset, 0)
            picked.append(
                take(everyone, at, (1, rows, 1, student_width)).reshape(rows, student_width)
            )
        return jnp.stack(picked)

    sh_rows = fetch(0)
    dy_rows = fetch(student_hidden.shape[2])
    dy = lax.all_gather(dy_rows, "mp", axis=0, tiled=False)

    hidden = residual.astype(full) + jnp.concatenate(
        [total(v) for v in teacher_terms(attention, out_proj, mp, (sh_rows, dy_rows))], axis=0
    )
    squares = jnp.sum(hidden * hidden, axis=1)
    gained_hidden = hidden * final_gain
    parts = jnp.einsum(
        "ktd,dce->kcte",
        gained_hidden.astype(half).reshape(blocks, BLK, width_here),
        adapter_weight.reshape(width_here, groups, cols),
        preferred_element_type=full,
    ).astype(half)
    sh_parts = jnp.swapaxes(sh_rows.reshape(blocks, rows, groups, cols), 1, 2)
    sq_parts = jnp.zeros((8, cols), half).at[:3, :tokens].set(three_parts(squares))
    message = jnp.concatenate(
        [
            parts,
            sh_parts,
            jnp.broadcast_to(sq_parts[None, None], (blocks, groups) + sq_parts.shape),
        ],
        axis=2,
    )
    message = exchange(message.reshape(n_mp, BLK + rows + 8, cols), "mp")
    states, inverse_rms = pool(message, token_slot, mp // groups, width_full)
    states = exchange(states, "mp")

    slots_block = token_slot.reshape(blocks, BLK)
    onehot = slots_block[:, None, :] == jnp.arange(BLK, dtype=jnp.int32)[None, :, None]
    counts = jnp.maximum(jnp.sum(onehot.astype(full), axis=2), 1.0)
    onehot = onehot.astype(half)
    normed = (gained_hidden * inverse_rms.reshape(tokens, 1)).astype(half).reshape(blocks, BLK, width_here)
    pooled = jnp.einsum("krt,ktd->krd", onehot, normed, preferred_element_type=full)
    pooled = (pooled / counts[:, :, None]).astype(half)
    pooled_all = lax.all_gather(pooled.reshape(n_mp, mine_rows, width_here), "dp", axis=0, tiled=False)
    pooled_all = jnp.swapaxes(pooled_all, 0, 1).reshape(n_dp * tokens, width_here)

    state, gate, up, output = forward(
        states, student_gain, gate_weight, up_weight, down_weight, pooled
    )
    grad_gate, grad_up = backward(dy.reshape(tokens, student_width), down_weight, gate, up, output)
    dn = (times_rows(grad_gate, gate_weight) + times_rows(grad_up, up_weight)).astype(half)
    output = exchange(output, "mp")
    dn, output = lax.optimization_barrier((dn, output))
    dn = exchange(dn.reshape(n_mp, mine_rows, student_width), "mp")
    here = mp * mine_rows
    state_rows = take(
        state.reshape(blocks, BLK, student_width),
        (0, mp * rows, 0),
        (blocks, rows, student_width),
    )
    out_rows = home(output, state_rows.reshape(mine_rows, student_width))
    dproj = slope(
        dn,
        take(
            dy, ((mp % groups) * blocks, mp // groups, 0, 0), (blocks, 1, rows, student_width)
        ).reshape(mine_rows, student_width),
        take(state, (here, 0), (mine_rows, student_width)),
        student_gain,
        n_dp,
        out_rows,
    )
    dproj = exchange(spread(exchange(dproj, "dp"), n_mp), "mp")
    adapter_grad = lax.dot_general(
        pooled_all,
        dproj.reshape(n_dp * tokens, out_cols),
        (((0,), (0,)), ((), ())),
        preferred_element_type=full,
    )

    back = lax.all_gather(out_rows, "dp", axis=0, tiled=False)
    before = (block_owner[None, :] == block_owner[:, None]) & (ids[None, :] < ids[:, None])
    ranks = jnp.sum(before, axis=1, dtype=jnp.int32)
    mine = block_owner == dp
    picks = []
    for slot in range(slots):
        chosen = mine & (ranks == slot)
        index = jnp.sum(jnp.where(chosen, ids, 0))
        at = (index // blocks, (index % blocks) * rows, 0)
        piece = take(back, at, (1, rows, student_width))[0]
        picks.append(jnp.where(jnp.any(chosen), piece, jnp.zeros((), half)))
    student_out = jnp.stack(picks, axis=1)
    return (student_out[None], adapter_grad)


def solution(mesh):
    return jax.shard_map(
        on_device,
        mesh=mesh,
        in_specs=(
            P("dp", "mp"),
            P("mp", None),
            P("dp", "mp"),
            P("mp"),
            P("mp", None),
            P("dp"),
            P(),
            P("dp", "mp", None, None),
            P("dp", "mp", None, None),
            P(),
            P(None, "mp"),
            P(None, "mp"),
            P(None, "mp"),
        ),
        out_specs=(P("dp", "mp", None, None), P("mp", "dp")),
        check_vma=False,
    )
```

```python
import jax
import jax.numpy as jnp
from jax import lax
from jax.experimental import pallas as pl
from jax.experimental.pallas import tpu as pltpu
from jax.sharding import PartitionSpec as P

BLK = 128
epsilon = 1e-06
half = jnp.bfloat16
full = jnp.float32


def exchange(pieces, axis):
    return lax.all_to_all(pieces, axis, split_axis=0, concat_axis=0, tiled=True)


def take(array, starts, sizes):
    return lax.dynamic_slice(array, starts, sizes, allow_negative_indices=False)


def three_parts(value):
    first = lax.reduce_precision(value, 8, 7)
    rest = value - first
    second = lax.reduce_precision(rest, 8, 7)
    return jnp.stack([first, second, rest - second]).astype(half)


def times_rows(left, right):
    return lax.dot_general(left, right, (((1,), (1,)), ((), ())), preferred_element_type=full)


SIDE = 4


def step(value, along_y, along_z):
    pairs = []
    for y in range(SIDE):
        for z in range(SIDE):
            to = ((y + along_y) % SIDE) * SIDE + (z + along_z) % SIDE
            pairs.append((y * SIDE + z, to))
    return lax.ppermute(value, "mp", pairs)


def far_kernel(place, left, right, lower0, upper0, lower1, upper1, held, sems):
    width = held.shape[2]
    y, z = lax.rem(place[0] + 2, SIDE), lax.rem(place[1] + 2, SIDE)
    middle = BLK // 2
    loads = []
    for index in range(2 * SIDE):
        piece = y * SIDE + index if index < SIDE else (index - SIDE) * SIDE + z
        columns = pl.ds(pl.multiple_of(piece * width, width), width)
        load = pltpu.make_async_copy(right.at[:, columns], held.at[index], sems.at[index])
        load.start()
        loads.append(load)
    for index in range(2 * SIDE):
        loads[index].wait()
        block, at = index // SIDE, index % SIDE
        value = jnp.dot(
            left[pl.ds(block * BLK, BLK), :], held[index], preferred_element_type=full
        ).astype(half)
        lower, upper = (lower0, upper0) if block == 0 else (lower1, upper1)
        lower[at] = value[:middle]
        upper[at] = value[middle:]


def near_kernel(place, left, right, kept0, up0, down0, kept1, up1, down1, held, sems):
    outs = {0: (kept0, kept1), 1: (up0, up1), 3: (down0, down1)}
    width = held.shape[2]
    y, z = place[0], place[1]

    def load(index):
        piece = lax.rem(y + index // SIDE, SIDE) * SIDE + lax.rem(index, SIDE)
        columns = pl.ds(pl.multiple_of(piece * width, width), width)
        return pltpu.make_async_copy(right.at[:, columns], held.at[index], sems.at[index])

    for index in range(SIDE * SIDE):
        load(index).start()

    @pl.loop(0, SIDE * SIDE)
    def _(index):
        load(index).wait()
        value = jnp.dot(left[...], held[index], preferred_element_type=full).astype(half)
        along_y, at_z = index // SIDE, lax.rem(index, SIDE)
        at_y, along_z = lax.rem(y + along_y, SIDE), lax.rem(at_z - z + SIDE, SIDE)
        for distance, (first, second) in outs.items():

            @pl.when(along_y == distance)
            def _():
                first[at_z] = value[:BLK]

            @pl.when(along_z == distance)
            def _():
                second[at_y] = value[BLK:]


def merge_kernel(*refs):
    ins, outs = refs[:8], refs[8:]
    middle = BLK // 2
    for block in (0, 1):
        up, down, lower, upper = ins[4 * block : 4 * block + 4]
        to_up, to_down = outs[2 * block], outs[2 * block + 1]
        to_up[0, :middle] = (up[0, :middle].astype(full) + lower[0].astype(full)).astype(half)
        to_up[0, middle:] = up[0, middle:]
        to_down[0, :middle] = down[0, :middle]
        to_down[0, middle:] = (down[0, middle:].astype(full) + upper[0].astype(full)).astype(half)


def gather_kernel(place, *refs):
    ins, outs = refs[:6], refs[7:]
    for block in (0, 1):
        kept, from_down, from_up = ins[3 * block : 3 * block + 3]
        here = place[1 - block]
        for distance in range(SIDE):
            at = lax.rem(here + distance, SIDE)
            value = kept[at].astype(full) + from_down[at].astype(full) + from_up[at].astype(full)
            out = outs[SIDE * block + distance]
            out[...] = value.astype(out.dtype)


def teacher_terms(attention, out_proj, mp, order):
    width = attention.shape[1]
    whole = pl.BlockSpec(memory_space=pltpu.VMEM)
    scalars = pl.BlockSpec(memory_space=pltpu.SMEM)
    anywhere = pl.BlockSpec(memory_space=pl.ANY)
    limit = pltpu.CompilerParams(vmem_limit_bytes=40 * 1024 * 1024)
    place = jnp.stack([mp // SIDE, mp % SIDE]).astype(jnp.int32)
    full_piece = jax.ShapeDtypeStruct((SIDE, BLK, width), half)
    half_piece = jax.ShapeDtypeStruct((SIDE, BLK // 2, width), half)
    moves = full_piece.size
    one_piece = pl.BlockSpec((1, BLK, width), lambda i: (i, 0, 0))
    one_half = pl.BlockSpec((1, BLK // 2, width), lambda i: (i, 0, 0))

    def terms(kernel, pieces, count, blocks):
        return pl.pallas_call(
            kernel,
            in_specs=[scalars, whole, pl.BlockSpec(memory_space=pltpu.HBM)],
            out_specs=[whole] * len(pieces),
            out_shape=pieces,
            scratch_shapes=[
                pltpu.VMEM((count, width, width), half),
                pltpu.SemaphoreType.DMA((count,)),
            ],
            compiler_params=pltpu.CompilerParams(vmem_limit_bytes=48 * 1024 * 1024),
            cost_estimate=pl.CostEstimate(
                flops=2 * blocks * BLK * count * width * width,
                bytes_accessed=2 * count * width * width,
                transcendentals=0,
            ),
        )(place, attention, out_proj)

    lower0, upper0, lower1, upper1 = terms(far_kernel, [half_piece] * 4, 2 * SIDE, 1)
    kept0, up0, down0, kept1, up1, down1 = terms(near_kernel, [full_piece] * 6, SIDE * SIDE, 2)
    lower0, upper0 = step(lower0, 1, 0), step(upper0, -1, 0)
    lower1, upper1 = step(lower1, 0, 1), step(upper1, 0, -1)
    up0, down0, up1, down1 = pl.pallas_call(
        merge_kernel,
        grid=(SIDE,),
        in_specs=[one_piece, one_piece, one_half, one_half] * 2,
        out_specs=[one_piece] * 4,
        out_shape=[full_piece] * 4,
        compiler_params=limit,
        cost_estimate=pl.CostEstimate(
            flops=4 * moves, bytes_accessed=20 * moves, transcendentals=0
        ),
    )(up0, down0, lower0, upper0, up1, down1, lower1, upper1)
    from_down0, from_up0 = step(up0, 1, 0), step(down0, -1, 0)
    from_down1, from_up1 = step(up1, 0, 1), step(down1, 0, -1)
    sums = pl.pallas_call(
        gather_kernel,
        in_specs=[scalars] + [whole] * 6 + [anywhere],
        out_specs=[whole] * (2 * SIDE),
        out_shape=[
            jax.ShapeDtypeStruct((BLK, width), half if distance else full)
            for block in (0, 1)
            for distance in range(SIDE)
        ],
        compiler_params=limit,
        cost_estimate=pl.CostEstimate(
            flops=4 * moves, bytes_accessed=16 * moves, transcendentals=0
        ),
    )(place, kept0, from_down0, from_up0, kept1, from_down1, from_up1, *order)
    results = []
    for block in (0, 1):
        mine = sums[SIDE * block : SIDE * block + SIDE]
        arrived = [
            step(mine[d], 0, d) if block == 0 else step(mine[d], d, 0) for d in range(1, SIDE)
        ]
        results.append([mine[0]] + arrived)
    return results


def total(values):
    result = values[0].astype(full)
    for value in values[1:]:
        result = result + value.astype(full)
    return result


def backward_kernel(dy, down, gate, up, order, grad_gate, grad_up, dh):
    del order
    rows = 8
    for chunk in range(2):
        columns = pl.ds(chunk * (down.shape[1] // 2), down.shape[1] // 2)
        value = jnp.dot(dy[...], down[:, columns], preferred_element_type=full)
        for index in range(value.shape[0] // rows):
            to = (index % 2) * BLK + (index // 2) * rows
            dh[pl.ds(to, rows), columns] = value[index * rows : index * rows + rows]
    gate_val = gate[...]
    sigma = jax.nn.sigmoid(gate_val)
    grad_gate[...] = (dh[...] * up[...] * sigma * (1.0 + gate_val * (1.0 - sigma))).astype(half)
    grad_up[...] = (dh[...] * (gate_val * sigma)).astype(half)


def backward(dy, down, gate, up, order):
    whole = pl.BlockSpec(memory_space=pltpu.VMEM)
    shape = jax.ShapeDtypeStruct(gate.shape, half)
    return pl.pallas_call(
        backward_kernel,
        in_specs=[whole] * 4 + [pl.BlockSpec(memory_space=pl.ANY)],
        out_specs=[whole, whole],
        out_shape=[shape, shape],
        scratch_shapes=[pltpu.VMEM(gate.shape, full)],
        compiler_params=pltpu.CompilerParams(vmem_limit_bytes=56 * 1024 * 1024),
        cost_estimate=pl.CostEstimate(
            flops=2 * dy.shape[0] * down.size,
            bytes_accessed=2 * (down.size + dy.size) + 16 * gate.size,
            transcendentals=gate.size,
        ),
    )(dy, down, gate, up, order)


def spread_kernel(piece, out, sems):
    copies = [
        pltpu.make_async_copy(piece, out.at[to], sems.at[to]) for to in range(out.shape[0])
    ]
    for copy in copies:
        copy.start()
    for copy in copies:
        copy.wait()


def spread(piece, count):
    whole = pl.BlockSpec(memory_space=pltpu.VMEM)
    return pl.pallas_call(
        spread_kernel,
        in_specs=[whole],
        out_specs=pl.BlockSpec(memory_space=pltpu.HBM),
        scratch_shapes=[pltpu.SemaphoreType.DMA((count,))],
        out_shape=jax.ShapeDtypeStruct((count,) + piece.shape, piece.dtype),
        compiler_params=pltpu.CompilerParams(vmem_limit_bytes=16 * 1024 * 1024),
        cost_estimate=pl.CostEstimate(
            flops=0, bytes_accessed=4 * count * piece.size, transcendentals=0
        ),
    )(piece)


def home_kernel(terms, state, out):
    value = state[...].astype(full)
    for source in range(terms.shape[0]):
        value = value + terms[source].astype(full)
    rows = state.shape[0]
    out[pl.ds(0, rows), :] = value.astype(half)
    out[pl.ds(rows, rows), :] = jnp.zeros(state.shape, half)


def home(terms, state):
    rows, width = state.shape
    whole = pl.BlockSpec(memory_space=pltpu.VMEM)
    return pl.pallas_call(
        home_kernel,
        in_specs=[whole, whole],
        out_specs=whole,
        out_shape=jax.ShapeDtypeStruct((2 * rows, width), half),
        compiler_params=pltpu.CompilerParams(vmem_limit_bytes=16 * 1024 * 1024),
        cost_estimate=pl.CostEstimate(
            flops=17 * rows * width, bytes_accessed=40 * rows * width, transcendentals=0
        ),
    )(terms, state)


def pool_kernel(place, message, token_slot, out, inverse, sh, weights, state, sems):
    sources, _, cols = message.shape
    rows = BLK // sources
    token_proj = message[0, :BLK].astype(full)
    for source in range(1, sources):
        token_proj = token_proj + message[source, :BLK].astype(full)
    squares = jnp.zeros((rows, cols), full)
    for source in range(sources):
        tail = message[source, BLK:].astype(full)
        sh[pl.ds(source * rows, rows), :] = tail[:rows]
        squares = squares + tail[rows:]
    tokens = token_slot.shape[1]
    squares = jnp.sum(squares, axis=0, keepdims=True)[:, :tokens]
    inverse[...] = lax.rsqrt(squares / place[1].astype(full) + epsilon)
    slots = jnp.where(place[0] == 0, token_slot[:, :BLK], token_slot[:, BLK:])
    scale = jnp.where(place[0] == 0, inverse[:, :BLK], inverse[:, BLK:])
    hits = slots == lax.broadcasted_iota(jnp.int32, (BLK, BLK), 0)
    counts = jnp.maximum(jnp.sum(hits.astype(full), axis=1, keepdims=True), 1.0)
    weights[...] = jnp.where(hits, scale, 0.0)
    first = weights[...].astype(half)
    second = (weights[...] - lax.reduce_precision(weights[...], 8, 7)).astype(half)
    token_proj = token_proj.astype(half)
    placed = jnp.dot(first, token_proj, preferred_element_type=full)
    placed = placed + jnp.dot(second, token_proj, preferred_element_type=full)
    placed = (placed / counts).astype(half).astype(full)
    state[...] = (sh[...] + placed).astype(half)
    copies = [
        pltpu.make_async_copy(state, out.at[to], sems.at[to]) for to in range(sources)
    ]
    for copy in copies:
        copy.start()
    for copy in copies:
        copy.wait()


def pool(message, token_slot, block, width_full):
    sources, _, cols = message.shape
    whole = pl.BlockSpec(memory_space=pltpu.VMEM)
    tokens = token_slot.shape[0]
    place = jnp.stack([block, jnp.full_like(block, width_full)]).astype(jnp.int32)
    return pl.pallas_call(
        pool_kernel,
        in_specs=[pl.BlockSpec(memory_space=pltpu.SMEM), whole, whole],
        out_specs=[pl.BlockSpec(memory_space=pltpu.HBM), whole],
        out_shape=[
            jax.ShapeDtypeStruct((sources, BLK, cols), half),
            jax.ShapeDtypeStruct((1, tokens), full),
        ],
        scratch_shapes=[
            pltpu.VMEM((BLK, cols), full),
            pltpu.VMEM((BLK, BLK), full),
            pltpu.VMEM((BLK, cols), half),
            pltpu.SemaphoreType.DMA((sources,)),
        ],
        compiler_params=pltpu.CompilerParams(vmem_limit_bytes=40 * 1024 * 1024),
        cost_estimate=pl.CostEstimate(
            flops=6 * message.size, bytes_accessed=4 * message.size, transcendentals=tokens
        ),
    )(place, message, token_slot[None])


def forward_kernel(
    pieces, gain, order, gate_hbm, up_hbm, down_hbm, state, gate, up, out, normed, act, held, sems
):
    del order
    parts = 3
    part = gate_hbm.shape[0] // parts

    def load(which, source, third):
        at = pl.ds(third * part, part)
        return pltpu.make_async_copy(
            source.at[at], held.at[which, at], sems.at[parts * which + third]
        )

    for third in range(parts):
        load(0, gate_hbm, third).start()
        load(1, up_hbm, third).start()
    cols = pieces.shape[2]
    groups = state.shape[1] // cols
    for block in range(state.shape[0] // BLK):
        rows = pl.ds(block * BLK, BLK)
        squares = jnp.zeros((BLK, 128), full)
        for group in range(groups):
            value = pieces[block * groups + group]
            state[rows, pl.ds(group * cols, cols)] = value
            wide = value.astype(full)
            wide = wide * wide
            for lane in range(0, cols, 128):
                squares = squares + wide[:, lane : lane + 128]
        mean = jnp.sum(squares, axis=1, keepdims=True) / state.shape[1]
        inverse = lax.rsqrt(mean + epsilon)
        for group in range(groups):
            at = pl.ds(group * cols, cols)
            wide = pieces[block * groups + group].astype(full)
            normed[rows, at] = (wide * inverse * gain[:, at]).astype(normed.dtype)
    half_hidden = gate.shape[1] // 2
    for third in range(parts):
        load(0, gate_hbm, third).wait()
        load(1, up_hbm, third).wait()
        load(2, down_hbm, third).start()
        depth = pl.ds(third * part, part)
        for index in range(2):
            at = pl.ds(index * half_hidden, half_hidden)
            for which, total_ref in ((0, gate), (1, up)):
                value = jnp.dot(
                    normed[:, depth], held[which, depth, at], preferred_element_type=full
                )
                total_ref[:, at] = value if third == 0 else total_ref[:, at] + value
    gate_val = gate[...]
    act[...] = (gate_val * jax.nn.sigmoid(gate_val) * up[...]).astype(half)
    for third in range(parts):
        load(2, down_hbm, third).wait()
    down_w = held.at[2]
    rows = out.shape[1] // 2
    wide_chunk = 512

    @pl.loop(0, state.shape[1] // wide_chunk)
    def _(index):
        at = pl.ds(pl.multiple_of(index * wide_chunk, wide_chunk), wide_chunk)
        value = times_rows(act[...], down_w[at, :])
        for to in range(out.shape[0]):
            first = value[to * rows : to * rows + rows]
            second = value[BLK + to * rows : BLK + to * rows + rows]
            out[to, :, at] = jnp.concatenate([first, second], axis=0).astype(half)


def forward(pieces, gain, gate_w, up_w, down_w, order):
    width, hidden = gate_w.shape
    n_mp = pieces.shape[0]
    rows = 2 * BLK
    whole = pl.BlockSpec(memory_space=pltpu.VMEM)
    return pl.pallas_call(
        forward_kernel,
        in_specs=[whole, whole, pl.BlockSpec(memory_space=pl.ANY)]
        + [pl.BlockSpec(memory_space=pltpu.HBM)] * 3,
        out_specs=[whole] * 4,
        out_shape=[
            jax.ShapeDtypeStruct((rows, width), half),
            jax.ShapeDtypeStruct((rows, hidden), full),
            jax.ShapeDtypeStruct((rows, hidden), full),
            jax.ShapeDtypeStruct((n_mp, rows // n_mp, width), half),
        ],
        scratch_shapes=[
            pltpu.VMEM((rows, width), half),
            pltpu.VMEM((rows, hidden), half),
            pltpu.VMEM((3, width, hidden), half),
            pltpu.SemaphoreType.DMA((9,)),
        ],
        compiler_params=pltpu.CompilerParams(vmem_limit_bytes=56 * 1024 * 1024),
        cost_estimate=pl.CostEstimate(
            flops=6 * rows * width * hidden,
            bytes_accessed=6 * width * hidden + 10 * rows * width,
            transcendentals=rows * hidden,
        ),
    )(pieces, gain[None], order, gate_w, up_w, down_w)


def slope_kernel(terms, dy, state, gain, order, out):
    del order
    rows, width = dy.shape
    cols = out.shape[2]
    wide = state[...].astype(full)
    inverse = lax.rsqrt(jnp.mean(wide * wide, axis=1, keepdims=True) + epsilon)
    dn = terms[0].astype(full)
    for source in range(1, terms.shape[0]):
        dn = dn + terms[source].astype(full)
    gained = gain[...] * dn
    mean = jnp.mean(gained * wide, axis=1, keepdims=True)
    dx = dy[...].astype(full) + inverse * gained - wide * (inverse * inverse * inverse) * mean
    for group in range(out.shape[0]):
        out[group] = dx[:, group * cols : (group + 1) * cols].astype(out.dtype)


def slope(terms, dy, state, gain, groups, order):
    rows, width = dy.shape
    whole = pl.BlockSpec(memory_space=pltpu.VMEM)
    return pl.pallas_call(
        slope_kernel,
        in_specs=[whole] * 4 + [pl.BlockSpec(memory_space=pl.ANY)],
        out_specs=whole,
        out_shape=jax.ShapeDtypeStruct((groups, rows, width // groups), half),
        compiler_params=pltpu.CompilerParams(vmem_limit_bytes=16 * 1024 * 1024),
        cost_estimate=pl.CostEstimate(
            flops=30 * rows * width, bytes_accessed=40 * rows * width, transcendentals=rows
        ),
    )(terms, dy, state, gain[None], order)


def on_device(
    attention,
    out_proj,
    residual,
    final_gain,
    adapter_weight,
    token_slot,
    block_owner,
    student_hidden,
    cotangent,
    student_gain,
    gate_weight,
    up_weight,
    down_weight,
):
    tokens, width_here = attention.shape
    width_full = out_proj.shape[1]
    student_width = adapter_weight.shape[1]
    blocks = tokens // BLK
    n_mp = lax.axis_size("mp")
    n_dp = lax.axis_size("dp")
    dp = lax.axis_index("dp")
    mp = lax.axis_index("mp")
    slots = student_hidden.shape[2]
    rows = BLK // n_mp
    groups = n_mp // blocks
    cols = student_width // groups
    out_cols = student_width // n_dp
    mine_rows = blocks * rows

    ids = jnp.arange(block_owner.shape[0], dtype=jnp.int32)
    my_ids = dp * blocks + jnp.arange(blocks, dtype=jnp.int32)
    my_owner = take(block_owner, (dp * blocks,), (blocks,))
    my_slot = jnp.sum(
        (block_owner[None, :] == my_owner[:, None]) & (ids[None, :] < my_ids[:, None]),
        axis=1,
        dtype=jnp.int32,
    )

    both = jnp.concatenate([student_hidden[0], cotangent[0]], axis=1)
    everyone = lax.all_gather(both, "dp", axis=0, tiled=False)

    def fetch(offset):
        picked = []
        for k in range(blocks):
            at = (my_owner[k], 0, my_slot[k] + offset, 0)
            picked.append(
                take(everyone, at, (1, rows, 1, student_width)).reshape(rows, student_width)
            )
        return jnp.stack(picked)

    sh_rows = fetch(0)
    dy_rows = fetch(student_hidden.shape[2])
    dy = lax.all_gather(dy_rows, "mp", axis=0, tiled=False)

    hidden = residual.astype(full) + jnp.concatenate(
        [total(v) for v in teacher_terms(attention, out_proj, mp, (sh_rows,))], axis=0
    )
    squares = jnp.sum(hidden * hidden, axis=1)
    gained_hidden = hidden * final_gain
    parts = jnp.einsum(
        "ktd,dce->kcte",
        gained_hidden.astype(half).reshape(blocks, BLK, width_here),
        adapter_weight.reshape(width_here, groups, cols),
        preferred_element_type=full,
    ).astype(half)
    sh_parts = jnp.swapaxes(sh_rows.reshape(blocks, rows, groups, cols), 1, 2)
    sq_parts = jnp.zeros((8, cols), half).at[:3, :tokens].set(three_parts(squares))
    message = jnp.concatenate(
        [
            parts,
            sh_parts,
            jnp.broadcast_to(sq_parts[None, None], (blocks, groups) + sq_parts.shape),
        ],
        axis=2,
    )
    message = exchange(message.reshape(n_mp, BLK + rows + 8, cols), "mp")
    states, inverse_rms = pool(message, token_slot, mp // groups, width_full)
    states = exchange(states, "mp")

    slots_block = token_slot.reshape(blocks, BLK)
    onehot = slots_block[:, None, :] == jnp.arange(BLK, dtype=jnp.int32)[None, :, None]
    counts = jnp.maximum(jnp.sum(onehot.astype(full), axis=2), 1.0)
    onehot = onehot.astype(half)
    normed = (gained_hidden * inverse_rms.reshape(tokens, 1)).astype(half).reshape(blocks, BLK, width_here)
    pooled = jnp.einsum("krt,ktd->krd", onehot, normed, preferred_element_type=full)
    pooled = (pooled / counts[:, :, None]).astype(half)
    pooled_all = lax.all_gather(pooled.reshape(n_mp, mine_rows, width_here), "dp", axis=0, tiled=False)
    pooled_all = jnp.swapaxes(pooled_all, 0, 1).reshape(n_dp * tokens, width_here)

    state, gate, up, output = forward(
        states, student_gain, gate_weight, up_weight, down_weight, pooled
    )
    grad_gate, grad_up = backward(dy.reshape(tokens, student_width), down_weight, gate, up, output)
    dn = (times_rows(grad_gate, gate_weight) + times_rows(grad_up, up_weight)).astype(half)
    output = exchange(output, "mp")
    dn, output = lax.optimization_barrier((dn, output))
    dn = exchange(dn.reshape(n_mp, mine_rows, student_width), "mp")
    here = mp * mine_rows
    state_rows = take(
        state.reshape(blocks, BLK, student_width),
        (0, mp * rows, 0),
        (blocks, rows, student_width),
    )
    out_rows = home(output, state_rows.reshape(mine_rows, student_width))
    dproj = slope(
        dn,
        take(
            dy, ((mp % groups) * blocks, mp // groups, 0, 0), (blocks, 1, rows, student_width)
        ).reshape(mine_rows, student_width),
        take(state, (here, 0), (mine_rows, student_width)),
        student_gain,
        n_dp,
        out_rows,
    )
    dproj = exchange(spread(exchange(dproj, "dp"), n_mp), "mp")
    adapter_grad = lax.dot_general(
        pooled_all,
        dproj.reshape(n_dp * tokens, out_cols),
        (((0,), (0,)), ((), ())),
        preferred_element_type=full,
    )

    back = lax.all_gather(out_rows, "dp", axis=0, tiled=False)
    before = (block_owner[None, :] == block_owner[:, None]) & (ids[None, :] < ids[:, None])
    ranks = jnp.sum(before, axis=1, dtype=jnp.int32)
    mine = block_owner == dp
    picks = []
    for slot in range(slots):
        chosen = mine & (ranks == slot)
        index = jnp.sum(jnp.where(chosen, ids, 0))
        at = (index // blocks, (index % blocks) * rows, 0)
        piece = take(back, at, (1, rows, student_width))[0]
        picks.append(jnp.where(jnp.any(chosen), piece, jnp.zeros((), half)))
    student_out = jnp.stack(picks, axis=1)
    return (student_out[None], adapter_grad)


def solution(mesh):
    return jax.shard_map(
        on_device,
        mesh=mesh,
        in_specs=(
            P("dp", "mp"),
            P("mp", None),
            P("dp", "mp"),
            P("mp"),
            P("mp", None),
            P("dp"),
            P(),
            P("dp", "mp", None, None),
            P("dp", "mp", None, None),
            P(),
            P(None, "mp"),
            P(None, "mp"),
            P(None, "mp"),
        ),
        out_specs=(P("dp", "mp", None, None), P("mp", "dp")),
        check_vma=False,
    )
```
